32 devices in a mesh: rep: 4 (over z), exp: 8 (over y, x, core).
Axes of the slice: x: 2, y: 2, z: 4, core: 2. Of those that a mesh axis runs over, the one named last changes fastest.
Arguments:
- tokens: bfloat16 [36864, 768], P(('rep', 'exp')), may hold values from -6 to 6
- cotangent: bfloat16 [36864, 768], P(('rep', 'exp')), may hold values from -6 to 6
- expert_ids: int32 [36864, 2], P(('rep', 'exp')), may hold values from 0 to 7, as said below
- expert_slots: int32 [36864, 2], P(('rep', 'exp')), may hold values from -1 to 143, as said below
- w_qkv: bfloat16 [768, 2304], replicated, may hold values from -0.21875 to 0.21875
- q_bias: bfloat16 [768], replicated, may hold values from -1.75 to 1.75
- v_bias: bfloat16 [768], replicated, may hold values from -1.75 to 1.75
- w_proj: bfloat16 [768, 768], replicated, may hold values from -0.875 to 0.875
- proj_bias: bfloat16 [768], replicated, may hold values from -1.75 to 1.75
- gain_one: float32 [768], replicated, may hold values from 0.25 to 1.75
- shift_one: float32 [768], replicated, may hold values from -1.75 to 1.75
- gain_two: float32 [768], replicated, may hold values from 0.25 to 1.75
- shift_two: float32 [768], replicated, may hold values from -1.75 to 1.75
- w_router: float32 [768, 8], replicated, may hold values from -0.15625 to 0.15625
- expert_in: bfloat16 [8, 768, 3072], P('exp'), may hold values from -0.21875 to 0.21875
- expert_in_bias: bfloat16 [8, 3072], P('exp'), may hold values from -1.75 to 1.75
- expert_out: bfloat16 [8, 3072, 768], P('exp'), may hold values from -0.4375 to 0.4375
- expert_out_bias: bfloat16 [8, 768], P('exp'), may hold values from -1.5 to 1.5
Outputs:
- mixed: bfloat16 [36864, 768], P(('rep', 'exp'))
- grad_tokens: float32 [36864, 768], P(('rep', 'exp'))
- grad_w_qkv: float32 [768, 2304], replicated
- grad_q_bias: float32 [768], replicated
- grad_v_bias: float32 [768], replicated
- grad_w_proj: float32 [768, 768], replicated
- grad_proj_bias: float32 [768], replicated
- grad_gain_one: float32 [768], replicated
- grad_shift_one: float32 [768], replicated
- grad_gain_two: float32 [768], replicated
- grad_shift_two: float32 [768], replicated
- grad_w_router: float32 [768, 8], replicated
- grad_expert_in: float32 [8, 768, 3072], P('exp', None, 'rep')
- grad_expert_in_bias: float32 [8, 3072], P('exp', 'rep')
- grad_expert_out: float32 [8, 3072, 768], P('exp', 'rep')
- grad_expert_out_bias: float32 [8, 768], P('exp', 'rep')
The draws below stay inside these ranges and needn't reach their ends.
Inputs may be any that keep to these rules, and one draw needn't show every extreme that they name: `expert_ids`: the two experts of a patch differ. `expert_slots`: among the pairs of one device (aligned blocks of 1152 rows), each expert's kept pairs hold the slots 0, 1, 2, ... once each in a priority order of those pairs, and a pair is -1 exactly when its expert already has 144 pairs of that device before it.
All inputs are finite; a program needn't handle non-finite values.
Results may differ from the reference program's by a relative error of at most 0.014.
Values may be sent and summed in bfloat16 or wider, within the bound.
No kernel may reach another device: no remote copies, remote signals or barrier semaphores. Data moves between devices by JAX's collectives and lax.ppermute only.
A program may use at most 192 MiB of HBM per device.

```python
import jax
import jax.numpy as jnp
from jax import lax

HEADS = 12
HEAD_DIM = 64
D = 768
FF = 3072
SEQ = 576
TOK_DEV = 1152
EXPERTS = 8
CAP = 144
TOKENS = 36864
N_REP = 4
N_EXP = 8


def route_table(key):
    blocks = N_REP * N_EXP
    hot_count = max(EXPERTS // 8, 1)
    order_key, pick_key, hot_key, second_key, coin_key, rank_key = jax.random.split(key, 6)
    order = jax.random.permutation(order_key, EXPERTS)
    hot_set = order[:hot_count]
    coin_flip = jax.random.randint(coin_key, (blocks, TOK_DEV), 0, 2)
    hot_pick = jnp.take(hot_set, jax.random.randint(hot_key, (blocks, TOK_DEV), 0, hot_count))
    any_pick = jax.random.randint(pick_key, (blocks, TOK_DEV), 0, EXPERTS)
    first_id = jnp.where(coin_flip == 1, hot_pick, any_pick)
    second_id = (first_id + jax.random.randint(second_key, (blocks, TOK_DEV), 1, EXPERTS)) % EXPERTS
    id_pairs = jnp.stack([first_id, second_id], axis=-1)
    token_rank = jax.vmap(lambda sub_key: jax.random.permutation(sub_key, TOK_DEV))(jax.random.split(rank_key, blocks))
    priority = jnp.stack([token_rank, token_rank + TOK_DEV], axis=-1).reshape(blocks, 2 * TOK_DEV)
    flat_ids = id_pairs.reshape(blocks, 2 * TOK_DEV)
    sorting = jnp.argsort(priority, axis=1)
    sorted_ids = jnp.take_along_axis(flat_ids, sorting, axis=1)
    one_hot = (sorted_ids[:, :, None] == jnp.arange(EXPERTS, dtype=jnp.int32)).astype(jnp.int32)
    running = jnp.cumsum(one_hot, axis=1)
    sorted_rank = jnp.sum(running * one_hot, axis=-1) - 1
    unsorting = jnp.argsort(sorting, axis=1)
    ranks = jnp.take_along_axis(sorted_rank, unsorting, axis=1)
    slot_table = jnp.where(ranks < CAP, ranks, -1).astype(jnp.int32)
    return (id_pairs.reshape(TOKENS, 2).astype(jnp.int32), slot_table.reshape(TOKENS, 2))


def draw_expert_ids(key, part):
    id_pairs, slot_table = route_table(key)
    return id_pairs


def draw_expert_slots(key, part):
    id_pairs, slot_table = route_table(key)
    return slot_table


def block_scale(key, extent, cuts, least, high):
    factor_of, own = 1.0, jax.random.fold_in(key, 6)
    for axis_at, parts in cuts:
        heights = jnp.exp(jax.random.uniform(jax.random.fold_in(own, axis_at), (parts,), jnp.float32, least / len(cuts), high / len(cuts)))
        factor_of = factor_of * jnp.repeat(heights, extent[axis_at] // parts).reshape([-1 if axis == axis_at else 1 for axis in range(len(extent))])
    return factor_of


def normal_values(key, shape, width, reach, cuts=(), kind=jnp.bfloat16):
    values = jax.random.normal(key, shape, jnp.float32) * width
    if len(cuts) > 0:
        values = block_scale(key, shape, cuts, -0.22, 0.18) * values
    return jnp.clip(values, min=-reach, max=reach).astype(kind)


def setup_inputs(seed: int = 0) -> dict:
    keys = jax.random.split(jax.random.key(seed), 19)
    tokens = normal_values(keys[0], (TOKENS, D), 1.0, 6.0, ((0, 32),))
    cotangent = normal_values(keys[1], (TOKENS, D), 1.0, 6.0, ((0, 32),))
    expert_ids = draw_expert_ids(jax.random.fold_in(keys[18], 71), 0)
    expert_slots = draw_expert_slots(jax.random.fold_in(keys[18], 71), 0)
    w_qkv = normal_values(keys[4], (D, 3 * D), D ** -0.5, 0.21875)
    q_bias = normal_values(keys[5], (D,), 0.3, 1.75)
    v_bias = normal_values(keys[6], (D,), 0.3, 1.75)
    w_proj = normal_values(keys[7], (D, D), (D // 16) ** -0.5, 0.875)
    proj_bias = normal_values(keys[8], (D,), 0.3, 1.75)
    gain_one = jnp.clip(1.0 + 0.15 * jax.random.normal(keys[9], (D,), jnp.float32), 0.25, 1.75)
    shift_one = normal_values(keys[10], (D,), 0.3, 1.75, (), jnp.float32)
    gain_two = jnp.clip(1.0 + 0.15 * jax.random.normal(keys[11], (D,), jnp.float32), 0.25, 1.75)
    shift_two = normal_values(keys[12], (D,), 0.3, 1.75, (), jnp.float32)
    w_router = normal_values(keys[13], (D, EXPERTS), (2 * D) ** -0.5, 0.15625, (), jnp.float32)
    expert_in = normal_values(keys[14], (EXPERTS, D, FF), D ** -0.5, 0.21875, ((0, 8),))
    expert_in_bias = normal_values(keys[15], (EXPERTS, FF), 0.3, 1.75, ((0, 8),))
    expert_out = normal_values(keys[16], (EXPERTS, FF, D), (max(4 * FF // (EXPERTS * EXPERTS), 1)) ** -0.5, 0.4375, ((0, 8),))
    expert_out_bias = normal_values(keys[17], (EXPERTS, D), (0.03 * EXPERTS), 1.5, ((0, 8),))
    return {"tokens": tokens, "cotangent": cotangent, "expert_ids": expert_ids, "expert_slots": expert_slots, "w_qkv": w_qkv, "q_bias": q_bias, "v_bias": v_bias, "w_proj": w_proj, "proj_bias": proj_bias, "gain_one": gain_one, "shift_one": shift_one, "gain_two": gain_two, "shift_two": shift_two, "w_router": w_router, "expert_in": expert_in, "expert_in_bias": expert_in_bias, "expert_out": expert_out, "expert_out_bias": expert_out_bias}


@jax.custom_vjp
def low(v):
    return lax.optimization_barrier(v.astype(jnp.bfloat16)).astype(jnp.float32)

@jax.custom_vjp
def low_back(v):
    return v

def low_keep(v):
    return (low(v), None)

def low_pass(kept, grad):
    return (grad,)

def back_keep(v):
    return (v, None)

def back_low(kept, grad):
    return (low(grad),)
low.defvjp(low_keep, low_pass)
low_back.defvjp(back_keep, back_low)
EPSILON = 1e-06
HIGHEST = lax.Precision.HIGHEST

def layer_norm(field, norm_gain, norm_shift):
    average = lax.optimization_barrier(jnp.mean(field, axis=-1, keepdims=True))
    centred = field - average
    variance = lax.optimization_barrier(jnp.mean(centred * centred, axis=-1, keepdims=True))
    return centred * lax.rsqrt(variance + EPSILON) * norm_gain + norm_shift

def device_forward(params, pieces):
    w_qkv, q_bias, v_bias, w_proj, proj_bias, gain_one, shift_one, gain_two, shift_two, w_router, expert_in, expert_in_bias, expert_out, expert_out_bias = params
    inputs, expert_ids, expert_slots = pieces
    normed_one = low(layer_norm(inputs, gain_one, shift_one))
    qkv_mixed = jnp.dot(normed_one, w_qkv, precision=HIGHEST)
    queries = low(low_back(qkv_mixed[:, :D] + q_bias))
    key_rows = low(low_back(qkv_mixed[:, D:2 * D]))
    values = low(low_back(qkv_mixed[:, 2 * D:] + v_bias))
    head_shape = (TOK_DEV // SEQ, SEQ, HEADS, HEAD_DIM)
    scores = low_back(jnp.einsum('bqhd,bkhd->bhqk', queries.reshape(head_shape), key_rows.reshape(head_shape), precision=HIGHEST) * HEAD_DIM ** (-0.5))
    weights = low(jax.nn.softmax(scores, axis=-1))
    context = jnp.einsum('bhqk,bkhd->bqhd', weights, values.reshape(head_shape), precision=HIGHEST)
    context = low(low_back(context.reshape(TOK_DEV, D)))
    branch = low_back(jnp.dot(context, w_proj, precision=HIGHEST) + proj_bias)
    residual = inputs + branch
    normed_two = low(layer_norm(residual, gain_two, shift_two))
    router = jax.nn.softmax(jnp.dot(normed_two, w_router, precision=HIGHEST), axis=-1)
    chosen = (expert_ids[:, :, None] == jnp.arange(EXPERTS, dtype=jnp.int32)).astype(jnp.float32)
    placed = (expert_slots[:, :, None] == jnp.arange(CAP, dtype=jnp.int32)).astype(jnp.float32)
    pair_hits = chosen[:, :, :, None] * placed[:, :, None, :]
    gate_values = lax.optimization_barrier(jnp.sum(router[:, None, :] * chosen, axis=-1))
    dispatched = low_back(jnp.einsum('tkec,td->ecd', pair_hits, normed_two, precision=HIGHEST))
    hidden = low_back(jnp.einsum('ecd,edf->ecf', dispatched, expert_in, precision=HIGHEST) + expert_in_bias[:, None, :])
    activated = low(jax.nn.gelu(hidden, approximate=False))
    produced = low(low_back(jnp.einsum('ecf,efd->ecd', activated, expert_out, precision=HIGHEST) + expert_out_bias[:, None, :]))
    picked = jnp.einsum('tkec,ecd->tkd', pair_hits, produced, precision=HIGHEST)
    return residual + lax.optimization_barrier(jnp.sum(gate_values[:, :, None] * picked, axis=1))

def reference(tokens, cotangent, expert_ids, expert_slots, w_qkv, q_bias, v_bias, w_proj, proj_bias, gain_one, shift_one, gain_two, shift_two, w_router, expert_in, expert_in_bias, expert_out, expert_out_bias):
    params = tuple((array.astype(jnp.float32) for array in (w_qkv, q_bias, v_bias, w_proj, proj_bias, gain_one, shift_one, gain_two, shift_two, w_router, expert_in, expert_in_bias, expert_out, expert_out_bias)))
    blocks = N_REP * N_EXP
    id_blocks = expert_ids.reshape(blocks, TOK_DEV, 2)
    slot_blocks = expert_slots.reshape(blocks, TOK_DEV, 2)

    def forward(weight_set, inputs):

        def block_step(pieces):
            return device_forward(weight_set, pieces)
        return lax.map(jax.checkpoint(block_step), (inputs.reshape(blocks, TOK_DEV, D), id_blocks, slot_blocks)).reshape(TOKENS, D)
    result, pullback = jax.vjp(forward, params, tokens.astype(jnp.float32))
    grad_params, grad_tokens = pullback(cotangent.astype(jnp.float32))
    g_qkv, g_qbias, g_vbias, g_proj, g_pbias, g_gone, g_sone, g_gtwo, g_stwo, g_router, g_ein, g_einb, g_eout, g_eoutb = grad_params
    return (result.astype(jnp.bfloat16), grad_tokens, g_qkv, g_qbias, g_vbias, g_proj, g_pbias, g_gone, g_sone, g_gtwo, g_stwo, g_router, g_ein, g_einb, g_eout, g_eoutb)
```

```python
import functools

import jax
import jax.numpy as jnp
from jax import lax
from jax.experimental import pallas as pl
from jax.experimental.pallas import tpu as pltpu
from jax.sharding import PartitionSpec as P

HEAD_DIM = 64
SEQ = 576
PAIR = 2 * HEAD_DIM
SPLIT = 512
AUX = 128
EPSILON = 1e-06
F32 = jnp.float32
BF16 = jnp.bfloat16
VMEM_BYTES = 56 * 2**20


def dot(left, right):
    return lax.dot_general(left, right, (((1,), (0,)), ((), ())), preferred_element_type=F32)


def dot_last(left, right):
    return lax.dot_general(left, right, (((1,), (1,)), ((), ())), preferred_element_type=F32)


def dot_first(left, right):
    return lax.dot_general(left, right, (((0,), (0,)), ((), ())), preferred_element_type=F32)


def thirds(value):
    high = value.astype(BF16)
    rest = value - high.astype(F32)
    middle = rest.astype(BF16)
    return high, middle, (rest - middle.astype(F32)).astype(BF16)


def standardize(field):
    centred = field - jnp.mean(field, axis=-1, keepdims=True)
    inverse = lax.rsqrt(jnp.mean(centred * centred, axis=-1, keepdims=True) + EPSILON)
    return centred * inverse, inverse


def standardize_back(grad, gain, unit, inverse):
    scaled = grad * gain
    along = jnp.mean(scaled * unit, axis=-1, keepdims=True)
    return inverse * (scaled - jnp.mean(scaled, axis=-1, keepdims=True) - unit * along)


def column_sum(field):
    return jnp.sum(field, axis=0, keepdims=True)


def params():
    return pltpu.CompilerParams(vmem_limit_bytes=VMEM_BYTES)


def whole(array):
    return pl.BlockSpec(array.shape, lambda *ids: (0,) * array.ndim)


def shape(dims, kind):
    return jax.ShapeDtypeStruct(dims, kind)


def split_heads(pair):
    lane = lax.broadcasted_iota(jnp.int32, pair.shape, 1)
    zero = jnp.zeros_like(pair)
    first = jnp.where(lane < HEAD_DIM, pair, zero)
    second = jnp.where(lane < HEAD_DIM, zero, pair)
    return jnp.concatenate([first[:SPLIT], second[:SPLIT], first[SPLIT:], second[SPLIT:]], axis=0)


def key_sides():
    row = lax.broadcasted_iota(jnp.int32, (2 * SEQ, PAIR), 0)
    lane = lax.broadcasted_iota(jnp.int32, (2 * SEQ, PAIR), 1)
    is_first = (row < SPLIT) | ((row >= 2 * SPLIT) & (row < SPLIT + SEQ))
    return is_first, lane


def front_kernel(
    chunk,
    tokens,
    w_qkv,
    bias,
    w_proj,
    proj_bias,
    gain_one,
    shift_one,
    gain_two,
    shift_two,
    w_router,
    normed_one_out,
    qkv_out,
    weights_out,
    inverse_out,
    context_out,
    residual_out,
    normed_two_out,
    router_out,
    value_side,
):
    pair = pl.program_id(1)
    pairs = context_out.shape[1]

    @pl.when((pl.program_id(0) == 0) & (pair == 0))
    def _():
        is_first, lane = key_sides()
        value_side[:, PAIR:] = jnp.where(is_first == (lane < HEAD_DIM), 1.0, 0.0).astype(BF16)

    @pl.when(pair == 0)
    def _():
        unit, _ = standardize(tokens[...].astype(F32))
        normed = (unit * gain_one[...] + shift_one[...]).astype(BF16)
        normed_one_out[...] = normed
        width = w_qkv.shape[1]
        step = 2 * PAIR
        for at in range(0, width, step):
            part = dot(normed, w_qkv[:, at : at + step]) + bias[:, at : at + step]
            part = part.astype(BF16)
            if at < width // 3:
                part = part * jnp.asarray(HEAD_DIM**-0.5, BF16)
            qkv_out[0, at // PAIR] = part[:, :PAIR]
            qkv_out[0, at // PAIR + 1] = part[:, PAIR:]

    keys = split_heads(qkv_out[0, pairs + pair])
    value_side[:, :PAIR] = split_heads(qkv_out[0, 2 * pairs + pair])
    values = value_side[...]
    low = lax.broadcasted_iota(jnp.int32, (chunk, PAIR), 1) < HEAD_DIM
    for at in range(0, SEQ, chunk):
        rows = slice(at, at + chunk)
        scores = dot_last(qkv_out[0, pair, rows], keys)
        first = scores[:, :SPLIT]
        second = scores[:, SPLIT : 2 * SPLIT]
        tail = scores[:, 2 * SPLIT :]
        first_max = jnp.maximum(
            jnp.max(first, axis=1, keepdims=True),
            jnp.max(jnp.where(low, tail, -jnp.inf), axis=1, keepdims=True),
        )
        second_max = jnp.maximum(
            jnp.max(second, axis=1, keepdims=True),
            jnp.max(jnp.where(low, -jnp.inf, tail), axis=1, keepdims=True),
        )
        exponent = jnp.concatenate(
            [
                jnp.exp(first - first_max).astype(BF16),
                jnp.exp(second - second_max).astype(BF16),
                jnp.exp(tail - jnp.where(low, first_max, second_max)).astype(BF16),
            ],
            axis=1,
        )
        weights_out[0, 0, rows] = exponent
        summed = dot(exponent, values)
        inverse = 1.0 / summed[:, PAIR:]
        inverse_out[0, 0, rows] = inverse
        context_out[0, pair, rows] = (summed[:, :PAIR] * inverse).astype(BF16)

    @pl.when(pair == pairs - 1)
    def _():
        context = jnp.concatenate([context_out[0, at] for at in range(pairs)], axis=1)
        residual = tokens[...].astype(F32) + (dot(context, w_proj[...]) + proj_bias[...])
        residual_out[...] = residual
        unit, _ = standardize(residual)
        normed = (unit * gain_two[...] + shift_two[...]).astype(BF16)
        normed_two_out[...] = normed
        high, middle, rest = thirds(w_router[...])
        logits = dot(normed, high) + (dot(normed, middle) + dot(normed, rest))
        exponent = jnp.exp(logits - jnp.max(logits, axis=1, keepdims=True))
        router_out[...] = exponent / jnp.sum(exponent, axis=1, keepdims=True)


def front(tokens, w_qkv, bias, w_proj, proj_bias, gain_one, shift_one, gain_two, shift_two, w_router):
    rows, width = tokens.shape
    images = rows // SEQ
    pairs = width // PAIR
    experts = w_router.shape[1]

    def per_image(columns):
        return pl.BlockSpec((SEQ, columns), lambda i, p: (i, 0))

    fixed = (w_qkv, bias, w_proj, proj_bias, gain_one, shift_one, gain_two, shift_two, w_router)
    return pl.pallas_call(
        functools.partial(front_kernel, SEQ // 2),
        grid=(images, pairs),
        in_specs=[per_image(width)] + [whole(array) for array in fixed],
        out_specs=[
            per_image(width),
            pl.BlockSpec((1, 3 * pairs, SEQ, PAIR), lambda i, p: (i, 0, 0, 0)),
            pl.BlockSpec((1, 1, SEQ, 2 * SEQ), lambda i, p: (i, p, 0, 0)),
            pl.BlockSpec((1, 1, SEQ, PAIR), lambda i, p: (i, p, 0, 0)),
            pl.BlockSpec((1, pairs, SEQ, PAIR), lambda i, p: (i, 0, 0, 0)),
            per_image(width),
            per_image(width),
            per_image(experts),
        ],
        out_shape=[
            shape((rows, width), BF16),
            shape((images, 3 * pairs, SEQ, PAIR), BF16),
            shape((images, pairs, SEQ, 2 * SEQ), BF16),
            shape((images, pairs, SEQ, PAIR), F32),
            shape((images, pairs, SEQ, PAIR), BF16),
            shape((rows, width), F32),
            shape((rows, width), BF16),
            shape((rows, experts), F32),
        ],
        scratch_shapes=[pltpu.VMEM((2 * SEQ, 2 * PAIR), BF16)],
        compiler_params=params(),
        name="front",
    )(tokens, *fixed)


def slot_hits(columns, chunk):
    at = pl.program_id(0) * chunk
    slot = at + lax.broadcasted_iota(jnp.int32, (chunk, columns.shape[1]), 0)
    hit = (columns[0:1, :] == slot) | (columns[1:2, :] == slot)
    return jnp.where(hit, 1.0, 0.0).astype(BF16)


def gather_kernel(chunk, columns, rows, out):
    out[...] = dot(slot_hits(columns, chunk), rows[...]).astype(BF16)


def gather(columns, rows, chunk=288):
    count, width = rows.shape
    return pl.pallas_call(
        functools.partial(gather_kernel, chunk),
        grid=(count // chunk,),
        in_specs=[whole(columns), whole(rows)],
        out_specs=pl.BlockSpec((chunk, width), lambda i: (i, 0)),
        out_shape=shape((count, width), BF16),
        compiler_params=params(),
        name="gather",
    )(columns, rows)


def dispatch_kernel(chunk, slot_count, columns, rows, router, out):
    hits = slot_hits(columns, chunk)
    width = rows.shape[1]
    experts = router.shape[1]
    out[:, :width] = dot(hits, rows[...]).astype(BF16)
    high, middle, rest = thirds(router[...])
    gates = dot(hits, high) + (dot(hits, middle) + dot(hits, rest))
    slot = pl.program_id(0) * chunk + lax.broadcasted_iota(jnp.int32, (chunk, experts), 0)
    start = lax.broadcasted_iota(jnp.int32, (chunk, experts), 1) * slot_count
    own = (slot >= start) & (slot < start + slot_count)
    gate = jnp.sum(jnp.where(own, gates, 0.0), axis=1, keepdims=True)
    out[:, width:] = spread(gate)


def spread(column):
    high, middle, rest = thirds(jnp.broadcast_to(column, (column.shape[0], AUX)))
    lane = lax.broadcasted_iota(jnp.int32, (column.shape[0], AUX), 1)
    zero = jnp.zeros_like(high)
    return jnp.where(lane == 0, high, jnp.where(lane == 1, middle, jnp.where(lane == 2, rest, zero)))


def unspread(block):
    return jnp.sum(block.astype(F32), axis=1, keepdims=True)


def dispatch(columns, rows, router, slot_count, chunk=288):
    count, width = rows.shape
    return pl.pallas_call(
        functools.partial(dispatch_kernel, chunk, slot_count),
        grid=(count // chunk,),
        in_specs=[whole(columns), whole(rows), whole(router)],
        out_specs=pl.BlockSpec((chunk, width + AUX), lambda i: (i, 0)),
        out_shape=shape((count, width + AUX), BF16),
        compiler_params=params(),
        name="dispatch",
    )(columns, rows, router)


def raw_kernel(cotangent, weight_out, out):
    out[...] = dot_last(cotangent[...], weight_out[...]).astype(BF16)


def raw_active(cotangent, weight_out, chunk=512):
    count, width = cotangent.shape
    hidden = weight_out.shape[0]
    return pl.pallas_call(
        raw_kernel,
        grid=(hidden // chunk,),
        in_specs=[whole(cotangent), pl.BlockSpec((chunk, width), lambda i: (i, 0))],
        out_specs=pl.BlockSpec((count, chunk), lambda i: (0, i)),
        out_shape=shape((count, hidden), BF16),
        compiler_params=params(),
        name="raw_active",
    )(cotangent, weight_out)


def expert_kernel(
    row_chunk,
    arrived,
    cotangent,
    weight_in,
    bias_in,
    raw,
    bias_out,
    active_out,
    hidden_out,
    weight_grad,
    bias_grad,
    out_bias_grad,
    back,
    produced_grad,
    total,
    gate_total,
):
    step = pl.program_id(0)
    count, width = cotangent.shape

    @pl.when(step == 0)
    def _():
        gate = unspread(arrived[:, width:])
        gated = (gate * cotangent[...].astype(F32)).astype(BF16)
        produced_grad[...] = gated
        out_bias_grad[...] = column_sum(gated.astype(F32))
        total[...] = jnp.zeros_like(total)
        gate_total[...] = jnp.broadcast_to(
            jnp.sum(cotangent[...].astype(F32) * bias_out[...], axis=1, keepdims=True), gate_total.shape
        )

    sums = jnp.zeros(bias_grad.shape, F32)
    for at in range(0, count, row_chunk):
        rows = slice(at, at + row_chunk)
        gate = unspread(arrived[rows, width:])
        hidden = dot(arrived[rows, :width], weight_in[...]) + bias_in[...]
        cdf = 0.5 + 0.5 * lax.erf(hidden * (0.5**0.5))
        density = jnp.exp(hidden * hidden * -0.5) * (0.5 * 1.1283791670955126 * 0.5**0.5)
        active = (hidden * cdf).astype(BF16)
        incoming = raw[rows, :].astype(F32)
        gate_total[rows, :] += jnp.sum(active.astype(F32) * incoming, axis=1, keepdims=True)
        grad = (incoming * gate * (cdf + hidden * density)).astype(BF16)
        active_out[rows, :] = active
        hidden_out[rows, :] = grad
        sums += column_sum(grad.astype(F32))
        total[rows, :] += dot_last(grad, weight_in[...])
    bias_grad[...] = sums
    weight_grad[...] = dot_first(active_out[...], produced_grad[...]).astype(BF16)

    @pl.when(step == pl.num_programs(0) - 1)
    def _():
        back[:, :width] = total[...].astype(BF16)
        back[:, width:] = spread(gate_total[:, 0:1])


def expert(arrived, cotangent, weight_in, bias_in, raw, bias_out, chunk=512):
    count, width = cotangent.shape
    hidden = weight_in.shape[1]

    def column_block(rows):
        return pl.BlockSpec((rows, chunk), lambda i: (0, i))

    return pl.pallas_call(
        functools.partial(expert_kernel, 288),
        grid=(hidden // chunk,),
        in_specs=[
            whole(arrived),
            whole(cotangent),
            column_block(width),
            column_block(1),
            column_block(count),
            whole(bias_out),
        ],
        out_specs=[
            column_block(count),
            column_block(count),
            pl.BlockSpec((chunk, width), lambda i: (i, 0)),
            column_block(1),
            pl.BlockSpec((1, width), lambda i: (0, 0)),
            pl.BlockSpec((count, width + AUX), lambda i: (0, 0)),
        ],
        out_shape=[
            shape((count, hidden), BF16),
            shape((count, hidden), BF16),
            shape((hidden, width), BF16),
            shape((1, hidden), F32),
            shape((1, width), F32),
            shape((count, width + AUX), BF16),
        ],
        scratch_shapes=[
            pltpu.VMEM((count, width), BF16),
            pltpu.VMEM((count, width), F32),
            pltpu.VMEM((count, 128), F32),
        ],
        compiler_params=params(),
        name="expert",
    )(arrived, cotangent, weight_in, bias_in, raw, bias_out)


def weight_in_kernel(arrived, grad_hidden, bias_grad, out_bias_grad, out, turned):
    width = turned.shape[0]

    @pl.when(pl.program_id(0) == 0)
    def _():
        turned[...] = arrived[:, :width].T

    out[0, :width] = dot(turned[...], grad_hidden[...]).astype(BF16)
    row = lax.broadcasted_iota(jnp.int32, (out.shape[1] - width, out.shape[2]), 0)
    out[0, width:] = jnp.where(row == 0, bias_grad[...], jnp.where(row == 1, out_bias_grad[0], 0.0)).astype(BF16)


def weight_in_grad(arrived, grad_hidden, bias_grad, out_bias_grad, width, reps):
    count, hidden = grad_hidden.shape
    part = hidden // reps
    return pl.pallas_call(
        weight_in_kernel,
        grid=(reps,),
        in_specs=[
            whole(arrived),
            pl.BlockSpec((count, part), lambda i: (0, i)),
            pl.BlockSpec((1, part), lambda i: (0, i)),
            pl.BlockSpec((1, 1, part), lambda i: (i, 0, 0)),
        ],
        out_specs=pl.BlockSpec((1, width + 16, part), lambda i: (i, 0, 0)),
        out_shape=shape((reps, width + 16, part), BF16),
        scratch_shapes=[pltpu.VMEM((width, count), BF16)],
        compiler_params=params(),
        name="weight_in_grad",
    )(arrived, grad_hidden, bias_grad, out_bias_grad)


def produce_kernel(arrived, active, weight_out, bias_out, out):
    gate = unspread(arrived[...])
    out[...] = (gate * (dot(active[...], weight_out[...]) + bias_out[...])).astype(BF16)


def produce(arrived, active, weight_out, bias_out, chunk=288):
    count, hidden = active.shape
    width = weight_out.shape[1]
    return pl.pallas_call(
        produce_kernel,
        grid=(count // chunk,),
        in_specs=[
            pl.BlockSpec((chunk, AUX), lambda i: (i, width // AUX)),
            pl.BlockSpec((chunk, hidden), lambda i: (i, 0)),
            whole(weight_out),
            whole(bias_out),
        ],
        out_specs=pl.BlockSpec((chunk, width), lambda i: (i, 0)),
        out_shape=shape((count, width), BF16),
        compiler_params=params(),
        name="produce",
    )(arrived, active, weight_out, bias_out)


def token_hits(columns, slots):
    slot = lax.broadcasted_iota(jnp.int32, (columns.shape[0], slots), 1)
    hit = (columns[:, 0:1] == slot) | (columns[:, 1:2] == slot)
    return jnp.where(hit, 1.0, 0.0).astype(BF16)


def middle_kernel(
    slot_count,
    columns,
    source,
    router,
    normed_two,
    residual,
    cotangent,
    context,
    w_router,
    w_proj,
    gain_two,
    grad_residual_out,
    grad_context_out,
    proj_grad,
    vectors,
    router_grad,
    gate_side,
    proj_total,
):
    image = pl.program_id(0)
    slots = source.shape[0]
    experts, width = w_router.shape
    pairs = context.shape[1]

    @pl.when(image == 0)
    def _():
        gate = unspread(source[:, width:])
        slot = lax.broadcasted_iota(jnp.int32, (slots, experts), 0)
        start = lax.broadcasted_iota(jnp.int32, (slots, experts), 1) * slot_count
        own = (slot >= start) & (slot < start + slot_count)
        for at, part in enumerate(thirds(jnp.where(own, gate, 0.0))):
            gate_side[at] = part
        vectors[...] = jnp.zeros_like(vectors)
        router_grad[...] = jnp.zeros_like(router_grad)
        proj_total[...] = jnp.zeros_like(proj_total)

    hits = token_hits(columns, slots)
    grad_router = dot(hits, gate_side[0]) + (dot(hits, gate_side[1]) + dot(hits, gate_side[2]))
    probs = router[...]
    grad_logits = probs * (grad_router - jnp.sum(probs * grad_router, axis=1, keepdims=True))
    left = thirds(grad_logits)
    right = thirds(w_router[...])
    logits_part = dot(left[0], right[0])
    for one, other in ((0, 1), (1, 0), (1, 1), (0, 2), (2, 0)):
        logits_part += dot(left[one], right[other])
    grad_normed = dot(hits, source[:, :width]) + logits_part
    for part in left:
        router_grad[...] += dot_first(part, normed_two[...])
    unit, inverse = standardize(residual[...])
    grad_residual = cotangent[...].astype(F32) + standardize_back(grad_normed, gain_two[...], unit, inverse)
    grad_residual_out[...] = grad_residual
    branch = grad_residual.astype(BF16)
    vectors[0:1] += column_sum(grad_normed * unit)
    vectors[1:2] += column_sum(grad_normed)
    vectors[2:3] += column_sum(branch.astype(F32))
    for pair in range(pairs):
        rows = slice(pair * PAIR, (pair + 1) * PAIR)
        grad_context_out[0, pair] = dot_last(branch, w_proj[rows, :]).astype(BF16)
        proj_total[rows, :] += dot_first(context[0, pair], branch)
    proj_grad[...] = proj_total[...].astype(BF16)


def middle(columns, source, router, normed_two, residual, cotangent, context, w_router, w_proj, gain_two, slot_count):
    rows, width = residual.shape
    images, pairs = context.shape[:2]
    experts = router.shape[1]

    def per_image(columns):
        return pl.BlockSpec((SEQ, columns), lambda i: (i, 0))

    by_pair = pl.BlockSpec((1, pairs, SEQ, PAIR), lambda i: (i, 0, 0, 0))
    turned = w_router.T
    return pl.pallas_call(
        functools.partial(middle_kernel, slot_count),
        grid=(images,),
        in_specs=[
            per_image(2),
            whole(source),
            per_image(experts),
            per_image(width),
            per_image(width),
            per_image(width),
            by_pair,
            whole(turned),
            whole(w_proj),
            whole(gain_two),
        ],
        out_specs=[
            per_image(width),
            by_pair,
            pl.BlockSpec((width, width), lambda i: (0, 0)),
            pl.BlockSpec((8, width), lambda i: (0, 0)),
            pl.BlockSpec((experts, width), lambda i: (0, 0)),
        ],
        out_shape=[
            shape((rows, width), F32),
            shape((images, pairs, SEQ, PAIR), BF16),
            shape((width, width), BF16),
            shape((8, width), F32),
            shape((experts, width), F32),
        ],
        scratch_shapes=[pltpu.VMEM((3, rows, experts), BF16), pltpu.VMEM((width, width), F32)],
        compiler_params=params(),
        name="middle",
    )(columns, source, router, normed_two, residual, cotangent, context, turned, w_proj, gain_two)


def merge_heads(turned):
    first = jnp.concatenate([turned[:HEAD_DIM, :SPLIT], turned[:HEAD_DIM, 2 * SPLIT : SPLIT + SEQ]], axis=1)
    second = jnp.concatenate([turned[HEAD_DIM:, SPLIT : 2 * SPLIT], turned[HEAD_DIM:, SPLIT + SEQ :]], axis=1)
    return jnp.concatenate([first, second], axis=0).T


def attend_back_kernel(
    chunk,
    grad_context,
    queries,
    keys,
    values,
    weights,
    inverse,
    context,
    normed_one,
    grad_out,
    weight_grad,
    value_side,
    grad_scores,
):
    pair = pl.program_id(0)
    image = pl.program_id(1)

    @pl.when((pair == 0) & (image == 0))
    def _():
        is_first, lane = key_sides()
        taken = (is_first & (lane < 2)) | (jnp.logical_not(is_first) & (lane >= 2) & (lane < 4))
        value_side[:, PAIR:] = jnp.where(taken, -1.0, 0.0).astype(BF16)

    key_side = split_heads(keys[0, 0])
    value_side[:, :PAIR] = split_heads(values[0, 0])
    lane = lax.broadcasted_iota(jnp.int32, (chunk, PAIR), 1)
    low = lane < HEAD_DIM
    scaled = []
    for at in range(0, SEQ, chunk):
        rows = slice(at, at + chunk)
        grads = (grad_context[0, 0, rows].astype(F32) * inverse[0, 0, rows]).astype(BF16)
        scaled.append(grads)
        product = grads.astype(F32) * context[0, 0, rows].astype(F32)
        first = jnp.sum(jnp.where(low, product, 0.0), axis=1, keepdims=True)
        second = jnp.sum(jnp.where(low, 0.0, product), axis=1, keepdims=True)
        offset = jnp.where(lane < 2, first, second)
        high = offset.astype(BF16).astype(F32)
        extra = jnp.where(
            (lane == 0) | (lane == 2), high, jnp.where((lane == 1) | (lane == 3), offset - high, 0.0)
        ).astype(BF16)
        grad_weights = dot_last(jnp.concatenate([grads, extra], axis=1), value_side[...])
        part = grad_weights.astype(BF16) * weights[0, 0, rows]
        grad_scores[rows] = part
        place = pl.ds(pl.multiple_of(image * SEQ + at, 32), chunk)
        grad_out[0, pair, place] = (dot(part, key_side) * HEAD_DIM**-0.5).astype(BF16)
    grads = jnp.concatenate(scaled, axis=0)
    place = pl.ds(pl.multiple_of(image * SEQ, 64), SEQ)
    grad_out[1, pair, place] = merge_heads(dot_first(queries[0, 0], grad_scores[...])).astype(BF16)
    grad_out[2, pair, place] = merge_heads(dot_first(grads, weights[0, 0])).astype(BF16)

    @pl.when((pair == pl.num_programs(0) - 1) & (image == pl.num_programs(1) - 1))
    def _():
        for kind in range(3):
            joined = jnp.concatenate([grad_out[kind, at] for at in range(grad_out.shape[1])], axis=1)
            weight_grad[kind] = dot_first(normed_one[...], joined).astype(BF16)


def attend_back(grad_context, qkv, weights, inverse, context, normed_one, first, count):
    images, pairs = context.shape[:2]
    rows, width = normed_one.shape

    def block(offset):
        return pl.BlockSpec((1, 1, SEQ, PAIR), lambda p, i: (i, offset + p, 0, 0))

    return pl.pallas_call(
        functools.partial(attend_back_kernel, SEQ),
        grid=(count, images),
        in_specs=[
            block(first),
            block(first),
            block(pairs + first),
            block(2 * pairs + first),
            pl.BlockSpec((1, 1, SEQ, 2 * SEQ), lambda p, i: (i, first + p, 0, 0)),
            block(first),
            block(first),
            whole(normed_one),
        ],
        out_specs=[
            pl.BlockSpec((3, count, rows, PAIR), lambda p, i: (0, 0, 0, 0)),
            pl.BlockSpec((3, width, count * PAIR), lambda p, i: (0, 0, 0)),
        ],
        out_shape=[shape((3, count, rows, PAIR), BF16), shape((3, width, count * PAIR), BF16)],
        scratch_shapes=[pltpu.VMEM((2 * SEQ, 2 * PAIR), BF16), pltpu.VMEM((SEQ, 2 * SEQ), BF16)],
        compiler_params=params(),
        name="attend_back",
    )(grad_context, qkv, qkv, qkv, weights, inverse, context, normed_one)


def last_kernel(tokens, grad_qkv, w_qkv, grad_residual, gain_one, out, vectors):
    width = tokens.shape[1]
    pairs = width // PAIR

    @pl.when(pl.program_id(0) == 0)
    def _():
        vectors[...] = jnp.zeros_like(vectors)

    unit, inverse = standardize(tokens[...].astype(F32))
    grad_normed = jnp.zeros(tokens.shape, F32)
    for kind in range(3):
        joined = jnp.concatenate([grad_qkv[kind, at] for at in range(pairs)], axis=1)
        grad_normed += dot_last(joined, w_qkv[:, kind * width : (kind + 1) * width])
        if kind == 0:
            vectors[2:3] += column_sum(joined.astype(F32))
        if kind == 2:
            vectors[3:4] += column_sum(joined.astype(F32))
    out[...] = grad_residual[...] + standardize_back(grad_normed, gain_one[...], unit, inverse)
    vectors[0:1] += column_sum(grad_normed * unit)
    vectors[1:2] += column_sum(grad_normed)


def last(tokens, grad_qkv, w_qkv, grad_residual, gain_one):
    rows, width = tokens.shape
    pairs = width // PAIR
    per_image = pl.BlockSpec((SEQ, width), lambda i: (i, 0))
    return pl.pallas_call(
        last_kernel,
        grid=(rows // SEQ,),
        in_specs=[
            per_image,
            pl.BlockSpec((3, pairs, SEQ, PAIR), lambda i: (0, 0, i, 0)),
            whole(w_qkv),
            per_image,
            whole(gain_one),
        ],
        out_specs=[per_image, pl.BlockSpec((8, width), lambda i: (0, 0))],
        out_shape=[shape((rows, width), F32), shape((8, width), F32)],
        compiler_params=params(),
        name="last",
    )(tokens, grad_qkv, w_qkv, grad_residual, gain_one)


def combine_kernel(columns, source, residual, out):
    hits = token_hits(columns, source.shape[0])
    out[...] = (residual[...] + dot(hits, source[...])).astype(BF16)


def combine(columns, source, residual, chunk=288):
    rows, width = residual.shape
    return pl.pallas_call(
        combine_kernel,
        grid=(rows // chunk,),
        in_specs=[
            pl.BlockSpec((chunk, 2), lambda i: (i, 0)),
            whole(source),
            pl.BlockSpec((chunk, width), lambda i: (i, 0)),
        ],
        out_specs=pl.BlockSpec((chunk, width), lambda i: (i, 0)),
        out_shape=shape((rows, width), BF16),
        compiler_params=params(),
        name="combine",
    )(columns, source, residual)


def exchange(rows, experts):
    blocks = rows.reshape(experts, rows.shape[0] // experts, rows.shape[1])
    return lax.all_to_all(blocks, "exp", split_axis=0, concat_axis=0, tiled=True).reshape(rows.shape)


def axis_steps(sizes, swap):
    steps = []
    for name in ("exp", "rep"):
        bits = []
        bit = 1
        while bit < sizes[name]:
            bits.append((name, bit))
            bit *= 2
        if swap and name == "exp" and len(bits) > 2:
            bits[1], bits[2] = bits[2], bits[1]
        steps += bits
    return steps


def sum_everywhere(block, sizes, swap):
    steps = axis_steps(sizes, swap)
    sides = []
    for name, bit in steps:
        side = (lax.axis_index(name) // bit) % 2
        sides.append(side)
        pairs = [(at, at ^ bit) for at in range(sizes[name])]
        halves = block.reshape((2, block.shape[0] // 2) + block.shape[1:])
        kept = lax.dynamic_index_in_dim(halves, side, 0, keepdims=False)
        sent = lax.dynamic_index_in_dim(halves, 1 - side, 0, keepdims=False)
        received = lax.ppermute(sent, name, pairs)
        block = (kept.astype(F32) + received.astype(F32)).astype(BF16)
    for (name, bit), side in zip(reversed(steps), reversed(sides)):
        pairs = [(at, at ^ bit) for at in range(sizes[name])]
        received = lax.ppermute(block, name, pairs)
        block = jnp.where(side == 0, jnp.stack([block, received]), jnp.stack([received, block]))
        block = block.reshape((-1,) + block.shape[2:])
    return block


def sum_two_ways(block, sizes):
    half = block.shape[0] // 2
    return jnp.concatenate(
        [sum_everywhere(block[:half], sizes, False), sum_everywhere(block[half:], sizes, True)], axis=0
    )


def padded(rows, total):
    return jnp.pad(rows, ((0, total - rows.shape[0]), (0, 0)))


def on_device(
    sizes,
    tokens,
    cotangent,
    expert_ids,
    expert_slots,
    w_qkv,
    q_bias,
    v_bias,
    w_proj,
    proj_bias,
    gain_one,
    shift_one,
    gain_two,
    shift_two,
    w_router,
    expert_in,
    expert_in_bias,
    expert_out,
    expert_out_bias,
):
    row_count, width = tokens.shape
    experts = w_router.shape[1]
    slot_count = row_count // experts
    reps = sizes["rep"]
    gain_one, shift_one, gain_two, shift_two = (
        row[None] for row in (gain_one, shift_one, gain_two, shift_two)
    )
    bias = jnp.concatenate([q_bias.astype(F32), jnp.zeros((width,), F32), v_bias.astype(F32)])[None]
    columns = jnp.where(expert_slots >= 0, expert_ids * slot_count + expert_slots, -1)
    turned = columns.T
    weight_in = expert_in[0]
    weight_out = expert_out[0]
    bias_in = expert_in_bias.astype(F32)
    bias_out = expert_out_bias.astype(F32)

    cot_arrived = exchange(gather(turned, cotangent), experts)
    normed_one, qkv, weights, inverse, context, residual, normed_two, router = front(
        tokens,
        w_qkv,
        bias,
        w_proj,
        proj_bias.astype(F32)[None],
        gain_one,
        shift_one,
        gain_two,
        shift_two,
        w_router,
    )
    arrived = exchange(dispatch(turned, normed_two, router, slot_count), experts)
    raw = raw_active(cot_arrived, weight_out)
    active, grad_hidden, out_grad, in_bias_grad, out_bias_grad, back = expert(
        arrived, cot_arrived, weight_in, bias_in, raw, bias_out
    )
    grad_eout = lax.psum_scatter(out_grad, "rep", scatter_dimension=0, tiled=True)
    source = exchange(back, experts)
    part = weight_in.shape[1] // reps
    out_part = width // reps
    tail = jnp.pad(out_bias_grad.reshape(reps, 1, out_part), ((0, 0), (0, 0), (0, part - out_part)))
    in_grad = weight_in_grad(arrived, grad_hidden, in_bias_grad, tail, width, reps)
    packed_in = lax.psum_scatter(
        in_grad.reshape(reps * (width + 16), part), "rep", scatter_dimension=0, tiled=True
    )
    returned = exchange(produce(arrived, active, weight_out, bias_out), experts)
    grad_residual, grad_context, proj_grad, vectors_two, router_grad = middle(
        columns, source, router, normed_two, residual, cotangent, context, w_router, w_proj, gain_two, slot_count
    )
    grain = 2 * 16 * sizes["rep"] * sizes["exp"]
    early = jnp.concatenate([proj_grad, vectors_two.astype(BF16), router_grad.astype(BF16)], axis=0)
    early = sum_two_ways(padded(early, -(-early.shape[0] // grain) * grain), sizes)
    grad_qkv, qkv_grad = attend_back(
        grad_context, qkv, weights, inverse, context, normed_one, 0, width // PAIR
    )
    mixed = combine(columns, returned, residual)
    grad_tokens, vectors_one = last(tokens, grad_qkv, w_qkv, grad_residual, gain_one)
    late = jnp.concatenate([qkv_grad.reshape(3 * width, width), vectors_one.astype(BF16)], axis=0)
    late = sum_two_ways(padded(late, -(-late.shape[0] // grain) * grain), sizes)
    grad_w_qkv = jnp.transpose(late[: 3 * width].reshape(3, width, width), (1, 0, 2)).reshape(width, 3 * width)
    vectors_one = late[3 * width : 3 * width + 8].astype(F32)
    vectors_two = early[width : width + 8].astype(F32)
    return (
        mixed,
        grad_tokens,
        grad_w_qkv.astype(F32),
        vectors_one[2],
        vectors_one[3],
        early[:width].astype(F32),
        vectors_two[2],
        vectors_one[0],
        vectors_one[1],
        vectors_two[0],
        vectors_two[1],
        early[width + 8 : width + 8 + experts].astype(F32).T,
        packed_in[None, :width].astype(F32),
        packed_in[width : width + 1].astype(F32),
        grad_eout[None].astype(F32),
        packed_in[width + 1 : width + 2, :out_part].astype(F32),
    )


def solution(mesh):
    rows = P(("rep", "exp"), None)
    placed = (rows,) * 4 + (P(),) * 10 + (
        P("exp", None, None),
        P("exp", None),
        P("exp", None, None),
        P("exp", None),
    )
    return jax.shard_map(
        functools.partial(on_device, dict(mesh.shape)),
        mesh=mesh,
        in_specs=placed,
        out_specs=(rows, rows)
        + (P(),) * 10
        + (P("exp", None, "rep"), P("exp", "rep"), P("exp", "rep", None), P("exp", "rep")),
        check_vma=False,
    )
```

```python
import functools

import jax
import jax.numpy as jnp
from jax import lax
from jax.experimental import pallas as pl
from jax.experimental.pallas import tpu as pltpu
from jax.sharding import PartitionSpec as P

HEAD_DIM = 64
SEQ = 576
PAIR = 2 * HEAD_DIM
SPLIT = 512
AUX = 128
EPSILON = 1e-06
F32 = jnp.float32
BF16 = jnp.bfloat16
VMEM_BYTES = 56 * 2**20


def dot(left, right):
    return lax.dot_general(left, right, (((1,), (0,)), ((), ())), preferred_element_type=F32)


def dot_last(left, right):
    return lax.dot_general(left, right, (((1,), (1,)), ((), ())), preferred_element_type=F32)


def dot_first(left, right):
    return lax.dot_general(left, right, (((0,), (0,)), ((), ())), preferred_element_type=F32)


def thirds(value):
    high = value.astype(BF16)
    rest = value - high.astype(F32)
    middle = rest.astype(BF16)
    return high, middle, (rest - middle.astype(F32)).astype(BF16)


def standardize(field):
    centred = field - jnp.mean(field, axis=-1, keepdims=True)
    inverse = lax.rsqrt(jnp.mean(centred * centred, axis=-1, keepdims=True) + EPSILON)
    return centred * inverse, inverse


def standardize_back(grad, gain, unit, inverse):
    scaled = grad * gain
    along = jnp.mean(scaled * unit, axis=-1, keepdims=True)
    return inverse * (scaled - jnp.mean(scaled, axis=-1, keepdims=True) - unit * along)


def as_row(ref):
    return ref[...].astype(F32).reshape(1, -1)


def column_sum(field):
    return jnp.sum(field, axis=0, keepdims=True)


def params():
    return pltpu.CompilerParams(vmem_limit_bytes=VMEM_BYTES)


SCALE = 0.01


def cost(flops, bytes_moved):
    return pl.CostEstimate(flops=int(flops * SCALE), transcendentals=0, bytes_accessed=int(bytes_moved * SCALE))


def whole(array):
    return pl.BlockSpec(array.shape, lambda *ids: (0,) * array.ndim)


def shape(dims, kind):
    return jax.ShapeDtypeStruct(dims, kind)


def split_heads(pair):
    lane = lax.broadcasted_iota(jnp.int32, pair.shape, 1)
    zero = jnp.zeros_like(pair)
    first = jnp.where(lane < HEAD_DIM, pair, zero)
    second = jnp.where(lane < HEAD_DIM, zero, pair)
    return jnp.concatenate([first[:SPLIT], second[:SPLIT], first[SPLIT:], second[SPLIT:]], axis=0)


def key_sides():
    row = lax.broadcasted_iota(jnp.int32, (2 * SEQ, PAIR), 0)
    lane = lax.broadcasted_iota(jnp.int32, (2 * SEQ, PAIR), 1)
    is_first = (row < SPLIT) | ((row >= 2 * SPLIT) & (row < SPLIT + SEQ))
    return is_first, lane


def front_kernel(
    chunk,
    tokens,
    w_qkv,
    q_bias,
    v_bias,
    w_proj,
    proj_bias,
    gain_one,
    shift_one,
    gain_two,
    shift_two,
    normed_one_out,
    qkv_out,
    weights_out,
    inverse_out,
    context_out,
    residual_out,
    normed_two_out,
    value_side,
):
    pair = pl.program_id(1)
    pairs = context_out.shape[1]

    @pl.when((pl.program_id(0) == 0) & (pair == 0))
    def _():
        is_first, lane = key_sides()
        value_side[:, PAIR:] = jnp.where(is_first == (lane < HEAD_DIM), 1.0, 0.0).astype(BF16)

    @pl.when(pair == 0)
    def _():
        unit, _ = standardize(tokens[...].astype(F32))
        normed = (unit * as_row(gain_one) + as_row(shift_one)).astype(BF16)
        normed_one_out[...] = normed
        width = w_qkv.shape[1]
        step = 2 * PAIR
        for at in range(0, width, step):
            part = dot(normed, w_qkv[:, at : at + step])
            third = width // 3
            if at < third:
                part = part + as_row(q_bias)[:, at : at + step]
            if at >= 2 * third:
                part = part + as_row(v_bias)[:, at - 2 * third : at - 2 * third + step]
            part = part.astype(BF16)
            if at < third:
                part = part * jnp.asarray(HEAD_DIM**-0.5, BF16)
            qkv_out[0, at // PAIR] = part[:, :PAIR]
            qkv_out[0, at // PAIR + 1] = part[:, PAIR:]

    keys = split_heads(qkv_out[0, pairs + pair])
    value_side[:, :PAIR] = split_heads(qkv_out[0, 2 * pairs + pair])
    values = value_side[...]
    low = lax.broadcasted_iota(jnp.int32, (chunk, PAIR), 1) < HEAD_DIM
    for at in range(0, SEQ, chunk):
        rows = slice(at, at + chunk)
        scores = dot_last(qkv_out[0, pair, rows], keys)
        first = scores[:, :SPLIT]
        second = scores[:, SPLIT : 2 * SPLIT]
        tail = scores[:, 2 * SPLIT :]
        first_max = jnp.maximum(
            jnp.max(first, axis=1, keepdims=True),
            jnp.max(jnp.where(low, tail, -jnp.inf), axis=1, keepdims=True),
        )
        second_max = jnp.maximum(
            jnp.max(second, axis=1, keepdims=True),
            jnp.max(jnp.where(low, -jnp.inf, tail), axis=1, keepdims=True),
        )
        exponent = jnp.concatenate(
            [
                jnp.exp(first - first_max).astype(BF16),
                jnp.exp(second - second_max).astype(BF16),
                jnp.exp(tail - jnp.where(low, first_max, second_max)).astype(BF16),
            ],
            axis=1,
        )
        weights_out[0, 0, rows] = exponent
        summed = dot(exponent, values)
        inverse = 1.0 / summed[:, PAIR:]
        inverse_out[0, 0, rows] = inverse
        context_out[0, pair, rows] = (summed[:, :PAIR] * inverse).astype(BF16)

    @pl.when(pair == pairs - 1)
    def _():
        context = jnp.concatenate([context_out[0, at] for at in range(pairs)], axis=1)
        residual = tokens[...].astype(F32) + (dot(context, w_proj[...]) + as_row(proj_bias))
        residual_out[...] = residual
        unit, _ = standardize(residual)
        normed = (unit * as_row(gain_two) + as_row(shift_two)).astype(BF16)
        normed_two_out[...] = normed


def front(tokens, w_qkv, q_bias, v_bias, w_proj, proj_bias, gain_one, shift_one, gain_two, shift_two):
    rows, width = tokens.shape
    images = rows // SEQ
    pairs = width // PAIR

    def per_image(columns):
        return pl.BlockSpec((SEQ, columns), lambda i, p: (i, 0))

    fixed = (w_qkv, q_bias, v_bias, w_proj, proj_bias, gain_one, shift_one, gain_two, shift_two)
    return pl.pallas_call(
        functools.partial(front_kernel, SEQ // 2),
        grid=(images, pairs),
        in_specs=[per_image(width)] + [whole(array) for array in fixed],
        out_specs=[
            per_image(width),
            pl.BlockSpec((1, 3 * pairs, SEQ, PAIR), lambda i, p: (i, 0, 0, 0)),
            pl.BlockSpec((1, 1, SEQ, 2 * SEQ), lambda i, p: (i, p, 0, 0)),
            pl.BlockSpec((1, 1, SEQ, PAIR), lambda i, p: (i, p, 0, 0)),
            pl.BlockSpec((1, pairs, SEQ, PAIR), lambda i, p: (i, 0, 0, 0)),
            per_image(width),
            per_image(width),
        ],
        out_shape=[
            shape((rows, width), BF16),
            shape((images, 3 * pairs, SEQ, PAIR), BF16),
            shape((images, pairs, SEQ, 2 * SEQ), BF16),
            shape((images, pairs, SEQ, PAIR), F32),
            shape((images, pairs, SEQ, PAIR), BF16),
            shape((rows, width), F32),
            shape((rows, width), BF16),
        ],
        scratch_shapes=[pltpu.VMEM((2 * SEQ, 2 * PAIR), BF16)],
        compiler_params=params(),
        cost_estimate=cost(30e9, 60e6),
        name="front",
    )(tokens, *fixed)


def columns_of(ids, slots, slot_count):
    return jnp.where(slots[...] >= 0, ids[...] * slot_count + slots[...], -1)


def gather_kernel(chunk, slot_count, ids, slots, rows, out):
    columns = columns_of(ids, slots, slot_count)
    at = pl.program_id(0) * chunk
    slot = at + lax.broadcasted_iota(jnp.int32, (chunk, columns.shape[1]), 0)
    hit = (columns[0:1, :] == slot) | (columns[1:2, :] == slot)
    out[...] = dot(jnp.where(hit, 1.0, 0.0).astype(BF16), rows[...]).astype(BF16)


def gather(ids, slots, rows, slot_count, chunk=288):
    count, width = rows.shape
    return pl.pallas_call(
        functools.partial(gather_kernel, chunk, slot_count),
        grid=(count // chunk,),
        in_specs=[whole(ids), whole(slots), whole(rows)],
        out_specs=pl.BlockSpec((chunk, width), lambda i: (i, 0)),
        out_shape=shape((count, width), BF16),
        compiler_params=params(),
        cost_estimate=cost(4e9, 8e6),
        name="gather",
    )(ids, slots, rows)


def raw_kernel(slot_count, ids, slots, cotangent, weight_out, out, columns_out):
    @pl.when(pl.program_id(0) == 0)
    def _():
        columns = columns_of(ids, slots, slot_count)
        pad = jnp.full((6, columns.shape[1]), -1, jnp.int32)
        columns_out[...] = jnp.concatenate([columns, pad], axis=0).T

    out[...] = dot_last(cotangent[...], weight_out[...]).astype(BF16)


def raw_active(ids, slots, cotangent, weight_out, slot_count, chunk=768):
    count, width = cotangent.shape
    hidden = weight_out.shape[0]
    return pl.pallas_call(
        functools.partial(raw_kernel, slot_count),
        grid=(hidden // chunk,),
        in_specs=[whole(ids), whole(slots), whole(cotangent), pl.BlockSpec((chunk, width), lambda i: (i, 0))],
        out_specs=[pl.BlockSpec((count, chunk), lambda i: (0, i)), pl.BlockSpec((count, 8), lambda i: (0, 0))],
        out_shape=[shape((count, hidden), BF16), shape((count, 8), jnp.int32)],
        compiler_params=params(),
        cost_estimate=cost(9e9, 14e6),
        name="raw_active",
    )(ids, slots, cotangent, weight_out)


def product_six(left, right):
    total = dot(left[0], right[0])
    for one, other in ((0, 1), (1, 0), (1, 1), (0, 2), (2, 0)):
        total += dot(left[one], right[other])
    return total


def expert_kernel(
    row_chunk,
    arrived,
    cotangent,
    weight_in,
    bias_in,
    raw,
    bias_out,
    w_router,
    active_out,
    hidden_out,
    weight_grad,
    bias_grad,
    out_bias_grad,
    gate_out,
    logits_grad,
    produced_grad,
    gate_total,
    router,
):
    step = pl.program_id(0)
    count = cotangent.shape[0]
    experts = w_router.shape[0]

    @pl.when(step == 0)
    def _():
        parts = thirds(w_router[...])
        logits = dot_last(arrived[...], parts[0]) + (
            dot_last(arrived[...], parts[1]) + dot_last(arrived[...], parts[2])
        )
        exponent = jnp.exp(logits - jnp.max(logits, axis=1, keepdims=True))
        probs = exponent / jnp.sum(exponent, axis=1, keepdims=True)
        router[...] = probs
        own = lax.broadcasted_iota(jnp.int32, (count, experts), 1) == lax.axis_index("exp")
        gate = jnp.sum(jnp.where(own, probs, 0.0), axis=1, keepdims=True)
        gate_out[...] = jnp.broadcast_to(gate, gate_out.shape)
        rows = cotangent[...].astype(F32)
        gated = (gate * rows).astype(BF16)
        produced_grad[...] = gated
        out_bias_grad[...] = column_sum(gated.astype(F32))
        along = jnp.sum(rows * bias_out[...], axis=1, keepdims=True)
        gate_total[...] = jnp.broadcast_to(along, gate_total.shape)

    sums = jnp.zeros(bias_grad.shape, F32)
    for at in range(0, count, row_chunk):
        rows = slice(at, at + row_chunk)
        hidden = dot(arrived[rows, :], weight_in[...]) + bias_in[...]
        cdf = 0.5 + 0.5 * lax.erf(hidden * (0.5**0.5))
        density = jnp.exp(hidden * hidden * -0.5) * (0.5 * 1.1283791670955126 * 0.5**0.5)
        active = (hidden * cdf).astype(BF16)
        incoming = raw[rows, :].astype(F32)
        gate_total[rows, :] += jnp.sum(active.astype(F32) * incoming, axis=1, keepdims=True)
        grad = (incoming * gate_out[rows, 0:1] * (cdf + hidden * density)).astype(BF16)
        active_out[rows, :] = active
        hidden_out[rows, :] = grad
        sums += column_sum(grad.astype(F32))
    bias_grad[...] = sums
    weight_grad[...] = dot_first(active_out[...], produced_grad[...]).astype(BF16)

    @pl.when(step == pl.num_programs(0) - 1)
    def _():
        own = lax.broadcasted_iota(jnp.int32, (count, experts), 1) == lax.axis_index("exp")
        scale = gate_total[:, 0:1] * gate_out[:, 0:1]
        logits_grad[...] = scale * (jnp.where(own, 1.0, 0.0) - router[...])


def expert(arrived, cotangent, weight_in, bias_in, raw, bias_out, w_router, chunk=512):
    count, width = cotangent.shape
    hidden = weight_in.shape[1]
    experts = w_router.shape[0]

    def column_block(rows):
        return pl.BlockSpec((rows, chunk), lambda i: (0, i))

    def fixed(rows, columns):
        return pl.BlockSpec((rows, columns), lambda i: (0, 0))

    return pl.pallas_call(
        functools.partial(expert_kernel, 288),
        grid=(hidden // chunk,),
        in_specs=[
            whole(arrived),
            whole(cotangent),
            column_block(width),
            column_block(1),
            column_block(count),
            whole(bias_out),
            whole(w_router),
        ],
        out_specs=[
            column_block(count),
            column_block(count),
            pl.BlockSpec((chunk, width), lambda i: (i, 0)),
            column_block(1),
            fixed(1, width),
            fixed(count, AUX),
            fixed(count, experts),
        ],
        out_shape=[
            shape((count, hidden), BF16),
            shape((count, hidden), BF16),
            shape((hidden, width), BF16),
            shape((1, hidden), F32),
            shape((1, width), F32),
            shape((count, AUX), F32),
            shape((count, experts), F32),
        ],
        scratch_shapes=[
            pltpu.VMEM((count, width), BF16),
            pltpu.VMEM((count, 128), F32),
            pltpu.VMEM((count, experts), F32),
        ],
        compiler_params=params(),
        cost_estimate=cost(24e9, 35e6),
        name="expert",
    )(arrived, cotangent, weight_in, bias_in, raw, bias_out, w_router)


def expert_back_kernel(grad_hidden, weight_in, logits_grad, w_router, arrived, out, router_grad):
    @pl.when(pl.program_id(0) == 0)
    def _():
        router_grad[...] = jnp.zeros_like(router_grad)

    left = thirds(logits_grad[...])
    total = dot_last(grad_hidden[...], weight_in[...]) + product_six(left, thirds(w_router[...]))
    out[...] = total.astype(BF16)
    for part in left:
        router_grad[...] += dot_first(part, arrived[...])


def expert_back(grad_hidden, weight_in, logits_grad, w_router, arrived, chunk=288):
    count, hidden = grad_hidden.shape
    experts, width = w_router.shape

    def rows(columns):
        return pl.BlockSpec((chunk, columns), lambda i: (i, 0))

    return pl.pallas_call(
        expert_back_kernel,
        grid=(count // chunk,),
        in_specs=[rows(hidden), whole(weight_in), rows(experts), whole(w_router), rows(width)],
        out_specs=[rows(width), pl.BlockSpec((experts, width), lambda i: (0, 0))],
        out_shape=[shape((count, width), BF16), shape((experts, width), F32)],
        compiler_params=params(),
        cost_estimate=cost(12e9, 15e6),
        name="expert_back",
    )(grad_hidden, weight_in, logits_grad, w_router, arrived)


def weight_in_kernel(arrived, grad_hidden, bias_grad, out_bias_grad, first, second, turned):
    width = turned.shape[0]
    half = width // 2

    @pl.when(pl.program_id(0) == 0)
    def _():
        turned[...] = arrived[...].T

    total = dot(turned[...], grad_hidden[...]).astype(BF16)
    first[0] = total[:half]
    second[0, :half] = total[half:]
    row = lax.broadcasted_iota(jnp.int32, (second.shape[1] - half, second.shape[2]), 0)
    second[0, half:] = jnp.where(row == 0, bias_grad[...], jnp.where(row == 1, out_bias_grad[0], 0.0)).astype(BF16)


def weight_in_grad(arrived, grad_hidden, bias_grad, out_bias_grad, width, reps):
    count, hidden = grad_hidden.shape
    part = hidden // reps
    return pl.pallas_call(
        weight_in_kernel,
        grid=(reps,),
        in_specs=[
            whole(arrived),
            pl.BlockSpec((count, part), lambda i: (0, i)),
            pl.BlockSpec((1, part), lambda i: (0, i)),
            pl.BlockSpec((1, 1, part), lambda i: (i, 0, 0)),
        ],
        out_specs=[
            pl.BlockSpec((1, width // 2, part), lambda i: (i, 0, 0)),
            pl.BlockSpec((1, width // 2 + 16, part), lambda i: (i, 0, 0)),
        ],
        out_shape=[shape((reps, width // 2, part), BF16), shape((reps, width // 2 + 16, part), BF16)],
        scratch_shapes=[pltpu.VMEM((width, count), BF16)],
        compiler_params=params(),
        cost_estimate=cost(10e9, 15e6),
        name="weight_in_grad",
    )(arrived, grad_hidden, bias_grad, out_bias_grad)


def produce_kernel(gate, active, weight_out, bias_out, out):
    out[...] = (gate[:, 0:1] * (dot(active[...], weight_out[...]) + bias_out[...])).astype(BF16)


def produce(gate, active, weight_out, bias_out, chunk=288):
    count, hidden = active.shape
    width = weight_out.shape[1]
    return pl.pallas_call(
        produce_kernel,
        grid=(count // chunk,),
        in_specs=[
            pl.BlockSpec((chunk, AUX), lambda i: (i, 0)),
            pl.BlockSpec((chunk, hidden), lambda i: (i, 0)),
            whole(weight_out),
            whole(bias_out),
        ],
        out_specs=pl.BlockSpec((chunk, width), lambda i: (i, 0)),
        out_shape=shape((count, width), BF16),
        compiler_params=params(),
        cost_estimate=cost(10e9, 15e6),
        name="produce",
    )(gate, active, weight_out, bias_out)


def token_hits(columns, slots):
    slot = lax.broadcasted_iota(jnp.int32, (columns.shape[0], slots), 1)
    hit = (columns[:, 0:1] == slot) | (columns[:, 1:2] == slot)
    return jnp.where(hit, 1.0, 0.0).astype(BF16)


def split_rows(value, kept, sent):
    half = value.shape[0] // 2
    first = (lax.axis_index("exp") & 1) == 0
    low, high = value[:half], value[half:]
    kept[...] = jnp.where(first, low, high)
    sent[...] = jnp.where(first, high, low)


def middle_kernel(
    sub,
    columns,
    source,
    residual,
    cotangent,
    context,
    w_proj,
    gain_two,
    grad_residual_out,
    grad_context_out,
    proj_kept,
    proj_sent,
    vectors,
    branch,
    proj_total,
):
    step = pl.program_id(0)
    chunk = residual.shape[0]
    pairs = context.shape[1]

    @pl.when(step == 0)
    def _():
        vectors[...] = jnp.zeros_like(vectors)
        proj_total[...] = jnp.zeros_like(proj_total)

    hits = token_hits(columns, source.shape[0])
    grad_residual_out[...] = dot(hits, source[...])
    gain = as_row(gain_two)
    for at in range(0, chunk, sub):
        rows = slice(at, at + sub)
        grad_normed = grad_residual_out[rows, :]
        unit, inverse = standardize(residual[rows, :])
        grad_residual = cotangent[rows, :].astype(F32) + standardize_back(grad_normed, gain, unit, inverse)
        grad_residual_out[rows, :] = grad_residual
        rounded = grad_residual.astype(BF16)
        branch[rows, :] = rounded
        vectors[0:1] += column_sum(grad_normed * unit)
        vectors[1:2] += column_sum(grad_normed)
        vectors[2:3] += column_sum(rounded.astype(F32))
    grad_context = dot_last(branch[...], w_proj[...]).astype(BF16)
    for pair in range(pairs):
        grad_context_out[0, pair] = grad_context[:, pair * PAIR : (pair + 1) * PAIR]
    joined = jnp.concatenate([context[0, pair] for pair in range(pairs)], axis=1)
    proj_total[...] += dot_first(joined, branch[...])

    @pl.when(step == pl.num_programs(0) - 1)
    def _():
        split_rows(proj_total[...].astype(BF16), proj_kept, proj_sent)


def middle(columns, source, residual, cotangent, context, w_proj, gain_two, chunk=288):
    rows, width = residual.shape
    images, pairs = context.shape[:2]
    parts = SEQ // chunk

    def rows_of(columns):
        return pl.BlockSpec((chunk, columns), lambda i: (i, 0))

    by_pair = pl.BlockSpec((1, pairs, chunk, PAIR), lambda i: (i // parts, 0, i % parts, 0))
    return pl.pallas_call(
        functools.partial(middle_kernel, 32),
        grid=(rows // chunk,),
        in_specs=[
            rows_of(8),
            whole(source),
            rows_of(width),
            rows_of(width),
            by_pair,
            whole(w_proj),
            whole(gain_two),
        ],
        out_specs=[
            rows_of(width),
            by_pair,
            pl.BlockSpec((width // 2, width), lambda i: (0, 0)),
            pl.BlockSpec((width // 2, width), lambda i: (0, 0)),
            pl.BlockSpec((8, width), lambda i: (0, 0)),
        ],
        out_shape=[
            shape((rows, width), F32),
            shape((images, pairs, SEQ, PAIR), BF16),
            shape((width // 2, width), BF16),
            shape((width // 2, width), BF16),
            shape((8, width), F32),
        ],
        scratch_shapes=[pltpu.VMEM((chunk, width), BF16), pltpu.VMEM((width, width), F32)],
        compiler_params=params(),
        cost_estimate=cost(14e9, 20e6),
        name="middle",
    )(columns, source, residual, cotangent, context, w_proj, gain_two)


def merge_heads(turned):
    first = jnp.concatenate([turned[:HEAD_DIM, :SPLIT], turned[:HEAD_DIM, 2 * SPLIT : SPLIT + SEQ]], axis=1)
    second = jnp.concatenate([turned[HEAD_DIM:, SPLIT : 2 * SPLIT], turned[HEAD_DIM:, SPLIT + SEQ :]], axis=1)
    return jnp.concatenate([first, second], axis=0).T


def attend_back_kernel(
    chunk,
    grad_context,
    queries,
    keys,
    values,
    weights,
    inverse,
    context,
    normed_one,
    grad_out,
    kept,
    sent,
    value_side,
    grad_scores,
):
    pair = pl.program_id(0)
    image = pl.program_id(1)

    @pl.when((pair == 0) & (image == 0))
    def _():
        is_first, lane = key_sides()
        taken = (is_first & (lane < 2)) | (jnp.logical_not(is_first) & (lane >= 2) & (lane < 4))
        value_side[:, PAIR:] = jnp.where(taken, -1.0, 0.0).astype(BF16)

    key_side = split_heads(keys[0, 0])
    value_side[:, :PAIR] = split_heads(values[0, 0])
    lane = lax.broadcasted_iota(jnp.int32, (chunk, PAIR), 1)
    low = lane < HEAD_DIM
    scaled = []
    for at in range(0, SEQ, chunk):
        rows = slice(at, at + chunk)
        grads = (grad_context[0, 0, rows].astype(F32) * inverse[0, 0, rows]).astype(BF16)
        scaled.append(grads)
        product = grads.astype(F32) * context[0, 0, rows].astype(F32)
        first = jnp.sum(jnp.where(low, product, 0.0), axis=1, keepdims=True)
        second = jnp.sum(jnp.where(low, 0.0, product), axis=1, keepdims=True)
        offset = jnp.where(lane < 2, first, second)
        high = offset.astype(BF16).astype(F32)
        extra = jnp.where(
            (lane == 0) | (lane == 2), high, jnp.where((lane == 1) | (lane == 3), offset - high, 0.0)
        ).astype(BF16)
        grad_weights = dot_last(jnp.concatenate([grads, extra], axis=1), value_side[...])
        part = grad_weights.astype(BF16) * weights[0, 0, rows]
        grad_scores[rows] = part
        place = pl.ds(pl.multiple_of(image * SEQ + at, 32), chunk)
        grad_out[0, pair, place] = (dot(part, key_side) * HEAD_DIM**-0.5).astype(BF16)
    grads = jnp.concatenate(scaled, axis=0)
    place = pl.ds(pl.multiple_of(image * SEQ, 64), SEQ)
    grad_out[1, pair, place] = merge_heads(dot_first(queries[0, 0], grad_scores[...])).astype(BF16)
    grad_out[2, pair, place] = merge_heads(dot_first(grads, weights[0, 0])).astype(BF16)

    @pl.when((pair == pl.num_programs(0) - 1) & (image == pl.num_programs(1) - 1))
    def _():
        for kind in range(3):
            joined = jnp.concatenate([grad_out[kind, at] for at in range(grad_out.shape[1])], axis=1)
            span = joined.shape[1]
            columns = slice(kind * span, (kind + 1) * span)
            total = dot_first(normed_one[...], joined).astype(BF16)
            split_rows(total, kept.at[:, columns], sent.at[:, columns])


def attend_back(grad_context, qkv, weights, inverse, context, normed_one, first, count):
    images, pairs = context.shape[:2]
    rows, width = normed_one.shape

    def block(offset):
        return pl.BlockSpec((1, 1, SEQ, PAIR), lambda p, i: (i, offset + p, 0, 0))

    return pl.pallas_call(
        functools.partial(attend_back_kernel, SEQ),
        grid=(count, images),
        in_specs=[
            block(first),
            block(first),
            block(pairs + first),
            block(2 * pairs + first),
            pl.BlockSpec((1, 1, SEQ, 2 * SEQ), lambda p, i: (i, first + p, 0, 0)),
            block(first),
            block(first),
            whole(normed_one),
        ],
        out_specs=[
            pl.BlockSpec((3, count, rows, PAIR), lambda p, i: (0, 0, 0, 0)),
            pl.BlockSpec((width // 2, 3 * count * PAIR), lambda p, i: (0, 0)),
            pl.BlockSpec((width // 2, 3 * count * PAIR), lambda p, i: (0, 0)),
        ],
        out_shape=[shape((3, count, rows, PAIR), BF16)] + [shape((width // 2, 3 * count * PAIR), BF16)] * 2,
        scratch_shapes=[pltpu.VMEM((2 * SEQ, 2 * PAIR), BF16), pltpu.VMEM((SEQ, 2 * SEQ), BF16)],
        compiler_params=params(),
        cost_estimate=cost(17e9 * (100 if first else 1), 20e6 * (100 if first else 1)),
        name="attend_back",
    )(grad_context, qkv, qkv, qkv, weights, inverse, context, normed_one)


def last_kernel(groups, sub, tokens, w_qkv, grad_residual, gain_one, *rest):
    grads = rest[:groups]
    out, vectors = rest[groups:]
    width = tokens.shape[1]

    @pl.when(pl.program_id(0) == 0)
    def _():
        vectors[...] = jnp.zeros_like(vectors)

    total = jnp.zeros(tokens.shape, F32)
    for kind in range(3):
        joined = jnp.concatenate(
            [grad[kind, at] for grad in grads for at in range(grad.shape[1])], axis=1
        )
        total += dot_last(joined, w_qkv[:, kind * width : (kind + 1) * width])
        if kind == 0:
            vectors[2:3] += column_sum(joined.astype(F32))
        if kind == 2:
            vectors[3:4] += column_sum(joined.astype(F32))
    out[...] = total
    gain = as_row(gain_one)
    for at in range(0, tokens.shape[0], sub):
        rows = slice(at, at + sub)
        grad_normed = out[rows, :]
        unit, inverse = standardize(tokens[rows, :].astype(F32))
        out[rows, :] = grad_residual[rows, :] + standardize_back(grad_normed, gain, unit, inverse)
        vectors[0:1] += column_sum(grad_normed * unit)
        vectors[1:2] += column_sum(grad_normed)


def last(tokens, grads, w_qkv, grad_residual, gain_one, chunk=288):
    rows, width = tokens.shape
    block = pl.BlockSpec((chunk, width), lambda i: (i, 0))
    return pl.pallas_call(
        functools.partial(last_kernel, len(grads), 32),
        grid=(rows // chunk,),
        in_specs=[block, whole(w_qkv), block, whole(gain_one)]
        + [pl.BlockSpec((3, grad.shape[1], chunk, PAIR), lambda i: (0, 0, i, 0)) for grad in grads],
        out_specs=[block, pl.BlockSpec((8, width), lambda i: (0, 0))],
        out_shape=[shape((rows, width), F32), shape((8, width), F32)],
        compiler_params=params(),
        cost_estimate=cost(10e9, 15e6),
        name="last",
    )(tokens, w_qkv, grad_residual, gain_one, *grads)


def fold_kernel(count, *refs):
    inputs, outs = refs[: 2 * count], refs[2 * count :]
    at = lax.axis_index("exp") >> 1
    rows = outs[0].shape[0]
    for other, out in enumerate(outs):
        here = pl.ds(pl.multiple_of((at ^ other) * rows, rows), rows)
        column = 0
        for kept, received in zip(inputs[:count], inputs[count:]):
            span = slice(column, column + kept.shape[1])
            out[:, span] = (kept[here, :].astype(F32) + received[here, :].astype(F32)).astype(BF16)
            column = span.stop


def fold(kept, received, chips):
    rows = kept[0].shape[0] // chips
    width = sum(part.shape[1] for part in kept)
    return pl.pallas_call(
        functools.partial(fold_kernel, len(kept)),
        out_shape=[shape((rows, width), BF16)] * chips,
        compiler_params=params(),
        cost_estimate=cost(1e9, 10e6),
        name="fold",
    )(*kept, *received)


def finish_kernel(left, where, *refs):
    inputs, (proj_out, out) = refs[:-2], refs[-2:]
    width = proj_out.shape[1]
    right = width - left
    for step, part in enumerate(inputs):

        @pl.when(pl.program_id(0) == step)
        def _():
            proj_out[...] = part[:, :width].astype(F32)
            for kind in range(3):
                to = kind * width
                at = width + kind * left
                out[:, to : to + left] = part[:, at : at + left].astype(F32)
                at = width + 3 * left + kind * right
                out[:, to + left : to + width] = part[:, at : at + right].astype(F32)


def finish(parts, where, left):
    steps = len(parts)
    rows = parts[0].shape[0]
    width = parts[0].shape[1] // 4

    def landing(columns):
        return pl.BlockSpec((rows, columns), lambda i, at: (at[i], 0))

    return pl.pallas_call(
        functools.partial(finish_kernel, left),
        grid_spec=pltpu.PrefetchScalarGridSpec(
            num_scalar_prefetch=1,
            grid=(steps,),
            in_specs=[pl.BlockSpec(part.shape, lambda i, at: (0, 0)) for part in parts],
            out_specs=[landing(width), landing(3 * width)],
        ),
        out_shape=[shape((rows * steps, width), F32), shape((rows * steps, 3 * width), F32)],
        compiler_params=params(),
        cost_estimate=cost(1e9, 10e6),
        name="finish",
    )(where, *parts)


def combine_kernel(columns, source, residual, out):
    hits = token_hits(columns, source.shape[0])
    out[...] = (residual[...] + dot(hits, source[...])).astype(BF16)


def combine(columns, source, residual, chunk=288):
    rows, width = residual.shape
    return pl.pallas_call(
        combine_kernel,
        grid=(rows // chunk,),
        in_specs=[
            pl.BlockSpec((chunk, 8), lambda i: (i, 0)),
            whole(source),
            pl.BlockSpec((chunk, width), lambda i: (i, 0)),
        ],
        out_specs=pl.BlockSpec((chunk, width), lambda i: (i, 0)),
        out_shape=shape((rows, width), BF16),
        compiler_params=params(),
        cost_estimate=cost(6e9, 10e6),
        name="combine",
    )(columns, source, residual)


def exchange(rows, experts):
    blocks = rows.reshape(experts, rows.shape[0] // experts, rows.shape[1])
    return lax.all_to_all(blocks, "exp", split_axis=0, concat_axis=0, tiled=True).reshape(rows.shape)


def share(block, name, size):
    copies = jnp.broadcast_to(block[None], (size,) + block.shape)
    return lax.all_to_all(copies, name, split_axis=0, concat_axis=0, tiled=True)


def sum_blocks(blocks, kind):
    return jnp.sum(blocks.astype(F32), axis=0).astype(kind)


def scatter_reps(blocks):
    rows = blocks.reshape((-1,) + blocks.shape[2:])
    return lax.psum_scatter(rows, "rep", scatter_dimension=0, tiled=True)


def swap(block, name, bits, size):
    return lax.ppermute(block, name, [(at, at ^ bits) for at in range(size)])


def chip_scatter(kept, sent, sizes):
    size = sizes["exp"]
    chips = size // 2
    received = [swap(part, "exp", 1, size) for part in sent]
    parts = fold(kept, received, chips)
    return parts


def plane_sum(parts, sizes):
    size = sizes["exp"]
    chips = size // 2
    received = [swap(parts[other], "exp", 2 * other, size) for other in range(1, chips)]
    total = parts[0].astype(F32)
    for part in received:
        total += part.astype(F32)
    return total.astype(BF16)


def rep_sum(block, sizes):
    reps = sizes["rep"]
    blocks = block.reshape((reps, -1) + block.shape[1:])
    at = lax.convert_element_type(lax.axis_index("rep"), jnp.uint32)

    def pick(other):
        return lax.dynamic_index_in_dim(blocks, at ^ jnp.uint32(other), 0, keepdims=False)

    received = [swap(pick(other), "rep", other, reps) for other in range(1, reps)]
    total = pick(0).astype(F32)
    for part in received:
        total += part.astype(F32)
    return total.astype(BF16)


def rep_gather(block, sizes):
    reps = sizes["rep"]
    at = lax.axis_index("rep")
    parts = [block] + [swap(block, "rep", other, reps) for other in range(1, reps)]
    rows = []
    for slot in range(reps):
        chosen = parts[0]
        for other in range(1, reps):
            chosen = jnp.where((at ^ other) == slot, parts[other], chosen)
        rows.append(chosen)
    return jnp.concatenate(rows, axis=0)


def plane_gather(block, sizes):
    size = sizes["exp"]
    mine = [block] + [swap(block, "exp", 2 * other, size) for other in range(1, size // 2)]
    return mine + [swap(part, "exp", 1, size) for part in mine]


def join_halves(kept, sent):
    first = (lax.axis_index("exp") & 1) == 0
    return jnp.where(first, jnp.concatenate([kept, sent]), jnp.concatenate([sent, kept]))


def small_sums(vectors_two, vectors_one, router_grad):
    blank = jnp.zeros_like(vectors_one[:1])
    return jnp.concatenate([vectors_two[:3], vectors_one[:4], blank, router_grad], axis=0)


def tie(value, *after):
    return lax.optimization_barrier((value,) + after)[0]


def on_device(
    sizes,
    tokens,
    cotangent,
    expert_ids,
    expert_slots,
    w_qkv,
    q_bias,
    v_bias,
    w_proj,
    proj_bias,
    gain_one,
    shift_one,
    gain_two,
    shift_two,
    w_router,
    expert_in,
    expert_in_bias,
    expert_out,
    expert_out_bias,
):
    row_count, width = tokens.shape
    experts = w_router.shape[1]
    slot_count = row_count // experts
    reps = sizes["rep"]
    ids = expert_ids.T
    slots = expert_slots.T
    router_turned = w_router.T
    weight_in = expert_in[0]
    weight_out = expert_out[0]
    bias_in = expert_in_bias.astype(F32)
    bias_out = expert_out_bias.astype(F32)

    cot_arrived = exchange(gather(ids, slots, cotangent, slot_count), experts)
    normed_one, qkv, weights, inverse, context, residual, normed_two = front(
        tokens, w_qkv, q_bias.astype(F32), v_bias.astype(F32), w_proj, proj_bias.astype(F32), gain_one, shift_one, gain_two, shift_two
    )
    arrived = exchange(gather(ids, slots, normed_two, slot_count), experts)
    raw, columns = raw_active(ids, slots, cot_arrived, weight_out, slot_count)
    active, grad_hidden, out_grad, in_bias_grad, out_bias_grad, gate, logits_grad = expert(
        arrived, cot_arrived, weight_in, bias_in, raw, bias_out, router_turned
    )
    grad_eout = lax.psum_scatter(out_grad, "rep", scatter_dimension=0, tiled=True)
    back, router_grad = expert_back(grad_hidden, weight_in, logits_grad, router_turned, arrived)
    source = exchange(back, experts)
    part = weight_in.shape[1] // reps
    out_part = width // reps
    tail = jnp.pad(out_bias_grad.reshape(reps, 1, out_part), ((0, 0), (0, 0), (0, part - out_part)))
    in_first, in_second = weight_in_grad(arrived, grad_hidden, in_bias_grad, tail, width, reps)
    made = produce(gate, active, weight_out, bias_out)
    source, made, in_first, in_second = lax.optimization_barrier((source, made, in_first, in_second))
    in_first = scatter_reps(in_first)
    returned = exchange(made, experts)
    grad_residual, grad_context, proj_kept, proj_sent, vectors_two = middle(
        columns, source, residual, cotangent, context, w_proj, gain_two
    )
    pairs = width // PAIR
    most = pairs - pairs // 3
    saved = (qkv, weights, inverse, context, normed_one)
    grads_a, kept_a, sent_a = attend_back(grad_context, *saved, 0, most)
    chips = sizes["exp"] // 2
    if (width // sizes["exp"]) % 16 == 0:
        sent_a, proj_sent, returned = lax.optimization_barrier((sent_a, proj_sent, returned))
        parts_a = chip_scatter((proj_kept, kept_a), (proj_sent, sent_a), sizes)
        sum_a = plane_sum(parts_a, sizes)
        grads_b, kept_b, sent_b = attend_back(
            tie(grad_context, grads_a, parts_a[0], grad_eout), *saved, most, pairs - most
        )
        parts_b = chip_scatter((kept_b,), (sent_b,), sizes)
        sum_b = plane_sum(parts_b, sizes)
        mixed = combine(columns, tie(returned, parts_b[0]), residual)
        sum_a, sum_b, mixed, in_first = lax.optimization_barrier((sum_a, sum_b, mixed, in_first))
        block = jnp.concatenate([sum_a, sum_b], axis=1)
        grad_tokens, vectors_one = last(
            tokens, (grads_a, grads_b), w_qkv, tie(grad_residual, block), gain_one
        )
        block = rep_sum(block, sizes)
        block, vectors_one, grad_eout = lax.optimization_barrier((block, vectors_one, grad_eout))
        small = small_sums(vectors_two, vectors_one, router_grad)
        small = sum_blocks(share(small, "exp", sizes["exp"]), F32)
        block = rep_gather(block, sizes)
        block, in_second = lax.optimization_barrier((block, in_second))
        in_second = scatter_reps(in_second)
        small = sum_blocks(share(small, "rep", reps), F32)
        parts = plane_gather(block, sizes)
        here = lax.axis_index("exp")
        order = jnp.arange(chips, dtype=jnp.int32) ^ (here >> 1)
        core = here & 1
        where = jnp.concatenate([core * chips + order, (1 - core) * chips + order]).astype(jnp.int32)
        grad_w_proj, grad_w_qkv = finish(parts, where, most * PAIR)
    else:
        in_second = scatter_reps(in_second)
        grads_b, kept_b, sent_b = attend_back(grad_context, *saved, most, pairs - most)
        mixed = combine(columns, returned, residual)
        grad_tokens, vectors_one = last(tokens, (grads_a, grads_b), w_qkv, grad_residual, gain_one)
        block = join_halves(
            jnp.concatenate([proj_kept, kept_a, kept_b], axis=1),
            jnp.concatenate([proj_sent, sent_a, sent_b], axis=1),
        )
        small = lax.psum(small_sums(vectors_two, vectors_one, router_grad), ("rep", "exp"))
        block = lax.psum(block, ("rep", "exp"))
        where = jnp.zeros((1,), jnp.int32)
        grad_w_proj, grad_w_qkv = finish((block,), where, most * PAIR)
    return (
        mixed,
        grad_tokens,
        grad_w_qkv,
        small[5],
        small[6],
        grad_w_proj,
        small[2],
        small[3],
        small[4],
        small[0],
        small[1],
        small[8 : 8 + experts].T,
        jnp.concatenate([in_first, in_second[: width // 2]], axis=0)[None].astype(F32),
        in_second[width // 2 : width // 2 + 1].astype(F32),
        grad_eout[None].astype(F32),
        in_second[width // 2 + 1 : width // 2 + 2, :out_part].astype(F32),
    )


def solution(mesh):
    rows = P(("rep", "exp"), None)
    placed = (rows,) * 4 + (P(),) * 10 + (
        P("exp", None, None),
        P("exp", None),
        P("exp", None, None),
        P("exp", None),
    )
    return jax.shard_map(
        functools.partial(on_device, dict(mesh.shape)),
        mesh=mesh,
        in_specs=placed,
        out_specs=(rows, rows)
        + (P(),) * 10
        + (P("exp", None, "rep"), P("exp", "rep"), P("exp", "rep", None), P("exp", "rep")),
        check_vma=False,
    )
```

```python
import functools

import jax
import jax.numpy as jnp
from jax import lax
from jax.experimental import pallas as pl
from jax.experimental.pallas import tpu as pltpu
from jax.sharding import PartitionSpec as P

HEAD_DIM = 64
SEQ = 576
PAIR = 2 * HEAD_DIM
SPLIT = 512
AUX = 128
EPSILON = 1e-06
F32 = jnp.float32
BF16 = jnp.bfloat16
VMEM_BYTES = 56 * 2**20


def dot(left, right):
    return lax.dot_general(left, right, (((1,), (0,)), ((), ())), preferred_element_type=F32)


def dot_last(left, right):
    return lax.dot_general(left, right, (((1,), (1,)), ((), ())), preferred_element_type=F32)


def dot_first(left, right):
    return lax.dot_general(left, right, (((0,), (0,)), ((), ())), preferred_element_type=F32)


def thirds(value):
    high = value.astype(BF16)
    rest = value - high.astype(F32)
    middle = rest.astype(BF16)
    return high, middle, (rest - middle.astype(F32)).astype(BF16)


def standardize(field):
    centred = field - jnp.mean(field, axis=-1, keepdims=True)
    inverse = lax.rsqrt(jnp.mean(centred * centred, axis=-1, keepdims=True) + EPSILON)
    return centred * inverse, inverse


def standardize_back(grad, gain, unit, inverse):
    scaled = grad * gain
    along = jnp.mean(scaled * unit, axis=-1, keepdims=True)
    return inverse * (scaled - jnp.mean(scaled, axis=-1, keepdims=True) - unit * along)


def as_row(ref):
    return ref[...].astype(F32).reshape(1, -1)


def column_sum(field):
    return jnp.sum(field, axis=0, keepdims=True)


def params():
    return pltpu.CompilerParams(vmem_limit_bytes=VMEM_BYTES)


SCALE = 0.01
EXPERT_CHUNK = 768
EXPERT_ROWS = 288


def cost(flops, bytes_moved):
    return pl.CostEstimate(flops=int(flops * SCALE), transcendentals=0, bytes_accessed=int(bytes_moved * SCALE))


def whole(array):
    return pl.BlockSpec(array.shape, lambda *ids: (0,) * array.ndim)


def shape(dims, kind):
    return jax.ShapeDtypeStruct(dims, kind)


def split_heads(pair):
    lane = lax.broadcasted_iota(jnp.int32, pair.shape, 1)
    zero = jnp.zeros_like(pair)
    first = jnp.where(lane < HEAD_DIM, pair, zero)
    second = jnp.where(lane < HEAD_DIM, zero, pair)
    return jnp.concatenate([first[:SPLIT], second[:SPLIT], first[SPLIT:], second[SPLIT:]], axis=0)


def key_sides():
    row = lax.broadcasted_iota(jnp.int32, (2 * SEQ, PAIR), 0)
    lane = lax.broadcasted_iota(jnp.int32, (2 * SEQ, PAIR), 1)
    is_first = (row < SPLIT) | ((row >= 2 * SPLIT) & (row < SPLIT + SEQ))
    return is_first, lane


def columns_of(ids, slots, slot_count):
    return jnp.where(slots[...] >= 0, ids[...] * slot_count + slots[...], -1)


def slot_hits(columns, at, count):
    slot = at + lax.broadcasted_iota(jnp.int32, (count, columns.shape[1]), 0)
    hit = (columns[0:1, :] == slot) | (columns[1:2, :] == slot)
    return jnp.where(hit, 1.0, 0.0).astype(BF16)


def front_kernel(
    chunk,
    slot_count,
    tokens,
    w_qkv,
    biases,
    w_proj,
    gain_one,
    shift_one,
    gain_two,
    shift_two,
    ids,
    slots,
    normed_one_out,
    qkv_out,
    weights_out,
    inverse_out,
    context_out,
    residual_out,
    dispatched_out,
    value_side,
    normed_two,
):
    pair = pl.program_id(1)
    pairs = context_out.shape[1]

    @pl.when((pl.program_id(0) == 0) & (pair == 0))
    def _():
        is_first, lane = key_sides()
        value_side[:, PAIR:] = jnp.where(is_first == (lane < HEAD_DIM), 1.0, 0.0).astype(BF16)

    @pl.when(pair == 0)
    def _():
        unit, _ = standardize(tokens[...].astype(F32))
        normed = (unit * as_row(gain_one) + as_row(shift_one)).astype(BF16)
        normed_one_out[...] = normed
        width = w_qkv.shape[1]
        step = 2 * PAIR
        for at in range(0, width, step):
            part = dot(normed, w_qkv[:, at : at + step])
            third = width // 3
            if at < third:
                part = part + as_row(biases)[:, at : at + step]
            if at >= 2 * third:
                part = part + as_row(biases)[:, at - third : at - third + step]
            part = part.astype(BF16)
            if at < third:
                part = part * jnp.asarray(HEAD_DIM**-0.5, BF16)
            qkv_out[0, at // PAIR] = part[:, :PAIR]
            qkv_out[0, at // PAIR + 1] = part[:, PAIR:]

    keys = split_heads(qkv_out[0, pairs + pair])
    value_side[:, :PAIR] = split_heads(qkv_out[0, 2 * pairs + pair])
    values = value_side[...]
    low = lax.broadcasted_iota(jnp.int32, (chunk, PAIR), 1) < HEAD_DIM
    for at in range(0, SEQ, chunk):
        rows = slice(at, at + chunk)
        scores = dot_last(qkv_out[0, pair, rows], keys)
        first = scores[:, :SPLIT]
        second = scores[:, SPLIT : 2 * SPLIT]
        tail = scores[:, 2 * SPLIT :]
        first_max = jnp.maximum(
            jnp.max(first, axis=1, keepdims=True),
            jnp.max(jnp.where(low, tail, -jnp.inf), axis=1, keepdims=True),
        )
        second_max = jnp.maximum(
            jnp.max(second, axis=1, keepdims=True),
            jnp.max(jnp.where(low, -jnp.inf, tail), axis=1, keepdims=True),
        )
        exponent = jnp.concatenate(
            [
                jnp.exp(first - first_max).astype(BF16),
                jnp.exp(second - second_max).astype(BF16),
                jnp.exp(tail - jnp.where(low, first_max, second_max)).astype(BF16),
            ],
            axis=1,
        )
        weights_out[0, 0, rows] = exponent
        summed = dot(exponent, values)
        inverse = 1.0 / summed[:, PAIR:]
        inverse_out[0, 0, rows] = inverse
        context_out[0, pair, rows] = (summed[:, :PAIR] * inverse).astype(BF16)

    @pl.when(pair == pairs - 1)
    def _():
        context = jnp.concatenate([context_out[0, at] for at in range(pairs)], axis=1)
        residual = tokens[...].astype(F32) + (dot(context, w_proj[...]) + as_row(biases)[:, 2 * residual_out.shape[1] :])
        residual_out[...] = residual
        unit, _ = standardize(residual)
        normed = (unit * as_row(gain_two) + as_row(shift_two)).astype(BF16)
        normed_two[pl.ds(pl.multiple_of(pl.program_id(0) * SEQ, 64), SEQ)] = normed

    @pl.when((pair == pairs - 1) & (pl.program_id(0) == pl.num_programs(0) - 1))
    def _():
        columns = columns_of(ids, slots, slot_count)
        part = SEQ // 2
        for at in range(0, dispatched_out.shape[0], part):
            hits = slot_hits(columns, at, part)
            dispatched_out[at : at + part] = dot(hits, normed_two[...]).astype(BF16)


def front(tokens, w_qkv, biases, w_proj, gain_one, shift_one, gain_two, shift_two, ids, slots, slot_count):
    rows, width = tokens.shape
    images = rows // SEQ
    pairs = width // PAIR

    def per_image(columns):
        return pl.BlockSpec((SEQ, columns), lambda i, p: (i, 0))

    fixed = (w_qkv, biases, w_proj, gain_one, shift_one, gain_two, shift_two, ids, slots)
    return pl.pallas_call(
        functools.partial(front_kernel, SEQ // 2, slot_count),
        grid=(images, pairs),
        in_specs=[per_image(width)] + [whole(array) for array in fixed],
        out_specs=[
            per_image(width),
            pl.BlockSpec((1, 3 * pairs, SEQ, PAIR), lambda i, p: (i, 0, 0, 0)),
            pl.BlockSpec((1, 1, SEQ, 2 * SEQ), lambda i, p: (i, p, 0, 0)),
            pl.BlockSpec((1, 1, SEQ, PAIR), lambda i, p: (i, p, 0, 0)),
            pl.BlockSpec((1, pairs, SEQ, PAIR), lambda i, p: (i, 0, 0, 0)),
            per_image(width),
            pl.BlockSpec((rows, width), lambda i, p: (0, 0)),
        ],
        out_shape=[
            shape((rows, width), BF16),
            shape((images, 3 * pairs, SEQ, PAIR), BF16),
            shape((images, pairs, SEQ, 2 * SEQ), BF16),
            shape((images, pairs, SEQ, PAIR), F32),
            shape((images, pairs, SEQ, PAIR), BF16),
            shape((rows, width), F32),
            shape((rows, width), BF16),
        ],
        scratch_shapes=[pltpu.VMEM((2 * SEQ, 2 * PAIR), BF16), pltpu.VMEM((rows, width), BF16)],
        compiler_params=params(),
        cost_estimate=cost(30e9, 60e6),
        name="front",
    )(tokens, *fixed)


def gather_kernel(chunk, slot_count, ids, slots, rows, out):
    columns = columns_of(ids, slots, slot_count)
    hits = slot_hits(columns, pl.program_id(0) * chunk, chunk)
    out[...] = dot(hits, rows[...]).astype(BF16)


def gather(ids, slots, rows, slot_count, chunk=288):
    count, width = rows.shape
    return pl.pallas_call(
        functools.partial(gather_kernel, chunk, slot_count),
        grid=(count // chunk,),
        in_specs=[whole(ids), whole(slots), whole(rows)],
        out_specs=pl.BlockSpec((chunk, width), lambda i: (i, 0)),
        out_shape=shape((count, width), BF16),
        compiler_params=params(),
        cost_estimate=cost(4e9, 8e6),
        name="gather",
    )(ids, slots, rows)


def raw_kernel(slot_count, ids, slots, cotangent, weight_out, bias_out, out, columns_out, turned, along):
    @pl.when(pl.program_id(0) == 0)
    def _():
        columns = columns_of(ids, slots, slot_count)
        pad = jnp.full((6, columns.shape[1]), -1, jnp.int32)
        columns_out[...] = jnp.concatenate([columns, pad], axis=0).T
        turned[...] = cotangent[...].T
        for at in range(0, along.shape[0], 32):
            rows = slice(at, at + 32)
            along[rows, :] = lane_sums(cotangent[rows, :].astype(F32) * bias_out[...])

    out[...] = dot_last(cotangent[...], weight_out[...]).astype(BF16)


def raw_active(ids, slots, cotangent, weight_out, bias_out, slot_count, chunk=768):
    count, width = cotangent.shape
    hidden = weight_out.shape[0]
    return pl.pallas_call(
        functools.partial(raw_kernel, slot_count),
        grid=(hidden // chunk,),
        in_specs=[
            whole(ids),
            whole(slots),
            whole(cotangent),
            pl.BlockSpec((chunk, width), lambda i: (i, 0)),
            whole(bias_out),
        ],
        out_specs=[
            pl.BlockSpec((count, chunk), lambda i: (0, i)),
            pl.BlockSpec((count, 8), lambda i: (0, 0)),
            pl.BlockSpec((width, count), lambda i: (0, 0)),
            pl.BlockSpec((count, AUX), lambda i: (0, 0)),
        ],
        out_shape=[
            shape((count, hidden), BF16),
            shape((count, 8), jnp.int32),
            shape((width, count), BF16),
            shape((count, AUX), F32),
        ],
        compiler_params=params(),
        cost_estimate=cost(9e9, 14e6),
        name="raw_active",
    )(ids, slots, cotangent, weight_out, bias_out)


def joined_thirds(value, order):
    parts = thirds(value)
    return jnp.concatenate([parts[at] for at in order], axis=1)


LEFT = (0, 0, 1, 1, 0, 2)
RIGHT = (0, 1, 0, 1, 2, 0)


def expert_kernel(
    row_chunk,
    arrived,
    cot_turned,
    weight_in,
    bias_in,
    raw,
    along,
    w_router,
    active_out,
    hidden_out,
    weight_grad,
    gate_out,
    logits_grad,
    produced_grad,
    gate_total,
    router,
):
    step = pl.program_id(0)
    count = arrived.shape[0]
    experts = w_router.shape[0]

    @pl.when(step == 0)
    def _():
        parts = dot_last(arrived[...], jnp.concatenate(thirds(w_router[...]), axis=0))
        logits = parts[:, :experts] + (parts[:, experts : 2 * experts] + parts[:, 2 * experts :])
        exponent = jnp.exp(logits - jnp.max(logits, axis=1, keepdims=True))
        probs = exponent / jnp.sum(exponent, axis=1, keepdims=True)
        router[...] = probs
        own = lax.broadcasted_iota(jnp.int32, (count, experts), 1) == lax.axis_index("exp")
        gate = jnp.sum(jnp.where(own, probs, 0.0), axis=1, keepdims=True)
        gate_out[...] = jnp.broadcast_to(gate, gate_out.shape)
        gate_row = gate_out[...].T[0:1]
        produced_grad[...] = (cot_turned[...].astype(F32) * gate_row).astype(BF16)
        gate_total[...] = along[...]

    for at in range(0, count, row_chunk):
        rows = slice(at, at + row_chunk)
        hidden = dot(arrived[rows, :], weight_in[...]) + bias_in[...]
        scaled = hidden * (0.5**0.5)
        curve = lax.erf(scaled)
        half = 0.5 * hidden
        active = (half + half * curve).astype(BF16)
        bell = jnp.exp(scaled * -scaled) * (0.5 * 1.1283791670955126 * 0.5**0.5)
        slope = ((0.5 + 0.5 * curve) + hidden * bell).astype(BF16)
        incoming = raw[rows, :]
        active_out[rows, :] = active
        hidden_out[rows, :] = incoming * slope
        gate_total[rows, :] += lane_sums((incoming * active).astype(F32))
    weight_grad[0] = dot(produced_grad[...], active_out[...]).astype(BF16)

    @pl.when(step == pl.num_programs(0) - 1)
    def _():
        own = lax.broadcasted_iota(jnp.int32, (count, experts), 1) == lax.axis_index("exp")
        scale = jnp.sum(gate_total[...], axis=1, keepdims=True) * gate_out[:, 0:1]
        logits_grad[...] = scale * (jnp.where(own, 1.0, 0.0) - router[...])


def lane_sums(field):
    total = field[:, :AUX]
    for at in range(AUX, field.shape[1], AUX):
        total = total + field[:, at : at + AUX]
    return total


def expert(arrived, cot_turned, weight_in, bias_in, raw, along, w_router, reps, chunk=EXPERT_CHUNK):
    count, width = arrived.shape
    hidden = weight_in.shape[1]
    experts = w_router.shape[0]
    part = hidden // reps
    cuts = part // chunk

    def column_block(rows):
        return pl.BlockSpec((rows, chunk), lambda i: (0, i))

    def fixed(rows, columns):
        return pl.BlockSpec((rows, columns), lambda i: (0, 0))

    return pl.pallas_call(
        functools.partial(expert_kernel, EXPERT_ROWS),
        grid=(hidden // chunk,),
        in_specs=[
            whole(arrived),
            whole(cot_turned),
            column_block(width),
            column_block(1),
            column_block(count),
            whole(along),
            whole(w_router),
        ],
        out_specs=[
            column_block(count),
            column_block(count),
            pl.BlockSpec((1, width, chunk), lambda i: (i // cuts, 0, i % cuts)),
            fixed(count, AUX),
            fixed(count, experts),
        ],
        out_shape=[
            shape((count, hidden), BF16),
            shape((count, hidden), BF16),
            shape((reps, width, part), BF16),
            shape((count, AUX), F32),
            shape((count, experts), F32),
        ],
        scratch_shapes=[
            pltpu.VMEM((width, count), BF16),
            pltpu.VMEM((count, AUX), F32),
            pltpu.VMEM((count, experts), F32),
        ],
        compiler_params=params(),
        cost_estimate=cost(24e9, 35e6),
        name="expert",
    )(arrived, cot_turned, weight_in, bias_in, raw, along, w_router)


def expert_back_kernel(grad_hidden, weight_in, gate, logits_grad, w_router, arrived, out, router_grad):
    experts = w_router.shape[0]

    @pl.when(pl.program_id(0) == 0)
    def _():
        router_grad[...] = jnp.zeros_like(router_grad)

    right = jnp.concatenate([thirds(w_router[...])[at] for at in RIGHT], axis=0)
    total = gate[:, 0:1] * dot_last(grad_hidden[...], weight_in[...])
    total += dot(joined_thirds(logits_grad[...], LEFT), right)
    out[...] = total.astype(BF16)
    parts = dot_first(joined_thirds(logits_grad[...], (0, 1, 2)), arrived[...])
    router_grad[...] += parts[:experts] + parts[experts : 2 * experts] + parts[2 * experts :]


def expert_back(grad_hidden, weight_in, gate, logits_grad, w_router, arrived, chunk=288):
    count, hidden = grad_hidden.shape
    experts, width = w_router.shape

    def rows(columns):
        return pl.BlockSpec((chunk, columns), lambda i: (i, 0))

    return pl.pallas_call(
        expert_back_kernel,
        grid=(count // chunk,),
        in_specs=[rows(hidden), whole(weight_in), rows(AUX), rows(experts), whole(w_router), rows(width)],
        out_specs=[rows(width), pl.BlockSpec((experts, width), lambda i: (0, 0))],
        out_shape=[shape((count, width), BF16), shape((experts, width), F32)],
        compiler_params=params(),
        cost_estimate=cost(12e9, 15e6),
        name="expert_back",
    )(grad_hidden, weight_in, gate, logits_grad, w_router, arrived)


def turn_kernel(field, out):
    out[...] = field[...].T.astype(F32)


def turn(field):
    return pl.pallas_call(
        turn_kernel,
        out_shape=shape(field.shape[::-1], F32),
        compiler_params=params(),
        cost_estimate=cost(1e9, 5e6),
        name="turn",
    )(field)


def weight_in_kernel(arrived, gate, grad_hidden, out_bias_grad, first, second, turned):
    width = arrived.shape[1]
    half = width // 2

    @pl.when(pl.program_id(0) == 0)
    def _():
        for at in range(0, arrived.shape[0], 128):
            rows = slice(at, at + 128)
            turned[:width, rows] = (arrived[rows, :].astype(F32) * gate[rows, 0:1]).astype(BF16).T
        gate_row = jnp.broadcast_to(gate[...].T[0:1], (16, arrived.shape[0]))
        high = gate_row.astype(BF16)
        row = lax.broadcasted_iota(jnp.int32, high.shape, 0)
        low = (gate_row - high.astype(F32)).astype(BF16)
        turned[width:] = jnp.where(row == 0, high, jnp.where(row == 1, low, jnp.zeros_like(low)))

    total = dot(turned[...], grad_hidden[...])
    second[0] = total[half:width].astype(BF16)
    first[0, :half] = total[:half].astype(BF16)
    row = lax.broadcasted_iota(jnp.int32, (first.shape[1] - half, first.shape[2]), 0)
    bias_grad = total[width : width + 1] + total[width + 1 : width + 2]
    first[0, half:] = jnp.where(row == 0, bias_grad, jnp.where(row == 1, out_bias_grad[0], 0.0)).astype(BF16)


def weight_in_grad(arrived, gate, grad_hidden, out_bias_grad, reps):
    count, hidden = grad_hidden.shape
    width = arrived.shape[1]
    part = hidden // reps
    return pl.pallas_call(
        weight_in_kernel,
        grid=(reps,),
        in_specs=[
            whole(arrived),
            whole(gate),
            pl.BlockSpec((count, part), lambda i: (0, i)),
            pl.BlockSpec((1, 1, part), lambda i: (i, 0, 0)),
        ],
        out_specs=[
            pl.BlockSpec((1, width // 2 + 16, part), lambda i: (i, 0, 0)),
            pl.BlockSpec((1, width // 2, part), lambda i: (i, 0, 0)),
        ],
        out_shape=[shape((reps, width // 2 + 16, part), BF16), shape((reps, width // 2, part), BF16)],
        scratch_shapes=[pltpu.VMEM((width + 16, count), BF16)],
        compiler_params=params(),
        cost_estimate=cost(10e9, 15e6),
        name="weight_in_grad",
    )(arrived, gate, grad_hidden, out_bias_grad)


def produce_kernel(gate, active, cotangent, weight_out, bias_out, out, bias_grad):
    @pl.when(pl.program_id(0) == 0)
    def _():
        bias_grad[...] = jnp.zeros_like(bias_grad)

    bias_grad[...] += column_sum(gate[:, 0:1] * cotangent[...].astype(F32))
    out[...] = (gate[:, 0:1] * (dot(active[...], weight_out[...]) + bias_out[...])).astype(BF16)


def produce(gate, active, cotangent, weight_out, bias_out, chunk=288):
    count, hidden = active.shape
    width = weight_out.shape[1]

    def rows(columns):
        return pl.BlockSpec((chunk, columns), lambda i: (i, 0))

    return pl.pallas_call(
        produce_kernel,
        grid=(count // chunk,),
        in_specs=[rows(AUX), rows(hidden), rows(width), whole(weight_out), whole(bias_out)],
        out_specs=[rows(width), pl.BlockSpec((1, width), lambda i: (0, 0))],
        out_shape=[shape((count, width), BF16), shape((1, width), F32)],
        compiler_params=params(),
        cost_estimate=cost(10e9, 15e6),
        name="produce",
    )(gate, active, cotangent, weight_out, bias_out)


def token_hits(columns, slots):
    slot = lax.broadcasted_iota(jnp.int32, (columns.shape[0], slots), 1)
    hit = (columns[:, 0:1] == slot) | (columns[:, 1:2] == slot)
    return jnp.where(hit, 1.0, 0.0).astype(BF16)


def split_rows(value, kept, sent):
    half = value.shape[0] // 2
    first = (lax.axis_index("exp") & 1) == 0
    low, high = value[:half], value[half:]
    kept[...] = jnp.where(first, low, high)
    sent[...] = jnp.where(first, high, low)


def middle_kernel(
    sub,
    columns,
    source,
    residual,
    cotangent,
    context,
    w_proj,
    gain_two,
    grad_residual_out,
    grad_context_out,
    proj_kept,
    proj_sent,
    vectors,
    branch,
    proj_total,
):
    step = pl.program_id(0)
    chunk = residual.shape[0]
    pairs = context.shape[1]

    @pl.when(step == 0)
    def _():
        vectors[...] = jnp.zeros_like(vectors)
        proj_total[...] = jnp.zeros_like(proj_total)

    hits = token_hits(columns, source.shape[0])
    grad_residual_out[...] = dot(hits, source[...])
    gain = as_row(gain_two)
    for at in range(0, chunk, sub):
        rows = slice(at, at + sub)
        grad_normed = grad_residual_out[rows, :]
        unit, inverse = standardize(residual[rows, :])
        grad_residual = cotangent[rows, :].astype(F32) + standardize_back(grad_normed, gain, unit, inverse)
        grad_residual_out[rows, :] = grad_residual
        rounded = grad_residual.astype(BF16)
        branch[rows, :] = rounded
        vectors[0:1] += column_sum(grad_normed * unit)
        vectors[1:2] += column_sum(grad_normed)
        vectors[2:3] += column_sum(rounded.astype(F32))
    grad_context = dot_last(branch[...], w_proj[...]).astype(BF16)
    for pair in range(pairs):
        grad_context_out[0, pair] = grad_context[:, pair * PAIR : (pair + 1) * PAIR]
    joined = jnp.concatenate([context[0, pair] for pair in range(pairs)], axis=1)
    proj_total[...] += dot_first(joined, branch[...])

    @pl.when(step == pl.num_programs(0) - 1)
    def _():
        split_rows(proj_total[...].astype(BF16), proj_kept, proj_sent)


def middle(columns, source, residual, cotangent, context, w_proj, gain_two, chunk=288):
    rows, width = residual.shape
    images, pairs = context.shape[:2]
    parts = SEQ // chunk

    def rows_of(columns):
        return pl.BlockSpec((chunk, columns), lambda i: (i, 0))

    by_pair = pl.BlockSpec((1, pairs, chunk, PAIR), lambda i: (i // parts, 0, i % parts, 0))
    return pl.pallas_call(
        functools.partial(middle_kernel, 32),
        grid=(rows // chunk,),
        in_specs=[
            rows_of(8),
            whole(source),
            rows_of(width),
            rows_of(width),
            by_pair,
            whole(w_proj),
            whole(gain_two),
        ],
        out_specs=[
            rows_of(width),
            by_pair,
            pl.BlockSpec((width // 2, width), lambda i: (0, 0)),
            pl.BlockSpec((width // 2, width), lambda i: (0, 0)),
            pl.BlockSpec((8, width), lambda i: (0, 0)),
        ],
        out_shape=[
            shape((rows, width), F32),
            shape((images, pairs, SEQ, PAIR), BF16),
            shape((width // 2, width), BF16),
            shape((width // 2, width), BF16),
            shape((8, width), F32),
        ],
        scratch_shapes=[pltpu.VMEM((chunk, width), BF16), pltpu.VMEM((width, width), F32)],
        compiler_params=params(),
        cost_estimate=cost(14e9, 20e6),
        name="middle",
    )(columns, source, residual, cotangent, context, w_proj, gain_two)


def merge_heads(turned):
    first = jnp.concatenate([turned[:HEAD_DIM, :SPLIT], turned[:HEAD_DIM, 2 * SPLIT : SPLIT + SEQ]], axis=1)
    second = jnp.concatenate([turned[HEAD_DIM:, SPLIT : 2 * SPLIT], turned[HEAD_DIM:, SPLIT + SEQ :]], axis=1)
    return jnp.concatenate([first, second], axis=0).T


def attend_back_kernel(
    chunk,
    grad_context,
    queries,
    keys,
    values,
    weights,
    inverse,
    context,
    normed_one,
    grad_out,
    kept,
    sent,
    value_side,
    grad_scores,
):
    pair = pl.program_id(0)
    image = pl.program_id(1)

    @pl.when((pair == 0) & (image == 0))
    def _():
        is_first, lane = key_sides()
        taken = (is_first & (lane < 2)) | (jnp.logical_not(is_first) & (lane >= 2) & (lane < 4))
        value_side[:, PAIR:] = jnp.where(taken, -1.0, 0.0).astype(BF16)

    key_side = split_heads(keys[0, 0])
    value_side[:, :PAIR] = split_heads(values[0, 0])
    lane = lax.broadcasted_iota(jnp.int32, (chunk, PAIR), 1)
    low = lane < HEAD_DIM
    scaled = []
    for at in range(0, SEQ, chunk):
        rows = slice(at, at + chunk)
        grads = (grad_context[0, 0, rows].astype(F32) * inverse[0, 0, rows]).astype(BF16)
        scaled.append(grads)
        product = grads.astype(F32) * context[0, 0, rows].astype(F32)
        first = jnp.sum(jnp.where(low, product, 0.0), axis=1, keepdims=True)
        second = jnp.sum(jnp.where(low, 0.0, product), axis=1, keepdims=True)
        offset = jnp.where(lane < 2, first, second)
        high = offset.astype(BF16).astype(F32)
        extra = jnp.where(
            (lane == 0) | (lane == 2), high, jnp.where((lane == 1) | (lane == 3), offset - high, 0.0)
        ).astype(BF16)
        grad_weights = dot_last(jnp.concatenate([grads, extra], axis=1), value_side[...])
        part = grad_weights.astype(BF16) * weights[0, 0, rows]
        grad_scores[rows] = part
        place = pl.ds(pl.multiple_of(image * SEQ + at, 32), chunk)
        grad_out[0, pair, place] = (dot(part, key_side) * HEAD_DIM**-0.5).astype(BF16)
    grads = jnp.concatenate(scaled, axis=0)
    place = pl.ds(pl.multiple_of(image * SEQ, 64), SEQ)
    grad_out[1, pair, place] = merge_heads(dot_first(queries[0, 0], grad_scores[...])).astype(BF16)
    grad_out[2, pair, place] = merge_heads(dot_first(grads, weights[0, 0])).astype(BF16)

    @pl.when((pair == pl.num_programs(0) - 1) & (image == pl.num_programs(1) - 1))
    def _():
        for kind in range(3):
            joined = jnp.concatenate([grad_out[kind, at] for at in range(grad_out.shape[1])], axis=1)
            span = joined.shape[1]
            columns = slice(kind * span, (kind + 1) * span)
            total = dot_first(normed_one[...], joined).astype(BF16)
            split_rows(total, kept.at[:, columns], sent.at[:, columns])


def attend_back(grad_context, qkv, weights, inverse, context, normed_one, first, count):
    images, pairs = context.shape[:2]
    rows, width = normed_one.shape

    def block(offset):
        return pl.BlockSpec((1, 1, SEQ, PAIR), lambda p, i: (i, offset + p, 0, 0))

    return pl.pallas_call(
        functools.partial(attend_back_kernel, SEQ),
        grid=(count, images),
        in_specs=[
            block(first),
            block(first),
            block(pairs + first),
            block(2 * pairs + first),
            pl.BlockSpec((1, 1, SEQ, 2 * SEQ), lambda p, i: (i, first + p, 0, 0)),
            block(first),
            block(first),
            whole(normed_one),
        ],
        out_specs=[
            pl.BlockSpec((3, count, rows, PAIR), lambda p, i: (0, 0, 0, 0)),
            pl.BlockSpec((width // 2, 3 * count * PAIR), lambda p, i: (0, 0)),
            pl.BlockSpec((width // 2, 3 * count * PAIR), lambda p, i: (0, 0)),
        ],
        out_shape=[shape((3, count, rows, PAIR), BF16)] + [shape((width // 2, 3 * count * PAIR), BF16)] * 2,
        scratch_shapes=[pltpu.VMEM((2 * SEQ, 2 * PAIR), BF16), pltpu.VMEM((SEQ, 2 * SEQ), BF16)],
        compiler_params=params(),
        cost_estimate=cost(17e9 * (100 if first else 1), 20e6 * (100 if first else 1)),
        name="attend_back",
    )(grad_context, qkv, qkv, qkv, weights, inverse, context, normed_one)


def last_kernel(groups, sub, tokens, w_qkv, grad_residual, gain_one, *rest):
    grads = rest[:groups]
    out, vectors = rest[groups:]
    width = tokens.shape[1]

    @pl.when(pl.program_id(0) == 0)
    def _():
        vectors[...] = jnp.zeros_like(vectors)

    total = jnp.zeros(tokens.shape, F32)
    for kind in range(3):
        joined = jnp.concatenate(
            [grad[kind, at] for grad in grads for at in range(grad.shape[1])], axis=1
        )
        total += dot_last(joined, w_qkv[:, kind * width : (kind + 1) * width])
        if kind == 0:
            vectors[2:3] += column_sum(joined.astype(F32))
        if kind == 2:
            vectors[3:4] += column_sum(joined.astype(F32))
    out[...] = total
    gain = as_row(gain_one)
    for at in range(0, tokens.shape[0], sub):
        rows = slice(at, at + sub)
        grad_normed = out[rows, :]
        unit, inverse = standardize(tokens[rows, :].astype(F32))
        out[rows, :] = grad_residual[rows, :] + standardize_back(grad_normed, gain, unit, inverse)
        vectors[0:1] += column_sum(grad_normed * unit)
        vectors[1:2] += column_sum(grad_normed)


def last(tokens, grads, w_qkv, grad_residual, gain_one, chunk=288):
    rows, width = tokens.shape
    block = pl.BlockSpec((chunk, width), lambda i: (i, 0))
    return pl.pallas_call(
        functools.partial(last_kernel, len(grads), 32),
        grid=(rows // chunk,),
        in_specs=[block, whole(w_qkv), block, whole(gain_one)]
        + [pl.BlockSpec((3, grad.shape[1], chunk, PAIR), lambda i: (0, 0, i, 0)) for grad in grads],
        out_specs=[block, pl.BlockSpec((8, width), lambda i: (0, 0))],
        out_shape=[shape((rows, width), F32), shape((8, width), F32)],
        compiler_params=params(),
        cost_estimate=cost(10e9, 15e6),
        name="last",
    )(tokens, w_qkv, grad_residual, gain_one, *grads)


def fold_kernel(count, *refs):
    inputs, outs = refs[: 2 * count], refs[2 * count :]
    at = lax.axis_index("exp") >> 1
    rows = outs[0].shape[0]
    for other, out in enumerate(outs):
        here = pl.ds(pl.multiple_of((at ^ other) * rows, rows), rows)
        column = 0
        for kept, received in zip(inputs[:count], inputs[count:]):
            span = slice(column, column + kept.shape[1])
            out[:, span] = (kept[here, :].astype(F32) + received[here, :].astype(F32)).astype(BF16)
            column = span.stop


def fold(kept, received, chips):
    rows = kept[0].shape[0] // chips
    width = sum(part.shape[1] for part in kept)
    return pl.pallas_call(
        functools.partial(fold_kernel, len(kept)),
        out_shape=[shape((rows, width), BF16)] * chips,
        compiler_params=params(),
        cost_estimate=cost(1e9, 10e6),
        name="fold",
    )(*kept, *received)


def finish_kernel(left, where, *refs):
    inputs, (proj_out, out) = refs[:-2], refs[-2:]
    width = proj_out.shape[1]
    right = width - left
    for step, part in enumerate(inputs):

        @pl.when(pl.program_id(0) == step)
        def _():
            proj_out[...] = part[:, :width].astype(F32)
            for kind in range(3):
                to = kind * width
                at = width + kind * left
                out[:, to : to + left] = part[:, at : at + left].astype(F32)
                at = width + 3 * left + kind * right
                out[:, to + left : to + width] = part[:, at : at + right].astype(F32)


def finish(parts, where, left):
    steps = len(parts)
    rows = parts[0].shape[0]
    width = parts[0].shape[1] // 4

    def landing(columns):
        return pl.BlockSpec((rows, columns), lambda i, at: (at[i], 0))

    return pl.pallas_call(
        functools.partial(finish_kernel, left),
        grid_spec=pltpu.PrefetchScalarGridSpec(
            num_scalar_prefetch=1,
            grid=(steps,),
            in_specs=[pl.BlockSpec(part.shape, lambda i, at: (0, 0)) for part in parts],
            out_specs=[landing(width), landing(3 * width)],
        ),
        out_shape=[shape((rows * steps, width), F32), shape((rows * steps, 3 * width), F32)],
        compiler_params=params(),
        cost_estimate=cost(1e9, 10e6),
        name="finish",
    )(where, *parts)


def combine_kernel(columns, source, residual, out):
    hits = token_hits(columns, source.shape[0])
    out[...] = (residual[...] + dot(hits, source[...])).astype(BF16)


def combine(columns, source, residual, chunk=288):
    rows, width = residual.shape
    return pl.pallas_call(
        combine_kernel,
        grid=(rows // chunk,),
        in_specs=[
            pl.BlockSpec((chunk, 8), lambda i: (i, 0)),
            whole(source),
            pl.BlockSpec((chunk, width), lambda i: (i, 0)),
        ],
        out_specs=pl.BlockSpec((chunk, width), lambda i: (i, 0)),
        out_shape=shape((rows, width), BF16),
        compiler_params=params(),
        cost_estimate=cost(6e9, 10e6),
        name="combine",
    )(columns, source, residual)


def exchange(rows, experts):
    blocks = rows.reshape(experts, rows.shape[0] // experts, rows.shape[1])
    return lax.all_to_all(blocks, "exp", split_axis=0, concat_axis=0, tiled=True).reshape(rows.shape)


def share(block, name, size):
    copies = jnp.broadcast_to(block[None], (size,) + block.shape)
    return lax.all_to_all(copies, name, split_axis=0, concat_axis=0, tiled=True)


def sum_blocks(blocks, kind):
    return jnp.sum(blocks.astype(F32), axis=0).astype(kind)


def scatter_reps(blocks):
    rows = blocks.reshape((-1,) + blocks.shape[2:])
    return lax.psum_scatter(rows, "rep", scatter_dimension=0, tiled=True)


def swap(block, name, bits, size):
    return lax.ppermute(block, name, [(at, at ^ bits) for at in range(size)])


def chip_scatter(kept, sent, sizes):
    size = sizes["exp"]
    chips = size // 2
    received = [swap(part, "exp", 1, size) for part in sent]
    parts = fold(kept, received, chips)
    return parts


def plane_sum(parts, sizes):
    size = sizes["exp"]
    chips = size // 2
    received = [swap(parts[other], "exp", 2 * other, size) for other in range(1, chips)]
    total = parts[0].astype(F32)
    for part in received:
        total += part.astype(F32)
    return total.astype(BF16)


def rep_sum(block, sizes):
    reps = sizes["rep"]
    blocks = block.reshape((reps, -1) + block.shape[1:])
    at = lax.convert_element_type(lax.axis_index("rep"), jnp.uint32)

    def pick(other):
        return lax.dynamic_index_in_dim(blocks, at ^ jnp.uint32(other), 0, keepdims=False)

    received = [swap(pick(other), "rep", other, reps) for other in range(1, reps)]
    total = pick(0).astype(F32)
    for part in received:
        total += part.astype(F32)
    return total.astype(BF16)


def rep_gather(block, sizes):
    reps = sizes["rep"]
    at = lax.axis_index("rep")
    parts = [block] + [swap(block, "rep", other, reps) for other in range(1, reps)]
    rows = []
    for slot in range(reps):
        chosen = parts[0]
        for other in range(1, reps):
            chosen = jnp.where((at ^ other) == slot, parts[other], chosen)
        rows.append(chosen)
    return jnp.concatenate(rows, axis=0)


def plane_gather(block, sizes):
    size = sizes["exp"]
    mine = [block] + [swap(block, "exp", 2 * other, size) for other in range(1, size // 2)]
    return mine + [swap(part, "exp", 1, size) for part in mine]


def join_halves(kept, sent):
    first = (lax.axis_index("exp") & 1) == 0
    return jnp.where(first, jnp.concatenate([kept, sent]), jnp.concatenate([sent, kept]))


def small_sums(vectors_two, vectors_one, router_grad):
    blank = jnp.zeros_like(vectors_one[:1])
    return jnp.concatenate([vectors_two[:3], vectors_one[:4], blank, router_grad], axis=0)


def tie(value, *after):
    return lax.optimization_barrier((value,) + after)[0]


def on_device(
    sizes,
    tokens,
    cotangent,
    expert_ids,
    expert_slots,
    w_qkv,
    q_bias,
    v_bias,
    w_proj,
    proj_bias,
    gain_one,
    shift_one,
    gain_two,
    shift_two,
    w_router,
    expert_in,
    expert_in_bias,
    expert_out,
    expert_out_bias,
):
    row_count, width = tokens.shape
    experts = w_router.shape[1]
    slot_count = row_count // experts
    reps = sizes["rep"]
    ids = expert_ids.T
    slots = expert_slots.T
    router_turned = w_router.T
    weight_in = expert_in[0]
    weight_out = expert_out[0]
    bias_in = expert_in_bias.astype(F32)
    bias_out = expert_out_bias.astype(F32)

    cot_arrived = exchange(gather(ids, slots, cotangent, slot_count), experts)
    normed_one, qkv, weights, inverse, context, residual, dispatched = front(
        tokens,
        w_qkv,
        jnp.concatenate([q_bias, v_bias, proj_bias]).astype(F32),
        w_proj,
        gain_one,
        shift_one,
        gain_two,
        shift_two,
        ids,
        slots,
        slot_count,
    )
    arrived = exchange(dispatched, experts)
    raw, columns, cot_turned, along = raw_active(ids, slots, cot_arrived, weight_out, bias_out, slot_count)
    active, grad_hidden, out_grad, gate, logits_grad = expert(
        arrived, cot_turned, weight_in, bias_in, raw, along, router_turned, reps
    )
    grad_eout = scatter_reps(out_grad)
    back, router_grad = expert_back(grad_hidden, weight_in, gate, logits_grad, router_turned, arrived)
    source = exchange(back, experts)
    made, out_bias_grad = produce(gate, active, cot_arrived, weight_out, bias_out)
    part = weight_in.shape[1] // reps
    out_part = width // reps
    tail = jnp.pad(out_bias_grad.reshape(reps, 1, out_part), ((0, 0), (0, 0), (0, part - out_part)))
    in_first, in_second = weight_in_grad(arrived, gate, grad_hidden, tail, reps)
    source, made, in_first, in_second = lax.optimization_barrier((source, made, in_first, in_second))
    in_first = scatter_reps(in_first)
    returned = exchange(made, experts)
    grad_residual, grad_context, proj_kept, proj_sent, vectors_two = middle(
        columns, source, residual, cotangent, context, w_proj, gain_two
    )
    pairs = width // PAIR
    most = pairs - pairs // 3
    saved = (qkv, weights, inverse, context, normed_one)
    grads_a, kept_a, sent_a = attend_back(grad_context, *saved, 0, most)
    chips = sizes["exp"] // 2
    if (width // sizes["exp"]) % 16 == 0:
        sent_a, proj_sent, returned = lax.optimization_barrier((sent_a, proj_sent, returned))
        parts_a = chip_scatter((proj_kept, kept_a), (proj_sent, sent_a), sizes)
        sum_a = plane_sum(parts_a, sizes)
        grads_b, kept_b, sent_b = attend_back(
            tie(grad_context, grads_a, parts_a[0], grad_eout), *saved, most, pairs - most
        )
        parts_b = chip_scatter((kept_b,), (sent_b,), sizes)
        sum_b = plane_sum(parts_b, sizes)
        grad_tokens, vectors_one = last(
            tokens, (grads_a, grads_b), w_qkv, tie(grad_residual, parts_b[0]), gain_one
        )
        sum_a, sum_b, vectors_one, in_first = lax.optimization_barrier((sum_a, sum_b, vectors_one, in_first))
        block = jnp.concatenate([sum_a, sum_b], axis=1)
        small = small_sums(vectors_two, vectors_one, router_grad)
        small = sum_blocks(share(small, "exp", sizes["exp"]), F32)
        mixed = combine(columns, tie(returned, block), residual)
        block = rep_sum(block, sizes)
        block, mixed, small = lax.optimization_barrier((block, mixed, small))
        block = rep_gather(block, sizes)
        block, in_second = lax.optimization_barrier((block, in_second))
        in_second = scatter_reps(in_second)
        small = sum_blocks(share(small, "rep", reps), F32)
        parts = plane_gather(block, sizes)
        here = lax.axis_index("exp")
        order = jnp.arange(chips, dtype=jnp.int32) ^ (here >> 1)
        core = here & 1
        where = jnp.concatenate([core * chips + order, (1 - core) * chips + order]).astype(jnp.int32)
        grad_w_proj, grad_w_qkv = finish(parts, where, most * PAIR)
    else:
        in_second = scatter_reps(in_second)
        grads_b, kept_b, sent_b = attend_back(grad_context, *saved, most, pairs - most)
        mixed = combine(columns, returned, residual)
        grad_tokens, vectors_one = last(tokens, (grads_a, grads_b), w_qkv, grad_residual, gain_one)
        block = join_halves(
            jnp.concatenate([proj_kept, kept_a, kept_b], axis=1),
            jnp.concatenate([proj_sent, sent_a, sent_b], axis=1),
        )
        small = lax.psum(small_sums(vectors_two, vectors_one, router_grad), ("rep", "exp"))
        block = lax.psum(block, ("rep", "exp"))
        where = jnp.zeros((1,), jnp.int32)
        grad_w_proj, grad_w_qkv = finish((block,), where, most * PAIR)
    return (
        mixed,
        grad_tokens,
        grad_w_qkv,
        small[5],
        small[6],
        grad_w_proj,
        small[2],
        small[3],
        small[4],
        small[0],
        small[1],
        small[8 : 8 + experts].T,
        jnp.concatenate([in_first[: width // 2], in_second], axis=0)[None].astype(F32),
        in_first[width // 2 : width // 2 + 1].astype(F32),
        turn(grad_eout)[None],
        in_first[width // 2 + 1 : width // 2 + 2, :out_part].astype(F32),
    )


def solution(mesh):
    rows = P(("rep", "exp"), None)
    placed = (rows,) * 4 + (P(),) * 10 + (
        P("exp", None, None),
        P("exp", None),
        P("exp", None, None),
        P("exp", None),
    )
    return jax.shard_map(
        functools.partial(on_device, dict(mesh.shape)),
        mesh=mesh,
        in_specs=placed,
        out_specs=(rows, rows)
        + (P(),) * 10
        + (P("exp", None, "rep"), P("exp", "rep"), P("exp", "rep", None), P("exp", "rep")),
        check_vma=False,
    )
```

```python
import functools

import jax
import jax.numpy as jnp
from jax import lax
from jax.experimental import pallas as pl
from jax.experimental.pallas import tpu as pltpu
from jax.sharding import PartitionSpec as P

HEAD_DIM = 64
SEQ = 576
PAIR = 2 * HEAD_DIM
SPLIT = 512
AUX = 128
EPSILON = 1e-06
F32 = jnp.float32
BF16 = jnp.bfloat16
VMEM_BYTES = 56 * 2**20


def dot(left, right):
    return lax.dot_general(left, right, (((1,), (0,)), ((), ())), preferred_element_type=F32)


def dot_last(left, right):
    return lax.dot_general(left, right, (((1,), (1,)), ((), ())), preferred_element_type=F32)


def dot_first(left, right):
    return lax.dot_general(left, right, (((0,), (0,)), ((), ())), preferred_element_type=F32)


def thirds(value):
    high = value.astype(BF16)
    rest = value - high.astype(F32)
    middle = rest.astype(BF16)
    return high, middle, (rest - middle.astype(F32)).astype(BF16)


def standardize(field):
    centred = field - jnp.mean(field, axis=-1, keepdims=True)
    inverse = lax.rsqrt(jnp.mean(centred * centred, axis=-1, keepdims=True) + EPSILON)
    return centred * inverse, inverse


def standardize_back(grad, gain, unit, inverse):
    scaled = grad * gain
    along = jnp.mean(scaled * unit, axis=-1, keepdims=True)
    return inverse * (scaled - jnp.mean(scaled, axis=-1, keepdims=True) - unit * along)


def as_row(ref):
    return ref[...].astype(F32).reshape(1, -1)


def column_sum(field):
    return jnp.sum(field, axis=0, keepdims=True)


def params(most=False):
    return pltpu.CompilerParams(vmem_limit_bytes=63 * 2**20 if most else VMEM_BYTES)


SCALE = 0.01
EARLY = 20
EXPERT_CHUNK = 768
EXPERT_ROWS = 576


def cost(flops, bytes_moved):
    return pl.CostEstimate(flops=int(flops * SCALE), transcendentals=0, bytes_accessed=int(bytes_moved * SCALE))


def whole(array):
    return pl.BlockSpec(array.shape, lambda *ids: (0,) * array.ndim)


def shape(dims, kind):
    return jax.ShapeDtypeStruct(dims, kind)


def split_heads(pair):
    lane = lax.broadcasted_iota(jnp.int32, pair.shape, 1)
    zero = jnp.zeros_like(pair)
    first = jnp.where(lane < HEAD_DIM, pair, zero)
    second = jnp.where(lane < HEAD_DIM, zero, pair)
    return jnp.concatenate([first[:SPLIT], second[:SPLIT], first[SPLIT:], second[SPLIT:]], axis=0)


def key_sides():
    row = lax.broadcasted_iota(jnp.int32, (2 * SEQ, PAIR), 0)
    lane = lax.broadcasted_iota(jnp.int32, (2 * SEQ, PAIR), 1)
    is_first = (row < SPLIT) | ((row >= 2 * SPLIT) & (row < SPLIT + SEQ))
    return is_first, lane


def columns_of(ids, slots, slot_count):
    return jnp.where(slots[...] >= 0, ids[...] * slot_count + slots[...], -1)


def slot_hits(columns, at, count):
    slot = at + lax.broadcasted_iota(jnp.int32, (count, columns.shape[1]), 0)
    hit = (columns[0:1, :] == slot) | (columns[1:2, :] == slot)
    return jnp.where(hit, 1.0, 0.0).astype(BF16)


def front_kernel(
    chunk,
    slot_count,
    tokens,
    w_qkv_hbm,
    biases,
    w_proj_hbm,
    gain_one,
    shift_one,
    gain_two,
    shift_two,
    ids,
    slots,
    normed_one_out,
    qkv_out,
    weights_out,
    inverse_out,
    context_out,
    residual_out,
    dispatched_out,
    value_side,
    normed_two,
    w_qkv,
    w_proj,
    normed_one,
    qkv,
    residual_held,
    arrivals,
    departures,
):
    image = pl.program_id(0)
    pair = pl.program_id(1)
    pairs = context_out.shape[1]
    here = pl.ds(pl.multiple_of(image * SEQ, SEQ), SEQ)
    load_qkv = pltpu.make_async_copy(w_qkv_hbm, w_qkv, arrivals.at[0])
    load_proj = pltpu.make_async_copy(w_proj_hbm, w_proj, arrivals.at[1])
    save_normed = pltpu.make_async_copy(normed_one, normed_one_out.at[here], departures.at[0])
    save_qkv = pltpu.make_async_copy(qkv, qkv_out.at[image], departures.at[1])
    save_residual = pltpu.make_async_copy(residual_held, residual_out.at[here], departures.at[2])

    @pl.when((image == 0) & (pair == 0))
    def _():
        load_qkv.start()
        load_proj.start()
        is_first, lane = key_sides()
        value_side[:, PAIR:] = jnp.where(is_first == (lane < HEAD_DIM), 1.0, 0.0).astype(BF16)

    @pl.when(pair == 0)
    def _():
        unit, _ = standardize(tokens[...].astype(F32))
        normed_one[...] = (unit * as_row(gain_one) + as_row(shift_one)).astype(BF16)

    @pl.when((image == 0) & (pair == 0))
    def _():
        load_qkv.wait()

    @pl.when(pair == 0)
    def _():
        normed = normed_one[...]
        width = w_qkv.shape[1]
        third = width // 3
        step = 2 * PAIR
        for at in range(0, width, step):
            part = dot(normed, w_qkv[:, at : at + step])
            if at < third:
                part = part + as_row(biases)[:, at : at + step]
            if at >= 2 * third:
                part = part + as_row(biases)[:, at - third : at - third + step]
            part = part.astype(BF16)
            if at < third:
                part = part * jnp.asarray(HEAD_DIM**-0.5, BF16)
            qkv[at // PAIR] = part[:, :PAIR]
            qkv[at // PAIR + 1] = part[:, PAIR:]
        save_normed.start()
        save_qkv.start()

    keys = split_heads(qkv[pairs + pair])
    value_side[:, :PAIR] = split_heads(qkv[2 * pairs + pair])
    values = value_side[...]
    low = lax.broadcasted_iota(jnp.int32, (chunk, PAIR), 1) < HEAD_DIM
    for at in range(0, SEQ, chunk):
        rows = slice(at, at + chunk)
        scores = dot_last(qkv[pair, rows], keys)
        first = scores[:, :SPLIT]
        second = scores[:, SPLIT : 2 * SPLIT]
        tail = scores[:, 2 * SPLIT :]
        first_max = jnp.maximum(
            jnp.max(first, axis=1, keepdims=True),
            jnp.max(jnp.where(low, tail, -jnp.inf), axis=1, keepdims=True),
        )
        second_max = jnp.maximum(
            jnp.max(second, axis=1, keepdims=True),
            jnp.max(jnp.where(low, -jnp.inf, tail), axis=1, keepdims=True),
        )
        exponent = jnp.concatenate(
            [
                jnp.exp(first - first_max).astype(BF16),
                jnp.exp(second - second_max).astype(BF16),
                jnp.exp(tail - jnp.where(low, first_max, second_max)).astype(BF16),
            ],
            axis=1,
        )
        weights_out[0, 0, rows] = exponent
        summed = dot(exponent, values)
        inverse = 1.0 / summed[:, PAIR:]
        inverse_out[0, 0, rows] = inverse
        context_out[0, pair, rows] = (summed[:, :PAIR] * inverse).astype(BF16)

    @pl.when((image == 0) & (pair == pairs - 1))
    def _():
        load_proj.wait()

    @pl.when((image > 0) & (pair == pairs - 1))
    def _():
        before = pl.ds(pl.multiple_of((image - 1) * SEQ, SEQ), SEQ)
        pltpu.make_async_copy(residual_held, residual_out.at[before], departures.at[2]).wait()

    @pl.when(pair == pairs - 1)
    def _():
        context = jnp.concatenate([context_out[0, at] for at in range(pairs)], axis=1)
        offset = as_row(biases)[:, 2 * tokens.shape[1] :]
        residual = tokens[...].astype(F32) + (dot(context, w_proj[...]) + offset)
        residual_held[...] = residual
        save_residual.start()
        unit, _ = standardize(residual)
        normed = (unit * as_row(gain_two) + as_row(shift_two)).astype(BF16)
        normed_two[here] = normed
        save_normed.wait()
        save_qkv.wait()

    @pl.when((pair == pairs - 1) & (image == pl.num_programs(0) - 1))
    def _():
        columns = columns_of(ids, slots, slot_count)
        part = SEQ // 2
        for at in range(0, dispatched_out.shape[0], part):
            hits = slot_hits(columns, at, part)
            dispatched_out[at : at + part] = dot(hits, normed_two[...]).astype(BF16)
        save_residual.wait()


def front(tokens, w_qkv, biases, w_proj, gain_one, shift_one, gain_two, shift_two, ids, slots, slot_count):
    rows, width = tokens.shape
    images = rows // SEQ
    pairs = width // PAIR

    def per_image(columns):
        return pl.BlockSpec((SEQ, columns), lambda i, p: (i, 0))

    anywhere = pl.BlockSpec(memory_space=pl.ANY)
    fixed = (gain_one, shift_one, gain_two, shift_two, ids, slots)
    return pl.pallas_call(
        functools.partial(front_kernel, SEQ // 2, slot_count),
        grid=(images, pairs),
        in_specs=[per_image(width), anywhere, whole(biases), anywhere] + [whole(array) for array in fixed],
        out_specs=[
            anywhere,
            anywhere,
            pl.BlockSpec((1, 1, SEQ, 2 * SEQ), lambda i, p: (i, p, 0, 0)),
            pl.BlockSpec((1, 1, SEQ, PAIR), lambda i, p: (i, p, 0, 0)),
            pl.BlockSpec((1, pairs, SEQ, PAIR), lambda i, p: (i, 0, 0, 0)),
            anywhere,
            pl.BlockSpec((rows, width), lambda i, p: (0, 0)),
        ],
        out_shape=[
            shape((rows, width), BF16),
            shape((images, 3 * pairs, SEQ, PAIR), BF16),
            shape((images, pairs, SEQ, 2 * SEQ), BF16),
            shape((images, pairs, SEQ, PAIR), F32),
            shape((images, pairs, SEQ, PAIR), BF16),
            shape((rows, width), F32),
            shape((rows, width), BF16),
        ],
        scratch_shapes=[
            pltpu.VMEM((2 * SEQ, 2 * PAIR), BF16),
            pltpu.VMEM((rows, width), BF16),
            pltpu.VMEM(w_qkv.shape, BF16),
            pltpu.VMEM(w_proj.shape, BF16),
            pltpu.VMEM((SEQ, width), BF16),
            pltpu.VMEM((3 * pairs, SEQ, PAIR), BF16),
            pltpu.VMEM((SEQ, width), F32),
            pltpu.SemaphoreType.DMA((2,)),
            pltpu.SemaphoreType.DMA((3,)),
        ],
        compiler_params=params(True),
        cost_estimate=cost(30e9, 60e6),
        name="front",
    )(tokens, w_qkv, biases, w_proj, *fixed)


def gather_kernel(chunk, slot_count, ids, slots, rows, out):
    columns = columns_of(ids, slots, slot_count)
    hits = slot_hits(columns, pl.program_id(0) * chunk, chunk)
    out[...] = dot(hits, rows[...]).astype(BF16)


def gather(ids, slots, rows, slot_count, chunk=288):
    count, width = rows.shape
    return pl.pallas_call(
        functools.partial(gather_kernel, chunk, slot_count),
        grid=(count // chunk,),
        in_specs=[whole(ids), whole(slots), whole(rows)],
        out_specs=pl.BlockSpec((chunk, width), lambda i: (i, 0)),
        out_shape=shape((count, width), BF16),
        compiler_params=params(True),
        cost_estimate=cost(4e9, 8e6),
        name="gather",
    )(ids, slots, rows)


def raw_kernel(slot_count, ids, slots, cotangent, weight_out, bias_out, out, columns_out, turned, along):
    @pl.when(pl.program_id(0) == 0)
    def _():
        columns = columns_of(ids, slots, slot_count)
        pad = jnp.full((6, columns.shape[1]), -1, jnp.int32)
        columns_out[...] = jnp.concatenate([columns, pad], axis=0).T
        turned[...] = cotangent[...].T
        for at in range(0, along.shape[0], 32):
            rows = slice(at, at + 32)
            along[rows, :] = lane_sums(cotangent[rows, :].astype(F32) * bias_out[...])

    out[...] = dot_last(cotangent[...], weight_out[...]).astype(BF16)


def raw_active(ids, slots, cotangent, weight_out, bias_out, slot_count, chunk=768):
    count, width = cotangent.shape
    hidden = weight_out.shape[0]
    return pl.pallas_call(
        functools.partial(raw_kernel, slot_count),
        grid=(hidden // chunk,),
        in_specs=[
            whole(ids),
            whole(slots),
            whole(cotangent),
            pl.BlockSpec((chunk, width), lambda i: (i, 0)),
            whole(bias_out),
        ],
        out_specs=[
            pl.BlockSpec((count, chunk), lambda i: (0, i)),
            pl.BlockSpec((count, 8), lambda i: (0, 0)),
            pl.BlockSpec((width, count), lambda i: (0, 0)),
            pl.BlockSpec((count, AUX), lambda i: (0, 0)),
        ],
        out_shape=[
            shape((count, hidden), BF16),
            shape((count, 8), jnp.int32),
            shape((width, count), BF16),
            shape((count, AUX), F32),
        ],
        compiler_params=params(True),
        cost_estimate=cost(9e9, 14e6),
        name="raw_active",
    )(ids, slots, cotangent, weight_out, bias_out)


def joined_thirds(value, order):
    parts = thirds(value)
    return jnp.concatenate([parts[at] for at in order], axis=1)


LEFT = (0, 0, 1, 1, 0, 2)
RIGHT = (0, 1, 0, 1, 2, 0)


def expert_kernel(
    row_chunk,
    arrived,
    cot_turned,
    weight_in,
    bias_in,
    raw,
    along,
    w_router,
    active_out,
    hidden_out,
    weight_grad,
    gate_out,
    logits_grad,
    produced_grad,
    gate_total,
    router,
):
    step = pl.program_id(0)
    count = arrived.shape[0]
    experts = w_router.shape[0]

    @pl.when(step == 0)
    def _():
        parts = dot_last(arrived[...], jnp.concatenate(thirds(w_router[...]), axis=0))
        logits = parts[:, :experts] + (parts[:, experts : 2 * experts] + parts[:, 2 * experts :])
        exponent = jnp.exp(logits - jnp.max(logits, axis=1, keepdims=True))
        probs = exponent / jnp.sum(exponent, axis=1, keepdims=True)
        router[...] = probs
        own = lax.broadcasted_iota(jnp.int32, (count, experts), 1) == lax.axis_index("exp")
        gate = jnp.sum(jnp.where(own, probs, 0.0), axis=1, keepdims=True)
        gate_out[...] = jnp.broadcast_to(gate, gate_out.shape)
        gate_row = gate_out[...].T[0:1]
        produced_grad[...] = (cot_turned[...].astype(F32) * gate_row).astype(BF16)
        gate_total[...] = along[...]

    for at in range(0, count, row_chunk):
        rows = slice(at, at + row_chunk)
        hidden = dot(arrived[rows, :], weight_in[...]) + bias_in[...]
        scaled = hidden * (0.5**0.5)
        curve = lax.erf(scaled)
        half = 0.5 * hidden
        active = (half + half * curve).astype(BF16)
        bell = jnp.exp(scaled * -scaled) * (0.5 * 1.1283791670955126 * 0.5**0.5)
        slope = ((0.5 + 0.5 * curve) + hidden * bell).astype(BF16)
        incoming = raw[rows, :]
        active_out[rows, :] = active
        hidden_out[rows, :] = incoming * slope
        gate_total[rows, :] += lane_sums((incoming * active).astype(F32))
    weight_grad[0] = dot(produced_grad[...], active_out[...]).astype(BF16)

    @pl.when(step == pl.num_programs(0) - 1)
    def _():
        own = lax.broadcasted_iota(jnp.int32, (count, experts), 1) == lax.axis_index("exp")
        scale = jnp.sum(gate_total[...], axis=1, keepdims=True) * gate_out[:, 0:1]
        logits_grad[...] = scale * (jnp.where(own, 1.0, 0.0) - router[...])


def lane_sums(field):
    total = field[:, :AUX]
    for at in range(AUX, field.shape[1], AUX):
        total = total + field[:, at : at + AUX]
    return total


def expert(arrived, cot_turned, weight_in, bias_in, raw, along, w_router, reps, chunk=EXPERT_CHUNK):
    count, width = arrived.shape
    hidden = weight_in.shape[1]
    experts = w_router.shape[0]
    part = hidden // reps
    cuts = part // chunk

    def column_block(rows):
        return pl.BlockSpec((rows, chunk), lambda i: (0, i))

    def fixed(rows, columns):
        return pl.BlockSpec((rows, columns), lambda i: (0, 0))

    return pl.pallas_call(
        functools.partial(expert_kernel, EXPERT_ROWS),
        grid=(hidden // chunk,),
        in_specs=[
            whole(arrived),
            whole(cot_turned),
            column_block(width),
            column_block(1),
            column_block(count),
            whole(along),
            whole(w_router),
        ],
        out_specs=[
            column_block(count),
            column_block(count),
            pl.BlockSpec((1, width, chunk), lambda i: (i // cuts, 0, i % cuts)),
            fixed(count, AUX),
            fixed(count, experts),
        ],
        out_shape=[
            shape((count, hidden), BF16),
            shape((count, hidden), BF16),
            shape((reps, width, part), BF16),
            shape((count, AUX), F32),
            shape((count, experts), F32),
        ],
        scratch_shapes=[
            pltpu.VMEM((width, count), BF16),
            pltpu.VMEM((count, AUX), F32),
            pltpu.VMEM((count, experts), F32),
        ],
        compiler_params=params(True),
        cost_estimate=cost(24e9, 35e6),
        name="expert",
    )(arrived, cot_turned, weight_in, bias_in, raw, along, w_router)


def expert_back_kernel(grad_hidden, weight_in, gate, logits_grad, w_router, arrived, out, router_grad):
    experts = w_router.shape[0]

    @pl.when(pl.program_id(0) == 0)
    def _():
        router_grad[...] = jnp.zeros_like(router_grad)

    right = jnp.concatenate([thirds(w_router[...])[at] for at in RIGHT], axis=0)
    total = gate[:, 0:1] * dot_last(grad_hidden[...], weight_in[...])
    total += dot(joined_thirds(logits_grad[...], LEFT), right)
    out[...] = total.astype(BF16)
    parts = dot_first(joined_thirds(logits_grad[...], (0, 1, 2)), arrived[...])
    router_grad[...] += parts[:experts] + parts[experts : 2 * experts] + parts[2 * experts :]


def expert_back(grad_hidden, weight_in, gate, logits_grad, w_router, arrived, chunk=288):
    count, hidden = grad_hidden.shape
    experts, width = w_router.shape

    def rows(columns):
        return pl.BlockSpec((chunk, columns), lambda i: (i, 0))

    return pl.pallas_call(
        expert_back_kernel,
        grid=(count // chunk,),
        in_specs=[rows(hidden), whole(weight_in), rows(AUX), rows(experts), whole(w_router), rows(width)],
        out_specs=[rows(width), pl.BlockSpec((experts, width), lambda i: (0, 0))],
        out_shape=[shape((count, width), BF16), shape((experts, width), F32)],
        compiler_params=params(True),
        cost_estimate=cost(12e9, 15e6),
        name="expert_back",
    )(grad_hidden, weight_in, gate, logits_grad, w_router, arrived)


def turn_kernel(field, out):
    out[...] = field[...].T.astype(F32)


def turn(field):
    return pl.pallas_call(
        turn_kernel,
        out_shape=shape(field.shape[::-1], F32),
        compiler_params=params(),
        cost_estimate=cost(1e9, 5e6),
        name="turn",
    )(field)


def early_rows(width):
    return width // 48 * EARLY


def weight_in_kernel(arrived, gate, grad_hidden, out_bias_grad, first, second, turned):
    width = arrived.shape[1]
    half = first.shape[1] - 16

    @pl.when(pl.program_id(0) == 0)
    def _():
        for at in range(0, arrived.shape[0], 128):
            rows = slice(at, at + 128)
            turned[:width, rows] = (arrived[rows, :].astype(F32) * gate[rows, 0:1]).astype(BF16).T
        gate_row = jnp.broadcast_to(gate[...].T[0:1], (16, arrived.shape[0]))
        high = gate_row.astype(BF16)
        row = lax.broadcasted_iota(jnp.int32, high.shape, 0)
        low = (gate_row - high.astype(F32)).astype(BF16)
        turned[width:] = jnp.where(row == 0, high, jnp.where(row == 1, low, jnp.zeros_like(low)))

    total = dot(turned[...], grad_hidden[...])
    second[0] = total[half:width].astype(BF16)
    first[0, :half] = total[:half].astype(BF16)
    row = lax.broadcasted_iota(jnp.int32, (first.shape[1] - half, first.shape[2]), 0)
    bias_grad = total[width : width + 1] + total[width + 1 : width + 2]
    first[0, half:] = jnp.where(row == 0, bias_grad, jnp.where(row == 1, out_bias_grad[0], 0.0)).astype(BF16)


def weight_in_grad(arrived, gate, grad_hidden, out_bias_grad, reps):
    count, hidden = grad_hidden.shape
    width = arrived.shape[1]
    early = early_rows(width)
    part = hidden // reps
    return pl.pallas_call(
        weight_in_kernel,
        grid=(reps,),
        in_specs=[
            whole(arrived),
            whole(gate),
            pl.BlockSpec((count, part), lambda i: (0, i)),
            pl.BlockSpec((1, 1, part), lambda i: (i, 0, 0)),
        ],
        out_specs=[
            pl.BlockSpec((1, early + 16, part), lambda i: (i, 0, 0)),
            pl.BlockSpec((1, width - early, part), lambda i: (i, 0, 0)),
        ],
        out_shape=[shape((reps, early + 16, part), BF16), shape((reps, width - early, part), BF16)],
        scratch_shapes=[pltpu.VMEM((width + 16, count), BF16)],
        compiler_params=params(True),
        cost_estimate=cost(10e9, 15e6),
        name="weight_in_grad",
    )(arrived, gate, grad_hidden, out_bias_grad)


def produce_kernel(gate, active, cotangent, weight_out, bias_out, out, bias_grad):
    @pl.when(pl.program_id(0) == 0)
    def _():
        bias_grad[...] = jnp.zeros_like(bias_grad)

    bias_grad[...] += column_sum(gate[:, 0:1] * cotangent[...].astype(F32))
    out[...] = (gate[:, 0:1] * (dot(active[...], weight_out[...]) + bias_out[...])).astype(BF16)


def produce(gate, active, cotangent, weight_out, bias_out, chunk=288):
    count, hidden = active.shape
    width = weight_out.shape[1]

    def rows(columns):
        return pl.BlockSpec((chunk, columns), lambda i: (i, 0))

    return pl.pallas_call(
        produce_kernel,
        grid=(count // chunk,),
        in_specs=[rows(AUX), rows(hidden), rows(width), whole(weight_out), whole(bias_out)],
        out_specs=[rows(width), pl.BlockSpec((1, width), lambda i: (0, 0))],
        out_shape=[shape((count, width), BF16), shape((1, width), F32)],
        compiler_params=params(True),
        cost_estimate=cost(10e9, 15e6),
        name="produce",
    )(gate, active, cotangent, weight_out, bias_out)


def token_hits(columns, slots):
    slot = lax.broadcasted_iota(jnp.int32, (columns.shape[0], slots), 1)
    hit = (columns[:, 0:1] == slot) | (columns[:, 1:2] == slot)
    return jnp.where(hit, 1.0, 0.0).astype(BF16)


def split_rows(value, kept, sent):
    half = value.shape[0] // 2
    first = (lax.axis_index("exp") & 1) == 0
    low, high = value[:half], value[half:]
    kept[...] = jnp.where(first, low, high)
    sent[...] = jnp.where(first, high, low)


def middle_kernel(
    sub,
    columns,
    source,
    residual,
    cotangent,
    context,
    w_proj,
    gain_two,
    grad_residual_out,
    grad_context_out,
    proj_kept,
    proj_sent,
    vectors,
    branch,
    proj_total,
):
    step = pl.program_id(0)
    chunk = residual.shape[0]
    pairs = context.shape[1]

    @pl.when(step == 0)
    def _():
        vectors[...] = jnp.zeros_like(vectors)
        proj_total[...] = jnp.zeros_like(proj_total)

    hits = token_hits(columns, source.shape[0])
    grad_residual_out[...] = dot(hits, source[...])
    gain = as_row(gain_two)
    for at in range(0, chunk, sub):
        rows = slice(at, at + sub)
        grad_normed = grad_residual_out[rows, :]
        unit, inverse = standardize(residual[rows, :])
        grad_residual = cotangent[rows, :].astype(F32) + standardize_back(grad_normed, gain, unit, inverse)
        grad_residual_out[rows, :] = grad_residual
        rounded = grad_residual.astype(BF16)
        branch[rows, :] = rounded
        vectors[0:1] += column_sum(grad_normed * unit)
        vectors[1:2] += column_sum(grad_normed)
        vectors[2:3] += column_sum(rounded.astype(F32))
    grad_context = dot_last(branch[...], w_proj[...]).astype(BF16)
    for pair in range(pairs):
        grad_context_out[0, pair] = grad_context[:, pair * PAIR : (pair + 1) * PAIR]
    joined = jnp.concatenate([context[0, pair] for pair in range(pairs)], axis=1)
    proj_total[...] += dot_first(joined, branch[...])

    @pl.when(step == pl.num_programs(0) - 1)
    def _():
        split_rows(proj_total[...].astype(BF16), proj_kept, proj_sent)


def middle(columns, source, residual, cotangent, context, w_proj, gain_two, chunk=288):
    rows, width = residual.shape
    images, pairs = context.shape[:2]
    parts = SEQ // chunk

    def rows_of(columns):
        return pl.BlockSpec((chunk, columns), lambda i: (i, 0))

    by_pair = pl.BlockSpec((1, pairs, chunk, PAIR), lambda i: (i // parts, 0, i % parts, 0))
    return pl.pallas_call(
        functools.partial(middle_kernel, 32),
        grid=(rows // chunk,),
        in_specs=[
            rows_of(8),
            whole(source),
            rows_of(width),
            rows_of(width),
            by_pair,
            whole(w_proj),
            whole(gain_two),
        ],
        out_specs=[
            rows_of(width),
            by_pair,
            pl.BlockSpec((width // 2, width), lambda i: (0, 0)),
            pl.BlockSpec((width // 2, width), lambda i: (0, 0)),
            pl.BlockSpec((8, width), lambda i: (0, 0)),
        ],
        out_shape=[
            shape((rows, width), F32),
            shape((images, pairs, SEQ, PAIR), BF16),
            shape((width // 2, width), BF16),
            shape((width // 2, width), BF16),
            shape((8, width), F32),
        ],
        scratch_shapes=[pltpu.VMEM((chunk, width), BF16), pltpu.VMEM((width, width), F32)],
        compiler_params=params(True),
        cost_estimate=cost(14e9, 20e6),
        name="middle",
    )(columns, source, residual, cotangent, context, w_proj, gain_two)


def merge_heads(turned):
    first = jnp.concatenate([turned[:HEAD_DIM, :SPLIT], turned[:HEAD_DIM, 2 * SPLIT : SPLIT + SEQ]], axis=1)
    second = jnp.concatenate([turned[HEAD_DIM:, SPLIT : 2 * SPLIT], turned[HEAD_DIM:, SPLIT + SEQ :]], axis=1)
    return jnp.concatenate([first, second], axis=0).T


def attend_back_kernel(
    chunk,
    grad_context,
    queries,
    keys,
    values,
    weights,
    inverse,
    context,
    normed_one,
    grad_out,
    kept,
    sent,
    value_side,
    grad_scores,
):
    pair = pl.program_id(0)
    image = pl.program_id(1)

    @pl.when((pair == 0) & (image == 0))
    def _():
        is_first, lane = key_sides()
        taken = (is_first & (lane < 2)) | (jnp.logical_not(is_first) & (lane >= 2) & (lane < 4))
        value_side[:, PAIR:] = jnp.where(taken, -1.0, 0.0).astype(BF16)

    key_side = split_heads(keys[0, 0])
    value_side[:, :PAIR] = split_heads(values[0, 0])
    lane = lax.broadcasted_iota(jnp.int32, (chunk, PAIR), 1)
    low = lane < HEAD_DIM
    scaled = []
    for at in range(0, SEQ, chunk):
        rows = slice(at, at + chunk)
        grads = (grad_context[0, 0, rows].astype(F32) * inverse[0, 0, rows]).astype(BF16)
        scaled.append(grads)
        product = grads.astype(F32) * context[0, 0, rows].astype(F32)
        first = jnp.sum(jnp.where(low, product, 0.0), axis=1, keepdims=True)
        second = jnp.sum(jnp.where(low, 0.0, product), axis=1, keepdims=True)
        offset = jnp.where(lane < 2, first, second)
        high = offset.astype(BF16).astype(F32)
        extra = jnp.where(
            (lane == 0) | (lane == 2), high, jnp.where((lane == 1) | (lane == 3), offset - high, 0.0)
        ).astype(BF16)
        grad_weights = dot_last(jnp.concatenate([grads, extra], axis=1), value_side[...])
        part = grad_weights.astype(BF16) * weights[0, 0, rows]
        grad_scores[rows] = part
        place = pl.ds(pl.multiple_of(image * SEQ + at, 32), chunk)
        grad_out[0, pair, place] = (dot(part, key_side) * HEAD_DIM**-0.5).astype(BF16)
    grads = jnp.concatenate(scaled, axis=0)
    place = pl.ds(pl.multiple_of(image * SEQ, 64), SEQ)
    grad_out[1, pair, place] = merge_heads(dot_first(queries[0, 0], grad_scores[...])).astype(BF16)
    grad_out[2, pair, place] = merge_heads(dot_first(grads, weights[0, 0])).astype(BF16)

    @pl.when((pair == pl.num_programs(0) - 1) & (image == pl.num_programs(1) - 1))
    def _():
        for kind in range(3):
            joined = jnp.concatenate([grad_out[kind, at] for at in range(grad_out.shape[1])], axis=1)
            span = joined.shape[1]
            columns = slice(kind * span, (kind + 1) * span)
            total = dot_first(normed_one[...], joined).astype(BF16)
            split_rows(total, kept.at[:, columns], sent.at[:, columns])


def attend_back(grad_context, qkv, weights, inverse, context, normed_one, first, count):
    images, pairs = context.shape[:2]
    rows, width = normed_one.shape

    def block(offset):
        return pl.BlockSpec((1, 1, SEQ, PAIR), lambda p, i: (i, offset + p, 0, 0))

    return pl.pallas_call(
        functools.partial(attend_back_kernel, SEQ),
        grid=(count, images),
        in_specs=[
            block(first),
            block(first),
            block(pairs + first),
            block(2 * pairs + first),
            pl.BlockSpec((1, 1, SEQ, 2 * SEQ), lambda p, i: (i, first + p, 0, 0)),
            block(first),
            block(first),
            whole(normed_one),
        ],
        out_specs=[
            pl.BlockSpec((3, count, rows, PAIR), lambda p, i: (0, 0, 0, 0)),
            pl.BlockSpec((width // 2, 3 * count * PAIR), lambda p, i: (0, 0)),
            pl.BlockSpec((width // 2, 3 * count * PAIR), lambda p, i: (0, 0)),
        ],
        out_shape=[shape((3, count, rows, PAIR), BF16)] + [shape((width // 2, 3 * count * PAIR), BF16)] * 2,
        scratch_shapes=[pltpu.VMEM((2 * SEQ, 2 * PAIR), BF16), pltpu.VMEM((SEQ, 2 * SEQ), BF16)],
        compiler_params=params(),
        cost_estimate=cost(17e9 * (1 if first else 1), 20e6 * (1 if first else 1)),
        name="attend_back",
    )(grad_context, qkv, qkv, qkv, weights, inverse, context, normed_one)


def last_kernel(groups, sub, tokens, w_qkv, grad_residual, gain_one, *rest):
    grads = rest[:groups]
    out, vectors = rest[groups:]
    width = tokens.shape[1]

    @pl.when(pl.program_id(0) == 0)
    def _():
        vectors[...] = jnp.zeros_like(vectors)

    total = jnp.zeros(tokens.shape, F32)
    for kind in range(3):
        joined = jnp.concatenate(
            [grad[kind, at] for grad in grads for at in range(grad.shape[1])], axis=1
        )
        total += dot_last(joined, w_qkv[:, kind * width : (kind + 1) * width])
        if kind == 0:
            vectors[2:3] += column_sum(joined.astype(F32))
        if kind == 2:
            vectors[3:4] += column_sum(joined.astype(F32))
    out[...] = total
    gain = as_row(gain_one)
    for at in range(0, tokens.shape[0], sub):
        rows = slice(at, at + sub)
        grad_normed = out[rows, :]
        unit, inverse = standardize(tokens[rows, :].astype(F32))
        out[rows, :] = grad_residual[rows, :] + standardize_back(grad_normed, gain, unit, inverse)
        vectors[0:1] += column_sum(grad_normed * unit)
        vectors[1:2] += column_sum(grad_normed)


def last(tokens, grads, w_qkv, grad_residual, gain_one, chunk=288):
    rows, width = tokens.shape
    block = pl.BlockSpec((chunk, width), lambda i: (i, 0))
    return pl.pallas_call(
        functools.partial(last_kernel, len(grads), 32),
        grid=(rows // chunk,),
        in_specs=[block, whole(w_qkv), block, whole(gain_one)]
        + [pl.BlockSpec((3, grad.shape[1], chunk, PAIR), lambda i: (0, 0, i, 0)) for grad in grads],
        out_specs=[block, pl.BlockSpec((8, width), lambda i: (0, 0))],
        out_shape=[shape((rows, width), F32), shape((8, width), F32)],
        compiler_params=params(),
        cost_estimate=cost(10e9, 15e6),
        name="last",
    )(tokens, w_qkv, grad_residual, gain_one, *grads)


def fold_kernel(count, *refs):
    inputs, outs = refs[: 2 * count], refs[2 * count :]
    at = lax.axis_index("exp") >> 1
    rows = outs[0].shape[0]
    for other, out in enumerate(outs):
        here = pl.ds(pl.multiple_of((at ^ other) * rows, rows), rows)
        column = 0
        for kept, received in zip(inputs[:count], inputs[count:]):
            span = slice(column, column + kept.shape[1])
            out[:, span] = (kept[here, :].astype(F32) + received[here, :].astype(F32)).astype(BF16)
            column = span.stop


def fold(kept, received, chips):
    rows = kept[0].shape[0] // chips
    width = sum(part.shape[1] for part in kept)
    return pl.pallas_call(
        functools.partial(fold_kernel, len(kept)),
        out_shape=[shape((rows, width), BF16)] * chips,
        compiler_params=params(),
        cost_estimate=cost(1e9, 10e6),
        name="fold",
    )(*kept, *received)


def finish_kernel(left, where, *refs):
    inputs, (proj_out, out) = refs[:-2], refs[-2:]
    width = proj_out.shape[1]
    right = width - left
    for step, part in enumerate(inputs):

        @pl.when(pl.program_id(0) == step)
        def _():
            proj_out[...] = part[:, :width].astype(F32)
            for kind in range(3):
                to = kind * width
                at = width + kind * left
                out[:, to : to + left] = part[:, at : at + left].astype(F32)
                at = width + 3 * left + kind * right
                out[:, to + left : to + width] = part[:, at : at + right].astype(F32)


def finish(parts, where, left):
    steps = len(parts)
    rows = parts[0].shape[0]
    width = parts[0].shape[1] // 4

    def landing(columns):
        return pl.BlockSpec((rows, columns), lambda i, at: (at[i], 0))

    return pl.pallas_call(
        functools.partial(finish_kernel, left),
        grid_spec=pltpu.PrefetchScalarGridSpec(
            num_scalar_prefetch=1,
            grid=(steps,),
            in_specs=[pl.BlockSpec(part.shape, lambda i, at: (0, 0)) for part in parts],
            out_specs=[landing(width), landing(3 * width)],
        ),
        out_shape=[shape((rows * steps, width), F32), shape((rows * steps, 3 * width), F32)],
        compiler_params=params(),
        cost_estimate=cost(1e9, 10e6),
        name="finish",
    )(where, *parts)


def combine_kernel(columns, source, residual, out):
    hits = token_hits(columns, source.shape[0])
    out[...] = (residual[...] + dot(hits, source[...])).astype(BF16)


def combine(columns, source, residual, chunk=288):
    rows, width = residual.shape
    return pl.pallas_call(
        combine_kernel,
        grid=(rows // chunk,),
        in_specs=[
            pl.BlockSpec((chunk, 8), lambda i: (i, 0)),
            whole(source),
            pl.BlockSpec((chunk, width), lambda i: (i, 0)),
        ],
        out_specs=pl.BlockSpec((chunk, width), lambda i: (i, 0)),
        out_shape=shape((rows, width), BF16),
        compiler_params=params(),
        cost_estimate=cost(6e9, 10e6),
        name="combine",
    )(columns, source, residual)


def exchange(rows, experts):
    blocks = rows.reshape(experts, rows.shape[0] // experts, rows.shape[1])
    return lax.all_to_all(blocks, "exp", split_axis=0, concat_axis=0, tiled=True).reshape(rows.shape)


def share(block, name, size):
    copies = jnp.broadcast_to(block[None], (size,) + block.shape)
    return lax.all_to_all(copies, name, split_axis=0, concat_axis=0, tiled=True)


def sum_blocks(blocks, kind):
    return jnp.sum(blocks.astype(F32), axis=0).astype(kind)


def scatter_reps(blocks):
    rows = blocks.reshape((-1,) + blocks.shape[2:])
    return lax.psum_scatter(rows, "rep", scatter_dimension=0, tiled=True)


def swap(block, name, bits, size):
    return lax.ppermute(block, name, [(at, at ^ bits) for at in range(size)])


def chip_scatter(kept, sent, sizes):
    size = sizes["exp"]
    chips = size // 2
    received = [swap(part, "exp", 1, size) for part in sent]
    parts = fold(kept, received, chips)
    return parts


def plane_sum(parts, sizes, after=()):
    size = sizes["exp"]
    chips = size // 2
    received = [swap(parts[other], "exp", 2 * other, size) for other in range(1, chips)]
    total = tie(parts[0], *after).astype(F32)
    for part in received:
        total += part.astype(F32)
    return total.astype(BF16)


def rep_sum(block, sizes):
    reps = sizes["rep"]
    blocks = block.reshape((reps, -1) + block.shape[1:])
    at = lax.convert_element_type(lax.axis_index("rep"), jnp.uint32)

    def pick(other):
        return lax.dynamic_index_in_dim(blocks, at ^ jnp.uint32(other), 0, keepdims=False)

    received = [swap(pick(other), "rep", other, reps) for other in range(1, reps)]
    total = pick(0).astype(F32)
    for part in received:
        total += part.astype(F32)
    return total.astype(BF16)


def rep_gather(block, sizes):
    reps = sizes["rep"]
    at = lax.axis_index("rep")
    parts = [block] + [swap(block, "rep", other, reps) for other in range(1, reps)]
    rows = []
    for slot in range(reps):
        chosen = parts[0]
        for other in range(1, reps):
            chosen = jnp.where((at ^ other) == slot, parts[other], chosen)
        rows.append(chosen)
    return jnp.concatenate(rows, axis=0)


def plane_gather(block, sizes):
    size = sizes["exp"]
    mine = [block] + [swap(block, "exp", 2 * other, size) for other in range(1, size // 2)]
    return mine + [swap(part, "exp", 1, size) for part in mine]


def join_halves(kept, sent):
    first = (lax.axis_index("exp") & 1) == 0
    return jnp.where(first, jnp.concatenate([kept, sent]), jnp.concatenate([sent, kept]))


def small_sums(vectors_two, vectors_one, router_grad):
    blank = jnp.zeros_like(vectors_one[:1])
    return jnp.concatenate([vectors_two[:3], vectors_one[:4], blank, router_grad], axis=0)


def tie(value, *after):
    return lax.optimization_barrier((value,) + after)[0]


def on_device(
    sizes,
    tokens,
    cotangent,
    expert_ids,
    expert_slots,
    w_qkv,
    q_bias,
    v_bias,
    w_proj,
    proj_bias,
    gain_one,
    shift_one,
    gain_two,
    shift_two,
    w_router,
    expert_in,
    expert_in_bias,
    expert_out,
    expert_out_bias,
):
    row_count, width = tokens.shape
    experts = w_router.shape[1]
    slot_count = row_count // experts
    reps = sizes["rep"]
    ids = expert_ids.T
    slots = expert_slots.T
    router_turned = w_router.T
    weight_in = expert_in[0]
    weight_out = expert_out[0]
    bias_in = expert_in_bias.astype(F32)
    bias_out = expert_out_bias.astype(F32)

    cot_arrived = exchange(gather(ids, slots, cotangent, slot_count), experts)
    normed_one, qkv, weights, inverse, context, residual, dispatched = front(
        tokens,
        w_qkv,
        jnp.concatenate([q_bias, v_bias, proj_bias]).astype(F32),
        w_proj,
        gain_one,
        shift_one,
        gain_two,
        shift_two,
        ids,
        slots,
        slot_count,
    )
    arrived = exchange(dispatched, experts)
    raw, columns, cot_turned, along = raw_active(ids, slots, cot_arrived, weight_out, bias_out, slot_count)
    active, grad_hidden, out_grad, gate, logits_grad = expert(
        arrived, cot_turned, weight_in, bias_in, raw, along, router_turned, reps
    )
    grad_eout = scatter_reps(out_grad)
    back, router_grad = expert_back(grad_hidden, weight_in, gate, logits_grad, router_turned, arrived)
    source = exchange(back, experts)
    made, out_bias_grad = produce(gate, active, cot_arrived, weight_out, bias_out)
    part = weight_in.shape[1] // reps
    out_part = width // reps
    early = early_rows(width)
    tail = jnp.pad(out_bias_grad.reshape(reps, 1, out_part), ((0, 0), (0, 0), (0, part - out_part)))
    in_first, in_second = weight_in_grad(arrived, gate, grad_hidden, tail, reps)
    source, made, in_first, in_second = lax.optimization_barrier((source, made, in_first, in_second))
    in_first = scatter_reps(in_first)
    returned = exchange(made, experts)
    grad_residual, grad_context, proj_kept, proj_sent, vectors_two = middle(
        columns, source, residual, cotangent, context, w_proj, gain_two
    )
    pairs = width // PAIR
    most = pairs // 2
    saved = (qkv, weights, inverse, context, normed_one)
    grads_a, kept_a, sent_a = attend_back(grad_context, *saved, 0, most)
    chips = sizes["exp"] // 2
    if (width // sizes["exp"]) % 16 == 0:
        sent_a, proj_sent, returned = lax.optimization_barrier((sent_a, proj_sent, returned))
        parts_a = chip_scatter((proj_kept, kept_a), (proj_sent, sent_a), sizes)
        grads_b, kept_b, sent_b = attend_back(
            tie(grad_context, grads_a, parts_a[0], grad_eout), *saved, most, pairs - most
        )
        sum_a = plane_sum(parts_a, sizes, (sent_b,))
        sum_a, sent_b = lax.optimization_barrier((sum_a, sent_b))
        parts_b = chip_scatter((kept_b,), (sent_b,), sizes)
        sum_b = plane_sum(parts_b, sizes)
        grad_tokens, vectors_one = last(
            tokens, (grads_a, grads_b), w_qkv, tie(grad_residual, parts_b[0]), gain_one
        )
        sum_a, sum_b, vectors_one, in_first = lax.optimization_barrier((sum_a, sum_b, vectors_one, in_first))
        block = jnp.concatenate([sum_a, sum_b], axis=1)
        small = small_sums(vectors_two, vectors_one, router_grad)
        small = sum_blocks(share(small, "exp", sizes["exp"]), F32)
        block = rep_sum(block, sizes)
        block, small, in_second = lax.optimization_barrier((block, small, in_second))
        in_second = scatter_reps(in_second)
        mixed = combine(columns, tie(returned, block), residual)
        block = rep_gather(block, sizes)
        block, mixed = lax.optimization_barrier((block, mixed))
        small = sum_blocks(share(small, "rep", reps), F32)
        parts = plane_gather(block, sizes)
        here = lax.axis_index("exp")
        order = jnp.arange(chips, dtype=jnp.int32) ^ (here >> 1)
        core = here & 1
        where = jnp.concatenate([core * chips + order, (1 - core) * chips + order]).astype(jnp.int32)
        grad_w_proj, grad_w_qkv = finish(parts, where, most * PAIR)
    else:
        in_second = scatter_reps(in_second)
        grads_b, kept_b, sent_b = attend_back(grad_context, *saved, most, pairs - most)
        mixed = combine(columns, returned, residual)
        grad_tokens, vectors_one = last(tokens, (grads_a, grads_b), w_qkv, grad_residual, gain_one)
        block = join_halves(
            jnp.concatenate([proj_kept, kept_a, kept_b], axis=1),
            jnp.concatenate([proj_sent, sent_a, sent_b], axis=1),
        )
        small = lax.psum(small_sums(vectors_two, vectors_one, router_grad), ("rep", "exp"))
        block = lax.psum(block, ("rep", "exp"))
        where = jnp.zeros((1,), jnp.int32)
        grad_w_proj, grad_w_qkv = finish((block,), where, most * PAIR)
    return (
        mixed,
        grad_tokens,
        grad_w_qkv,
        small[5],
        small[6],
        grad_w_proj,
        small[2],
        small[3],
        small[4],
        small[0],
        small[1],
        small[8 : 8 + experts].T,
        jnp.concatenate([in_first[:early], in_second], axis=0)[None].astype(F32),
        in_first[early : early + 1].astype(F32),
        turn(grad_eout)[None],
        in_first[early + 1 : early + 2, :out_part].astype(F32),
    )


def solution(mesh):
    rows = P(("rep", "exp"), None)
    placed = (rows,) * 4 + (P(),) * 10 + (
        P("exp", None, None),
        P("exp", None),
        P("exp", None, None),
        P("exp", None),
    )
    return jax.shard_map(
        functools.partial(on_device, dict(mesh.shape)),
        mesh=mesh,
        in_specs=placed,
        out_specs=(rows, rows)
        + (P(),) * 10
        + (P("exp", None, "rep"), P("exp", "rep"), P("exp", "rep", None), P("exp", "rep")),
        check_vma=False,
    )
```

```python
import functools

import jax
import jax.numpy as jnp
from jax import lax
from jax.experimental import pallas as pl
from jax.experimental.pallas import tpu as pltpu
from jax.sharding import PartitionSpec as P

HEAD_DIM = 64
SEQ = 576
PAIR = 2 * HEAD_DIM
SPLIT = 512
AUX = 128
EPSILON = 1e-06
F32 = jnp.float32
BF16 = jnp.bfloat16
VMEM_BYTES = 56 * 2**20


def dot(left, right):
    return lax.dot_general(left, right, (((1,), (0,)), ((), ())), preferred_element_type=F32)


def dot_last(left, right):
    return lax.dot_general(left, right, (((1,), (1,)), ((), ())), preferred_element_type=F32)


def dot_first(left, right):
    return lax.dot_general(left, right, (((0,), (0,)), ((), ())), preferred_element_type=F32)


def thirds(value):
    high = value.astype(BF16)
    rest = value - high.astype(F32)
    middle = rest.astype(BF16)
    return high, middle, (rest - middle.astype(F32)).astype(BF16)


def standardize(field):
    centred = field - jnp.mean(field, axis=-1, keepdims=True)
    inverse = lax.rsqrt(jnp.mean(centred * centred, axis=-1, keepdims=True) + EPSILON)
    return centred * inverse, inverse


def standardize_back(grad, gain, unit, inverse):
    scaled = grad * gain
    along = jnp.mean(scaled * unit, axis=-1, keepdims=True)
    return inverse * (scaled - jnp.mean(scaled, axis=-1, keepdims=True) - unit * along)


def as_row(ref):
    return ref[...].astype(F32).reshape(1, -1)


def column_sum(field):
    return jnp.sum(field, axis=0, keepdims=True)


def params(most=False):
    return pltpu.CompilerParams(vmem_limit_bytes=63 * 2**20 if most else VMEM_BYTES)


SCALE = 0.01
EARLY = 20
EXPERT_CHUNK = 768
EXPERT_ROWS = 576


def cost(flops, bytes_moved):
    return pl.CostEstimate(flops=int(flops * SCALE), transcendentals=0, bytes_accessed=int(bytes_moved * SCALE))


def whole(array):
    return pl.BlockSpec(array.shape, lambda *ids: (0,) * array.ndim)


def shape(dims, kind):
    return jax.ShapeDtypeStruct(dims, kind)


def split_heads(pair):
    lane = lax.broadcasted_iota(jnp.int32, pair.shape, 1)
    zero = jnp.zeros_like(pair)
    first = jnp.where(lane < HEAD_DIM, pair, zero)
    second = jnp.where(lane < HEAD_DIM, zero, pair)
    return jnp.concatenate([first[:SPLIT], second[:SPLIT], first[SPLIT:], second[SPLIT:]], axis=0)


def key_sides():
    row = lax.broadcasted_iota(jnp.int32, (2 * SEQ, PAIR), 0)
    lane = lax.broadcasted_iota(jnp.int32, (2 * SEQ, PAIR), 1)
    is_first = (row < SPLIT) | ((row >= 2 * SPLIT) & (row < SPLIT + SEQ))
    return is_first, lane


def columns_of(ids, slots, slot_count):
    return jnp.where(slots[...] >= 0, ids[...] * slot_count + slots[...], -1)


def slot_hits(columns, at, count):
    slot = at + lax.broadcasted_iota(jnp.int32, (count, columns.shape[1]), 0)
    hit = (columns[0:1, :] == slot) | (columns[1:2, :] == slot)
    return jnp.where(hit, 1.0, 0.0).astype(BF16)


def front_kernel(
    chunk,
    slot_count,
    tokens,
    w_qkv_hbm,
    biases,
    w_proj_hbm,
    gain_one,
    shift_one,
    gain_two,
    shift_two,
    ids,
    slots,
    normed_one_out,
    qkv_out,
    weights_out,
    inverse_out,
    context_out,
    residual_out,
    dispatched_out,
    value_side,
    normed_two,
    w_qkv,
    w_proj,
    normed_one,
    qkv,
    residual_held,
    arrivals,
    departures,
):
    image = pl.program_id(0)
    pair = pl.program_id(1)
    pairs = context_out.shape[1]
    here = pl.ds(pl.multiple_of(image * SEQ, SEQ), SEQ)
    load_qkv = pltpu.make_async_copy(w_qkv_hbm, w_qkv, arrivals.at[0])
    load_proj = pltpu.make_async_copy(w_proj_hbm, w_proj, arrivals.at[1])
    save_normed = pltpu.make_async_copy(normed_one, normed_one_out.at[here], departures.at[0])
    save_qkv = pltpu.make_async_copy(qkv, qkv_out.at[image], departures.at[1])
    save_residual = pltpu.make_async_copy(residual_held, residual_out.at[here], departures.at[2])

    @pl.when((image == 0) & (pair == 0))
    def _():
        load_qkv.start()
        load_proj.start()
        is_first, lane = key_sides()
        value_side[:, PAIR:] = jnp.where(is_first == (lane < HEAD_DIM), 1.0, 0.0).astype(BF16)

    @pl.when(pair == 0)
    def _():
        unit, _ = standardize(tokens[...].astype(F32))
        normed_one[...] = (unit * as_row(gain_one) + as_row(shift_one)).astype(BF16)

    @pl.when((image == 0) & (pair == 0))
    def _():
        load_qkv.wait()

    @pl.when(pair == 0)
    def _():
        normed = normed_one[...]
        width = w_qkv.shape[1]
        third = width // 3
        step = 2 * PAIR
        for at in range(0, width, step):
            part = dot(normed, w_qkv[:, at : at + step])
            if at < third:
                part = part + as_row(biases)[:, at : at + step]
            if at >= 2 * third:
                part = part + as_row(biases)[:, at - third : at - third + step]
            part = part.astype(BF16)
            if at < third:
                part = part * jnp.asarray(HEAD_DIM**-0.5, BF16)
            qkv[at // PAIR] = part[:, :PAIR]
            qkv[at // PAIR + 1] = part[:, PAIR:]
        save_normed.start()
        save_qkv.start()

    keys = split_heads(qkv[pairs + pair])
    value_side[:, :PAIR] = split_heads(qkv[2 * pairs + pair])
    values = value_side[...]
    low = lax.broadcasted_iota(jnp.int32, (chunk, PAIR), 1) < HEAD_DIM

    def soften(scores):
        first = scores[:, :SPLIT]
        second = scores[:, SPLIT : 2 * SPLIT]
        tail = scores[:, 2 * SPLIT :]
        first_max = jnp.maximum(
            jnp.max(first, axis=1, keepdims=True),
            jnp.max(jnp.where(low, tail, -jnp.inf), axis=1, keepdims=True),
        )
        second_max = jnp.maximum(
            jnp.max(second, axis=1, keepdims=True),
            jnp.max(jnp.where(low, -jnp.inf, tail), axis=1, keepdims=True),
        )
        return jnp.concatenate(
            [
                jnp.exp(first - first_max).astype(BF16),
                jnp.exp(second - second_max).astype(BF16),
                jnp.exp(tail - jnp.where(low, first_max, second_max)).astype(BF16),
            ],
            axis=1,
        )

    def settle(rows, exponent):
        summed = dot(exponent, values)
        inverse = 1.0 / summed[:, PAIR:]
        inverse_out[0, 0, rows] = inverse
        context_out[0, pair, rows] = (summed[:, :PAIR] * inverse).astype(BF16)

    spans = [slice(at, at + chunk) for at in range(0, SEQ, chunk)]
    coming = dot_last(qkv[pair, spans[0]], keys)
    waiting = None
    for at, rows in enumerate(spans):
        scores = coming
        if at + 1 < len(spans):
            coming = dot_last(qkv[pair, spans[at + 1]], keys)
        if waiting is not None:
            settle(*waiting)
        exponent = soften(scores)
        weights_out[0, 0, rows] = exponent
        waiting = (rows, exponent)
    settle(*waiting)

    @pl.when((image == 0) & (pair == pairs - 1))
    def _():
        load_proj.wait()

    @pl.when((image > 0) & (pair == pairs - 1))
    def _():
        before = pl.ds(pl.multiple_of((image - 1) * SEQ, SEQ), SEQ)
        pltpu.make_async_copy(residual_held, residual_out.at[before], departures.at[2]).wait()

    @pl.when(pair == pairs - 1)
    def _():
        context = jnp.concatenate([context_out[0, at] for at in range(pairs)], axis=1)
        offset = as_row(biases)[:, 2 * tokens.shape[1] :]
        residual = tokens[...].astype(F32) + (dot(context, w_proj[...]) + offset)
        residual_held[...] = residual
        save_residual.start()
        unit, _ = standardize(residual)
        normed = (unit * as_row(gain_two) + as_row(shift_two)).astype(BF16)
        normed_two[here] = normed
        save_normed.wait()
        save_qkv.wait()

    @pl.when((pair == pairs - 1) & (image == pl.num_programs(0) - 1))
    def _():
        columns = columns_of(ids, slots, slot_count)
        part = SEQ // 2
        for at in range(0, dispatched_out.shape[0], part):
            hits = slot_hits(columns, at, part)
            dispatched_out[at : at + part] = dot(hits, normed_two[...]).astype(BF16)
        save_residual.wait()


def front(tokens, w_qkv, biases, w_proj, gain_one, shift_one, gain_two, shift_two, ids, slots, slot_count):
    rows, width = tokens.shape
    images = rows // SEQ
    pairs = width // PAIR

    def per_image(columns):
        return pl.BlockSpec((SEQ, columns), lambda i, p: (i, 0))

    anywhere = pl.BlockSpec(memory_space=pl.ANY)
    fixed = (gain_one, shift_one, gain_two, shift_two, ids, slots)
    return pl.pallas_call(
        functools.partial(front_kernel, SEQ // 2, slot_count),
        grid=(images, pairs),
        in_specs=[per_image(width), anywhere, whole(biases), anywhere] + [whole(array) for array in fixed],
        out_specs=[
            anywhere,
            anywhere,
            pl.BlockSpec((1, 1, SEQ, 2 * SEQ), lambda i, p: (i, p, 0, 0)),
            pl.BlockSpec((1, 1, SEQ, PAIR), lambda i, p: (i, p, 0, 0)),
            pl.BlockSpec((1, pairs, SEQ, PAIR), lambda i, p: (i, 0, 0, 0)),
            anywhere,
            pl.BlockSpec((rows, width), lambda i, p: (0, 0)),
        ],
        out_shape=[
            shape((rows, width), BF16),
            shape((images, 3 * pairs, SEQ, PAIR), BF16),
            shape((images, pairs, SEQ, 2 * SEQ), BF16),
            shape((images, pairs, SEQ, PAIR), F32),
            shape((images, pairs, SEQ, PAIR), BF16),
            shape((rows, width), F32),
            shape((rows, width), BF16),
        ],
        scratch_shapes=[
            pltpu.VMEM((2 * SEQ, 2 * PAIR), BF16),
            pltpu.VMEM((rows, width), BF16),
            pltpu.VMEM(w_qkv.shape, BF16),
            pltpu.VMEM(w_proj.shape, BF16),
            pltpu.VMEM((SEQ, width), BF16),
            pltpu.VMEM((3 * pairs, SEQ, PAIR), BF16),
            pltpu.VMEM((SEQ, width), F32),
            pltpu.SemaphoreType.DMA((2,)),
            pltpu.SemaphoreType.DMA((3,)),
        ],
        compiler_params=params(True),
        cost_estimate=cost(30e9, 60e6),
        name="front",
    )(tokens, w_qkv, biases, w_proj, *fixed)


def gather_kernel(chunk, slot_count, ids, slots, rows, out):
    columns = columns_of(ids, slots, slot_count)
    for at in range(0, rows.shape[0], chunk):
        out[at : at + chunk] = dot(slot_hits(columns, at, chunk), rows[...]).astype(BF16)


def gather(ids, slots, rows, slot_count, chunk=288):
    return pl.pallas_call(
        functools.partial(gather_kernel, chunk, slot_count),
        out_shape=shape(rows.shape, BF16),
        compiler_params=params(True),
        cost_estimate=cost(4e9, 8e6),
        name="gather",
    )(ids, slots, rows)


def raw_kernel(slot_count, ids, slots, cotangent, weight_out, bias_out, out, columns_out, turned, along):
    @pl.when(pl.program_id(0) == 0)
    def _():
        columns = columns_of(ids, slots, slot_count)
        pad = jnp.full((6, columns.shape[1]), -1, jnp.int32)
        columns_out[...] = jnp.concatenate([columns, pad], axis=0).T
        turned[...] = cotangent[...].T
        for at in range(0, along.shape[0], 32):
            rows = slice(at, at + 32)
            along[rows, :] = lane_sums(cotangent[rows, :].astype(F32) * bias_out[...])

    out[...] = dot_last(cotangent[...], weight_out[...]).astype(BF16)


def raw_active(ids, slots, cotangent, weight_out, bias_out, slot_count, chunk=768):
    count, width = cotangent.shape
    hidden = weight_out.shape[0]
    return pl.pallas_call(
        functools.partial(raw_kernel, slot_count),
        grid=(hidden // chunk,),
        in_specs=[
            whole(ids),
            whole(slots),
            whole(cotangent),
            pl.BlockSpec((chunk, width), lambda i: (i, 0)),
            whole(bias_out),
        ],
        out_specs=[
            pl.BlockSpec((count, chunk), lambda i: (0, i)),
            pl.BlockSpec((count, 8), lambda i: (0, 0)),
            pl.BlockSpec((width, count), lambda i: (0, 0)),
            pl.BlockSpec((count, AUX), lambda i: (0, 0)),
        ],
        out_shape=[
            shape((count, hidden), BF16),
            shape((count, 8), jnp.int32),
            shape((width, count), BF16),
            shape((count, AUX), F32),
        ],
        compiler_params=params(True),
        cost_estimate=cost(9e9, 14e6),
        name="raw_active",
    )(ids, slots, cotangent, weight_out, bias_out)


def joined_thirds(value, order):
    parts = thirds(value)
    return jnp.concatenate([parts[at] for at in order], axis=1)


LEFT = (0, 0, 1, 1, 0, 2)
RIGHT = (0, 1, 0, 1, 2, 0)


def expert_kernel(
    row_chunk,
    arrived,
    cot_turned,
    weight_in,
    bias_in,
    raw,
    along,
    w_router,
    active_out,
    hidden_out,
    weight_grad,
    gate_out,
    logits_grad,
    produced_grad,
    gate_total,
    router,
):
    step = pl.program_id(0)
    count = arrived.shape[0]
    experts = w_router.shape[0]

    @pl.when(step == 0)
    def _():
        parts = dot_last(arrived[...], jnp.concatenate(thirds(w_router[...]), axis=0))
        logits = parts[:, :experts] + (parts[:, experts : 2 * experts] + parts[:, 2 * experts :])
        exponent = jnp.exp(logits - jnp.max(logits, axis=1, keepdims=True))
        probs = exponent / jnp.sum(exponent, axis=1, keepdims=True)
        router[...] = probs
        own = lax.broadcasted_iota(jnp.int32, (count, experts), 1) == lax.axis_index("exp")
        gate = jnp.sum(jnp.where(own, probs, 0.0), axis=1, keepdims=True)
        gate_out[...] = jnp.broadcast_to(gate, gate_out.shape)
        gate_row = gate_out[...].T[0:1]
        produced_grad[...] = (cot_turned[...].astype(F32) * gate_row).astype(BF16)
        gate_total[...] = along[...]

    for at in range(0, count, row_chunk):
        rows = slice(at, at + row_chunk)
        hidden = dot(arrived[rows, :], weight_in[...]) + bias_in[...]
        scaled = hidden * (0.5**0.5)
        curve = lax.erf(scaled)
        cdf = 0.5 + 0.5 * curve
        active = (hidden * cdf).astype(BF16)
        bell = jnp.exp(scaled * -scaled) * (0.5 * 1.1283791670955126 * 0.5**0.5)
        slope = (cdf + hidden * bell).astype(BF16)
        incoming = raw[rows, :]
        active_out[rows, :] = active
        hidden_out[rows, :] = incoming * slope
        gate_total[rows, :] += lane_sums((incoming * active).astype(F32))
    weight_grad[0] = dot(produced_grad[...], active_out[...]).astype(BF16)

    @pl.when(step == pl.num_programs(0) - 1)
    def _():
        own = lax.broadcasted_iota(jnp.int32, (count, experts), 1) == lax.axis_index("exp")
        scale = jnp.sum(gate_total[...], axis=1, keepdims=True) * gate_out[:, 0:1]
        logits_grad[...] = scale * (jnp.where(own, 1.0, 0.0) - router[...])


def lane_sums(field):
    total = field[:, :AUX]
    for at in range(AUX, field.shape[1], AUX):
        total = total + field[:, at : at + AUX]
    return total


def expert(arrived, cot_turned, weight_in, bias_in, raw, along, w_router, reps, chunk=EXPERT_CHUNK):
    count, width = arrived.shape
    hidden = weight_in.shape[1]
    experts = w_router.shape[0]
    part = hidden // reps
    cuts = part // chunk

    def column_block(rows):
        return pl.BlockSpec((rows, chunk), lambda i: (0, i))

    def fixed(rows, columns):
        return pl.BlockSpec((rows, columns), lambda i: (0, 0))

    return pl.pallas_call(
        functools.partial(expert_kernel, EXPERT_ROWS),
        grid=(hidden // chunk,),
        in_specs=[
            whole(arrived),
            whole(cot_turned),
            column_block(width),
            column_block(1),
            column_block(count),
            whole(along),
            whole(w_router),
        ],
        out_specs=[
            column_block(count),
            column_block(count),
            pl.BlockSpec((1, width, chunk), lambda i: (i // cuts, 0, i % cuts)),
            fixed(count, AUX),
            fixed(count, experts),
        ],
        out_shape=[
            shape((count, hidden), BF16),
            shape((count, hidden), BF16),
            shape((reps, width, part), BF16),
            shape((count, AUX), F32),
            shape((count, experts), F32),
        ],
        scratch_shapes=[
            pltpu.VMEM((width, count), BF16),
            pltpu.VMEM((count, AUX), F32),
            pltpu.VMEM((count, experts), F32),
        ],
        compiler_params=params(True),
        cost_estimate=cost(24e9, 35e6),
        name="expert",
    )(arrived, cot_turned, weight_in, bias_in, raw, along, w_router)


def expert_back_kernel(grad_hidden, weight_in, gate, logits_grad, w_router, out):
    right = jnp.concatenate([thirds(w_router[...])[at] for at in RIGHT], axis=0)
    total = gate[:, 0:1] * dot_last(grad_hidden[...], weight_in[...])
    total += dot(joined_thirds(logits_grad[...], LEFT), right)
    out[...] = total.astype(BF16)


def expert_back(grad_hidden, weight_in, gate, logits_grad, w_router, chunk=288):
    count, hidden = grad_hidden.shape
    experts, width = w_router.shape

    def rows(columns):
        return pl.BlockSpec((chunk, columns), lambda i: (i, 0))

    return pl.pallas_call(
        expert_back_kernel,
        grid=(count // chunk,),
        in_specs=[rows(hidden), whole(weight_in), rows(AUX), rows(experts), whole(w_router)],
        out_specs=rows(width),
        out_shape=shape((count, width), BF16),
        compiler_params=params(True),
        cost_estimate=cost(12e9, 15e6),
        name="expert_back",
    )(grad_hidden, weight_in, gate, logits_grad, w_router)


def turn_kernel(field, out):
    out[...] = field[...].T.astype(F32)


def turn(field):
    return pl.pallas_call(
        turn_kernel,
        out_shape=shape(field.shape[::-1], F32),
        compiler_params=params(),
        cost_estimate=cost(1e9, 5e6),
        name="turn",
    )(field)


def early_rows(width):
    return width // 48 * EARLY


def weight_in_kernel(arrived, gate, grad_hidden, out_bias_grad, logits_grad, first, second, router_grad, turned):
    width = arrived.shape[1]
    experts = logits_grad.shape[1]
    half = first.shape[1] - 16

    @pl.when(pl.program_id(0) == 0)
    def _():
        for at in range(0, arrived.shape[0], 128):
            rows = slice(at, at + 128)
            turned[:width, rows] = (arrived[rows, :].astype(F32) * gate[rows, 0:1]).astype(BF16).T
        gate_row = jnp.broadcast_to(gate[...].T[0:1], (16, arrived.shape[0]))
        high = gate_row.astype(BF16)
        row = lax.broadcasted_iota(jnp.int32, high.shape, 0)
        low = (gate_row - high.astype(F32)).astype(BF16)
        turned[width:] = jnp.where(row == 0, high, jnp.where(row == 1, low, jnp.zeros_like(low)))
        parts = dot_first(joined_thirds(logits_grad[...], (0, 1, 2)), arrived[...])
        router_grad[...] = parts[:experts] + parts[experts : 2 * experts] + parts[2 * experts :]

    total = dot(turned[...], grad_hidden[...])
    second[0] = total[half:width].astype(BF16)
    first[0, :half] = total[:half].astype(BF16)
    row = lax.broadcasted_iota(jnp.int32, (first.shape[1] - half, first.shape[2]), 0)
    bias_grad = total[width : width + 1] + total[width + 1 : width + 2]
    first[0, half:] = jnp.where(row == 0, bias_grad, jnp.where(row == 1, out_bias_grad[0], 0.0)).astype(BF16)


def weight_in_grad(arrived, gate, grad_hidden, out_bias_grad, logits_grad, reps):
    count, hidden = grad_hidden.shape
    width = arrived.shape[1]
    early = early_rows(width)
    part = hidden // reps
    return pl.pallas_call(
        weight_in_kernel,
        grid=(reps,),
        in_specs=[
            whole(arrived),
            whole(gate),
            pl.BlockSpec((count, part), lambda i: (0, i)),
            pl.BlockSpec((1, 1, part), lambda i: (i, 0, 0)),
            whole(logits_grad),
        ],
        out_specs=[
            pl.BlockSpec((1, early + 16, part), lambda i: (i, 0, 0)),
            pl.BlockSpec((1, width - early, part), lambda i: (i, 0, 0)),
            pl.BlockSpec((logits_grad.shape[1], width), lambda i: (0, 0)),
        ],
        out_shape=[
            shape((reps, early + 16, part), BF16),
            shape((reps, width - early, part), BF16),
            shape((logits_grad.shape[1], width), F32),
        ],
        scratch_shapes=[pltpu.VMEM((width + 16, count), BF16)],
        compiler_params=params(True),
        cost_estimate=cost(10e9, 15e6),
        name="weight_in_grad",
    )(arrived, gate, grad_hidden, out_bias_grad, logits_grad)


def produce_kernel(gate, active, cotangent, weight_out, bias_out, out, bias_grad):
    @pl.when(pl.program_id(0) == 0)
    def _():
        bias_grad[...] = jnp.zeros_like(bias_grad)

    bias_grad[...] += column_sum(gate[:, 0:1] * cotangent[...].astype(F32))
    out[...] = (gate[:, 0:1] * (dot(active[...], weight_out[...]) + bias_out[...])).astype(BF16)


def produce(gate, active, cotangent, weight_out, bias_out, chunk=288):
    count, hidden = active.shape
    width = weight_out.shape[1]

    def rows(columns):
        return pl.BlockSpec((chunk, columns), lambda i: (i, 0))

    return pl.pallas_call(
        produce_kernel,
        grid=(count // chunk,),
        in_specs=[rows(AUX), rows(hidden), rows(width), whole(weight_out), whole(bias_out)],
        out_specs=[rows(width), pl.BlockSpec((1, width), lambda i: (0, 0))],
        out_shape=[shape((count, width), BF16), shape((1, width), F32)],
        compiler_params=params(True),
        cost_estimate=cost(10e9, 15e6),
        name="produce",
    )(gate, active, cotangent, weight_out, bias_out)


def token_hits(columns, slots):
    slot = lax.broadcasted_iota(jnp.int32, (columns.shape[0], slots), 1)
    hit = (columns[:, 0:1] == slot) | (columns[:, 1:2] == slot)
    return jnp.where(hit, 1.0, 0.0).astype(BF16)


def split_rows(value, kept, sent):
    half = value.shape[0] // 2
    first = (lax.axis_index("exp") & 1) == 0
    low, high = value[:half], value[half:]
    kept[...] = jnp.where(first, low, high)
    sent[...] = jnp.where(first, high, low)


def middle_kernel(
    sub,
    columns,
    source,
    residual,
    cotangent,
    context,
    w_proj,
    gain_two,
    grad_residual_out,
    grad_context_out,
    proj_kept,
    proj_sent,
    vectors,
    branch,
    proj_total,
):
    step = pl.program_id(0)
    chunk = residual.shape[0]
    pairs = context.shape[1]

    @pl.when(step == 0)
    def _():
        vectors[...] = jnp.zeros_like(vectors)
        proj_total[...] = jnp.zeros_like(proj_total)

    hits = token_hits(columns, source.shape[0])
    grad_residual_out[...] = dot(hits, source[...])
    gain = as_row(gain_two)
    for at in range(0, chunk, sub):
        rows = slice(at, at + sub)
        grad_normed = grad_residual_out[rows, :]
        unit, inverse = standardize(residual[rows, :])
        grad_residual = cotangent[rows, :].astype(F32) + standardize_back(grad_normed, gain, unit, inverse)
        grad_residual_out[rows, :] = grad_residual
        rounded = grad_residual.astype(BF16)
        branch[rows, :] = rounded
        vectors[0:1] += column_sum(grad_normed * unit)
        vectors[1:2] += column_sum(grad_normed)
        vectors[2:3] += column_sum(rounded.astype(F32))
    grad_context = dot_last(branch[...], w_proj[...]).astype(BF16)
    for pair in range(pairs):
        grad_context_out[0, pair] = grad_context[:, pair * PAIR : (pair + 1) * PAIR]
    joined = jnp.concatenate([context[0, pair] for pair in range(pairs)], axis=1)
    proj_total[...] += dot_first(joined, branch[...])

    @pl.when(step == pl.num_programs(0) - 1)
    def _():
        split_rows(proj_total[...].astype(BF16), proj_kept, proj_sent)


def middle(columns, source, residual, cotangent, context, w_proj, gain_two, chunk=288):
    rows, width = residual.shape
    images, pairs = context.shape[:2]
    parts = SEQ // chunk

    def rows_of(columns):
        return pl.BlockSpec((chunk, columns), lambda i: (i, 0))

    by_pair = pl.BlockSpec((1, pairs, chunk, PAIR), lambda i: (i // parts, 0, i % parts, 0))
    return pl.pallas_call(
        functools.partial(middle_kernel, 32),
        grid=(rows // chunk,),
        in_specs=[
            rows_of(8),
            whole(source),
            rows_of(width),
            rows_of(width),
            by_pair,
            whole(w_proj),
            whole(gain_two),
        ],
        out_specs=[
            rows_of(width),
            by_pair,
            pl.BlockSpec((width // 2, width), lambda i: (0, 0)),
            pl.BlockSpec((width // 2, width), lambda i: (0, 0)),
            pl.BlockSpec((8, width), lambda i: (0, 0)),
        ],
        out_shape=[
            shape((rows, width), F32),
            shape((images, pairs, SEQ, PAIR), BF16),
            shape((width // 2, width), BF16),
            shape((width // 2, width), BF16),
            shape((8, width), F32),
        ],
        scratch_shapes=[pltpu.VMEM((chunk, width), BF16), pltpu.VMEM((width, width), F32)],
        compiler_params=params(True),
        cost_estimate=cost(14e9, 20e6),
        name="middle",
    )(columns, source, residual, cotangent, context, w_proj, gain_two)


def merge_heads(turned):
    first = jnp.concatenate([turned[:HEAD_DIM, :SPLIT], turned[:HEAD_DIM, 2 * SPLIT : SPLIT + SEQ]], axis=1)
    second = jnp.concatenate([turned[HEAD_DIM:, SPLIT : 2 * SPLIT], turned[HEAD_DIM:, SPLIT + SEQ :]], axis=1)
    return jnp.concatenate([first, second], axis=0).T


def attend_back_kernel(
    chunk,
    grad_context,
    queries,
    keys,
    values,
    weights,
    inverse,
    context,
    normed_one,
    grad_out,
    kept,
    sent,
    value_side,
    grad_scores,
):
    pair = pl.program_id(0)
    image = pl.program_id(1)

    @pl.when((pair == 0) & (image == 0))
    def _():
        is_first, lane = key_sides()
        taken = (is_first & (lane < 2)) | (jnp.logical_not(is_first) & (lane >= 2) & (lane < 4))
        value_side[:, PAIR:] = jnp.where(taken, -1.0, 0.0).astype(BF16)

    key_side = split_heads(keys[0, 0])
    value_side[:, :PAIR] = split_heads(values[0, 0])
    lane = lax.broadcasted_iota(jnp.int32, (chunk, PAIR), 1)
    low = lane < HEAD_DIM
    scaled = []
    for at in range(0, SEQ, chunk):
        rows = slice(at, at + chunk)
        grads = (grad_context[0, 0, rows].astype(F32) * inverse[0, 0, rows]).astype(BF16)
        scaled.append(grads)
        product = grads.astype(F32) * context[0, 0, rows].astype(F32)
        first = jnp.sum(jnp.where(low, product, 0.0), axis=1, keepdims=True)
        second = jnp.sum(jnp.where(low, 0.0, product), axis=1, keepdims=True)
        offset = jnp.where(lane < 2, first, second)
        high = offset.astype(BF16).astype(F32)
        extra = jnp.where(
            (lane == 0) | (lane == 2), high, jnp.where((lane == 1) | (lane == 3), offset - high, 0.0)
        ).astype(BF16)
        grad_weights = dot_last(jnp.concatenate([grads, extra], axis=1), value_side[...])
        part = grad_weights.astype(BF16) * weights[0, 0, rows]
        grad_scores[rows] = part
        place = pl.ds(pl.multiple_of(image * SEQ + at, 32), chunk)
        grad_out[0, pair, place] = (dot(part, key_side) * HEAD_DIM**-0.5).astype(BF16)
    grads = jnp.concatenate(scaled, axis=0)
    place = pl.ds(pl.multiple_of(image * SEQ, 64), SEQ)
    grad_out[1, pair, place] = merge_heads(dot_first(queries[0, 0], grad_scores[...])).astype(BF16)
    grad_out[2, pair, place] = merge_heads(dot_first(grads, weights[0, 0])).astype(BF16)

    @pl.when((pair == pl.num_programs(0) - 1) & (image == pl.num_programs(1) - 1))
    def _():
        for kind in range(3):
            joined = jnp.concatenate([grad_out[kind, at] for at in range(grad_out.shape[1])], axis=1)
            span = joined.shape[1]
            columns = slice(kind * span, (kind + 1) * span)
            total = dot_first(normed_one[...], joined).astype(BF16)
            split_rows(total, kept.at[:, columns], sent.at[:, columns])


def attend_back(grad_context, qkv, weights, inverse, context, normed_one, first, count):
    images, pairs = context.shape[:2]
    rows, width = normed_one.shape

    def block(offset):
        return pl.BlockSpec((1, 1, SEQ, PAIR), lambda p, i: (i, offset + p, 0, 0))

    return pl.pallas_call(
        functools.partial(attend_back_kernel, SEQ),
        grid=(count, images),
        in_specs=[
            block(first),
            block(first),
            block(pairs + first),
            block(2 * pairs + first),
            pl.BlockSpec((1, 1, SEQ, 2 * SEQ), lambda p, i: (i, first + p, 0, 0)),
            block(first),
            block(first),
            whole(normed_one),
        ],
        out_specs=[
            pl.BlockSpec((3, count, rows, PAIR), lambda p, i: (0, 0, 0, 0)),
            pl.BlockSpec((width // 2, 3 * count * PAIR), lambda p, i: (0, 0)),
            pl.BlockSpec((width // 2, 3 * count * PAIR), lambda p, i: (0, 0)),
        ],
        out_shape=[shape((3, count, rows, PAIR), BF16)] + [shape((width // 2, 3 * count * PAIR), BF16)] * 2,
        scratch_shapes=[pltpu.VMEM((2 * SEQ, 2 * PAIR), BF16), pltpu.VMEM((SEQ, 2 * SEQ), BF16)],
        compiler_params=params(),
        cost_estimate=cost(17e9 * (1 if first else 1), 20e6 * (1 if first else 1)),
        name="attend_back",
    )(grad_context, qkv, qkv, qkv, weights, inverse, context, normed_one)


def last_kernel(groups, sub, tokens, w_qkv, grad_residual, gain_one, *rest):
    grads = rest[:groups]
    out, vectors = rest[groups:]
    width = tokens.shape[1]

    @pl.when(pl.program_id(0) == 0)
    def _():
        vectors[...] = jnp.zeros_like(vectors)

    total = jnp.zeros(tokens.shape, F32)
    for kind in range(3):
        joined = jnp.concatenate(
            [grad[kind, at] for grad in grads for at in range(grad.shape[1])], axis=1
        )
        total += dot_last(joined, w_qkv[:, kind * width : (kind + 1) * width])
        if kind == 0:
            vectors[2:3] += column_sum(joined.astype(F32))
        if kind == 2:
            vectors[3:4] += column_sum(joined.astype(F32))
    out[...] = total
    gain = as_row(gain_one)
    for at in range(0, tokens.shape[0], sub):
        rows = slice(at, at + sub)
        grad_normed = out[rows, :]
        unit, inverse = standardize(tokens[rows, :].astype(F32))
        out[rows, :] = grad_residual[rows, :] + standardize_back(grad_normed, gain, unit, inverse)
        vectors[0:1] += column_sum(grad_normed * unit)
        vectors[1:2] += column_sum(grad_normed)


def last(tokens, grads, w_qkv, grad_residual, gain_one, chunk=288):
    rows, width = tokens.shape
    block = pl.BlockSpec((chunk, width), lambda i: (i, 0))
    return pl.pallas_call(
        functools.partial(last_kernel, len(grads), 32),
        grid=(rows // chunk,),
        in_specs=[block, whole(w_qkv), block, whole(gain_one)]
        + [pl.BlockSpec((3, grad.shape[1], chunk, PAIR), lambda i: (0, 0, i, 0)) for grad in grads],
        out_specs=[block, pl.BlockSpec((8, width), lambda i: (0, 0))],
        out_shape=[shape((rows, width), F32), shape((8, width), F32)],
        compiler_params=params(),
        cost_estimate=cost(10e9, 15e6),
        name="last",
    )(tokens, w_qkv, grad_residual, gain_one, *grads)


def fold_kernel(count, *refs):
    inputs, outs = refs[: 2 * count], refs[2 * count :]
    at = lax.axis_index("exp") >> 1
    rows = outs[0].shape[0]
    for other, out in enumerate(outs):
        here = pl.ds(pl.multiple_of((at ^ other) * rows, rows), rows)
        column = 0
        for kept, received in zip(inputs[:count], inputs[count:]):
            span = slice(column, column + kept.shape[1])
            out[:, span] = (kept[here, :].astype(F32) + received[here, :].astype(F32)).astype(BF16)
            column = span.stop


def fold(kept, received, chips):
    rows = kept[0].shape[0] // chips
    width = sum(part.shape[1] for part in kept)
    return pl.pallas_call(
        functools.partial(fold_kernel, len(kept)),
        out_shape=[shape((rows, width), BF16)] * chips,
        compiler_params=params(),
        cost_estimate=cost(1e9, 10e6),
        name="fold",
    )(*kept, *received)


def finish_kernel(left, where, *refs):
    inputs, (proj_out, out) = refs[:-2], refs[-2:]
    width = proj_out.shape[1]
    right = width - left
    for step, part in enumerate(inputs):

        @pl.when(pl.program_id(0) == step)
        def _():
            proj_out[...] = part[:, :width].astype(F32)
            for kind in range(3):
                to = kind * width
                at = width + kind * left
                out[:, to : to + left] = part[:, at : at + left].astype(F32)
                at = width + 3 * left + kind * right
                out[:, to + left : to + width] = part[:, at : at + right].astype(F32)


def finish(parts, where, left):
    steps = len(parts)
    rows = parts[0].shape[0]
    width = parts[0].shape[1] // 4

    def landing(columns):
        return pl.BlockSpec((rows, columns), lambda i, at: (at[i], 0))

    return pl.pallas_call(
        functools.partial(finish_kernel, left),
        grid_spec=pltpu.PrefetchScalarGridSpec(
            num_scalar_prefetch=1,
            grid=(steps,),
            in_specs=[pl.BlockSpec(part.shape, lambda i, at: (0, 0)) for part in parts],
            out_specs=[landing(width), landing(3 * width)],
        ),
        out_shape=[shape((rows * steps, width), F32), shape((rows * steps, 3 * width), F32)],
        compiler_params=params(),
        cost_estimate=cost(1e9, 10e6),
        name="finish",
    )(where, *parts)


def combine_kernel(columns, source, residual, out):
    hits = token_hits(columns, source.shape[0])
    out[...] = (residual[...] + dot(hits, source[...])).astype(BF16)


def combine(columns, source, residual, chunk=288):
    rows, width = residual.shape
    return pl.pallas_call(
        combine_kernel,
        grid=(rows // chunk,),
        in_specs=[
            pl.BlockSpec((chunk, 8), lambda i: (i, 0)),
            whole(source),
            pl.BlockSpec((chunk, width), lambda i: (i, 0)),
        ],
        out_specs=pl.BlockSpec((chunk, width), lambda i: (i, 0)),
        out_shape=shape((rows, width), BF16),
        compiler_params=params(),
        cost_estimate=cost(6e9, 10e6),
        name="combine",
    )(columns, source, residual)


def exchange(rows, experts):
    blocks = rows.reshape(experts, rows.shape[0] // experts, rows.shape[1])
    return lax.all_to_all(blocks, "exp", split_axis=0, concat_axis=0, tiled=True).reshape(rows.shape)


def share(block, name, size):
    copies = jnp.broadcast_to(block[None], (size,) + block.shape)
    return lax.all_to_all(copies, name, split_axis=0, concat_axis=0, tiled=True)


def sum_blocks(blocks, kind):
    return jnp.sum(blocks.astype(F32), axis=0).astype(kind)


def scatter_reps(blocks):
    rows = blocks.reshape((-1,) + blocks.shape[2:])
    return lax.psum_scatter(rows, "rep", scatter_dimension=0, tiled=True)


def swap(block, name, bits, size):
    return lax.ppermute(block, name, [(at, at ^ bits) for at in range(size)])


def chip_scatter(kept, sent, sizes):
    size = sizes["exp"]
    chips = size // 2
    received = [swap(part, "exp", 1, size) for part in sent]
    parts = fold(kept, received, chips)
    return parts


def plane_sum(parts, sizes, after=()):
    size = sizes["exp"]
    chips = size // 2
    received = [swap(parts[other], "exp", 2 * other, size) for other in range(1, chips)]
    total = tie(parts[0], *after).astype(F32)
    for part in received:
        total += part.astype(F32)
    return total.astype(BF16)


def rep_sum(block, sizes):
    reps = sizes["rep"]
    blocks = block.reshape((reps, -1) + block.shape[1:])
    at = lax.convert_element_type(lax.axis_index("rep"), jnp.uint32)

    def pick(other):
        return lax.dynamic_index_in_dim(blocks, at ^ jnp.uint32(other), 0, keepdims=False)

    received = [swap(pick(other), "rep", other, reps) for other in range(1, reps)]
    total = pick(0).astype(F32)
    for part in received:
        total += part.astype(F32)
    return total.astype(BF16)


def rep_gather(block, sizes):
    reps = sizes["rep"]
    at = lax.axis_index("rep")
    parts = [block] + [swap(block, "rep", other, reps) for other in range(1, reps)]
    rows = []
    for slot in range(reps):
        chosen = parts[0]
        for other in range(1, reps):
            chosen = jnp.where((at ^ other) == slot, parts[other], chosen)
        rows.append(chosen)
    return jnp.concatenate(rows, axis=0)


def plane_gather(block, sizes):
    size = sizes["exp"]
    mine = [block] + [swap(block, "exp", 2 * other, size) for other in range(1, size // 2)]
    return mine + [swap(part, "exp", 1, size) for part in mine]


def join_halves(kept, sent):
    first = (lax.axis_index("exp") & 1) == 0
    return jnp.where(first, jnp.concatenate([kept, sent]), jnp.concatenate([sent, kept]))


def small_sums(vectors_two, vectors_one, router_grad):
    blank = jnp.zeros_like(vectors_one[:1])
    return jnp.concatenate([vectors_two[:3], vectors_one[:4], blank, router_grad], axis=0)


def tie(value, *after):
    return lax.optimization_barrier((value,) + after)[0]


def on_device(
    sizes,
    tokens,
    cotangent,
    expert_ids,
    expert_slots,
    w_qkv,
    q_bias,
    v_bias,
    w_proj,
    proj_bias,
    gain_one,
    shift_one,
    gain_two,
    shift_two,
    w_router,
    expert_in,
    expert_in_bias,
    expert_out,
    expert_out_bias,
):
    row_count, width = tokens.shape
    experts = w_router.shape[1]
    slot_count = row_count // experts
    reps = sizes["rep"]
    ids = expert_ids.T
    slots = expert_slots.T
    router_turned = w_router.T
    weight_in = expert_in[0]
    weight_out = expert_out[0]
    bias_in = expert_in_bias.astype(F32)
    bias_out = expert_out_bias.astype(F32)

    cot_arrived = exchange(gather(ids, slots, cotangent, slot_count), experts)
    normed_one, qkv, weights, inverse, context, residual, dispatched = front(
        tokens,
        w_qkv,
        jnp.concatenate([q_bias, v_bias, proj_bias]).astype(F32),
        w_proj,
        gain_one,
        shift_one,
        gain_two,
        shift_two,
        ids,
        slots,
        slot_count,
    )
    arrived = exchange(dispatched, experts)
    raw, columns, cot_turned, along = raw_active(ids, slots, cot_arrived, weight_out, bias_out, slot_count)
    active, grad_hidden, out_grad, gate, logits_grad = expert(
        arrived, cot_turned, weight_in, bias_in, raw, along, router_turned, reps
    )
    grad_eout = scatter_reps(out_grad)
    back = expert_back(grad_hidden, weight_in, gate, logits_grad, router_turned)
    source = exchange(back, experts)
    made, out_bias_grad = produce(gate, active, cot_arrived, weight_out, bias_out)
    part = weight_in.shape[1] // reps
    out_part = width // reps
    early = early_rows(width)
    tail = jnp.pad(out_bias_grad.reshape(reps, 1, out_part), ((0, 0), (0, 0), (0, part - out_part)))
    in_first, in_second, router_grad = weight_in_grad(arrived, gate, grad_hidden, tail, logits_grad, reps)
    source, made, in_first, in_second = lax.optimization_barrier((source, made, in_first, in_second))
    in_first = scatter_reps(in_first)
    returned = exchange(made, experts)
    grad_residual, grad_context, proj_kept, proj_sent, vectors_two = middle(
        columns, source, residual, cotangent, context, w_proj, gain_two
    )
    pairs = width // PAIR
    most = pairs // 2
    saved = (qkv, weights, inverse, context, normed_one)
    grads_a, kept_a, sent_a = attend_back(grad_context, *saved, 0, most)
    chips = sizes["exp"] // 2
    if (width // sizes["exp"]) % 16 == 0:
        sent_a, proj_sent, returned = lax.optimization_barrier((sent_a, proj_sent, returned))
        parts_a = chip_scatter((proj_kept, kept_a), (proj_sent, sent_a), sizes)
        grads_b, kept_b, sent_b = attend_back(
            tie(grad_context, grads_a, parts_a[0], grad_eout), *saved, most, pairs - most
        )
        sum_a = plane_sum(parts_a, sizes, (sent_b,))
        sum_a, sent_b = lax.optimization_barrier((sum_a, sent_b))
        parts_b = chip_scatter((kept_b,), (sent_b,), sizes)
        sum_b = plane_sum(parts_b, sizes)
        grad_tokens, vectors_one = last(
            tokens, (grads_a, grads_b), w_qkv, tie(grad_residual, parts_b[0]), gain_one
        )
        sum_a, sum_b, vectors_one, in_first = lax.optimization_barrier((sum_a, sum_b, vectors_one, in_first))
        block = jnp.concatenate([sum_a, sum_b], axis=1)
        small = small_sums(vectors_two, vectors_one, router_grad)
        small = sum_blocks(share(small, "exp", sizes["exp"]), F32)
        block = rep_sum(block, sizes)
        block, small, in_second = lax.optimization_barrier((block, small, in_second))
        in_second = scatter_reps(in_second)
        mixed = combine(columns, tie(returned, block), residual)
        block = rep_gather(block, sizes)
        block, mixed = lax.optimization_barrier((block, mixed))
        small = sum_blocks(share(small, "rep", reps), F32)
        parts = plane_gather(block, sizes)
        here = lax.axis_index("exp")
        order = jnp.arange(chips, dtype=jnp.int32) ^ (here >> 1)
        core = here & 1
        where = jnp.concatenate([core * chips + order, (1 - core) * chips + order]).astype(jnp.int32)
        grad_w_proj, grad_w_qkv = finish(parts, where, most * PAIR)
    else:
        in_second = scatter_reps(in_second)
        grads_b, kept_b, sent_b = attend_back(grad_context, *saved, most, pairs - most)
        mixed = combine(columns, returned, residual)
        grad_tokens, vectors_one = last(tokens, (grads_a, grads_b), w_qkv, grad_residual, gain_one)
        block = join_halves(
            jnp.concatenate([proj_kept, kept_a, kept_b], axis=1),
            jnp.concatenate([proj_sent, sent_a, sent_b], axis=1),
        )
        small = lax.psum(small_sums(vectors_two, vectors_one, router_grad), ("rep", "exp"))
        block = lax.psum(block, ("rep", "exp"))
        where = jnp.zeros((1,), jnp.int32)
        grad_w_proj, grad_w_qkv = finish((block,), where, most * PAIR)
    return (
        mixed,
        grad_tokens,
        grad_w_qkv,
        small[5],
        small[6],
        grad_w_proj,
        small[2],
        small[3],
        small[4],
        small[0],
        small[1],
        small[8 : 8 + experts].T,
        jnp.concatenate([in_first[:early], in_second], axis=0)[None].astype(F32),
        in_first[early : early + 1].astype(F32),
        turn(grad_eout)[None],
        in_first[early + 1 : early + 2, :out_part].astype(F32),
    )


def solution(mesh):
    rows = P(("rep", "exp"), None)
    placed = (rows,) * 4 + (P(),) * 10 + (
        P("exp", None, None),
        P("exp", None),
        P("exp", None, None),
        P("exp", None),
    )
    return jax.shard_map(
        functools.partial(on_device, dict(mesh.shape)),
        mesh=mesh,
        in_specs=placed,
        out_specs=(rows, rows)
        + (P(),) * 10
        + (P("exp", None, "rep"), P("exp", "rep"), P("exp", "rep", None), P("exp", "rep")),
        check_vma=False,
    )
```

```python
import functools

import jax
import jax.numpy as jnp
from jax import lax
from jax.experimental import pallas as pl
from jax.experimental.pallas import tpu as pltpu
from jax.sharding import PartitionSpec as P

HEAD_DIM = 64
SEQ = 576
PAIR = 2 * HEAD_DIM
SPLIT = 512
AUX = 128
EPSILON = 1e-06
F32 = jnp.float32
BF16 = jnp.bfloat16
VMEM_BYTES = 56 * 2**20


def dot(left, right):
    return lax.dot_general(left, right, (((1,), (0,)), ((), ())), preferred_element_type=F32)


def dot_last(left, right):
    return lax.dot_general(left, right, (((1,), (1,)), ((), ())), preferred_element_type=F32)


def dot_first(left, right):
    return lax.dot_general(left, right, (((0,), (0,)), ((), ())), preferred_element_type=F32)


def thirds(value):
    high = value.astype(BF16)
    rest = value - high.astype(F32)
    middle = rest.astype(BF16)
    return high, middle, (rest - middle.astype(F32)).astype(BF16)


def standardize(field):
    centred = field - jnp.mean(field, axis=-1, keepdims=True)
    inverse = lax.rsqrt(jnp.mean(centred * centred, axis=-1, keepdims=True) + EPSILON)
    return centred * inverse, inverse


def standardize_back(grad, gain, unit, inverse):
    scaled = grad * gain
    along = jnp.mean(scaled * unit, axis=-1, keepdims=True)
    return inverse * (scaled - jnp.mean(scaled, axis=-1, keepdims=True) - unit * along)


def as_row(ref):
    return ref[...].astype(F32).reshape(1, -1)


def column_sum(field):
    return jnp.sum(field, axis=0, keepdims=True)


def params(most=False):
    return pltpu.CompilerParams(vmem_limit_bytes=63 * 2**20 if most else VMEM_BYTES)


SCALE = 0.01
EARLY = 19
EXPERT_CHUNK = 768
EXPERT_ROWS = 576


def cost(flops, bytes_moved):
    return pl.CostEstimate(flops=int(flops * SCALE), transcendentals=0, bytes_accessed=int(bytes_moved * SCALE))


def whole(array):
    return pl.BlockSpec(array.shape, lambda *ids: (0,) * array.ndim)


def shape(dims, kind):
    return jax.ShapeDtypeStruct(dims, kind)


def split_heads(pair):
    lane = lax.broadcasted_iota(jnp.int32, pair.shape, 1)
    zero = jnp.zeros_like(pair)
    first = jnp.where(lane < HEAD_DIM, pair, zero)
    second = jnp.where(lane < HEAD_DIM, zero, pair)
    return jnp.concatenate([first[:SPLIT], second[:SPLIT], first[SPLIT:], second[SPLIT:]], axis=0)


def key_sides():
    row = lax.broadcasted_iota(jnp.int32, (2 * SEQ, PAIR), 0)
    lane = lax.broadcasted_iota(jnp.int32, (2 * SEQ, PAIR), 1)
    is_first = (row < SPLIT) | ((row >= 2 * SPLIT) & (row < SPLIT + SEQ))
    return is_first, lane


def columns_of(ids, slots, slot_count):
    return jnp.where(slots[...] >= 0, ids[...] * slot_count + slots[...], -1)


def slot_hits(columns, at, count):
    slot = at + lax.broadcasted_iota(jnp.int32, (count, columns.shape[1]), 0)
    hit = (columns[0:1, :] == slot) | (columns[1:2, :] == slot)
    return jnp.where(hit, 1.0, 0.0).astype(BF16)


def front_kernel(
    chunk,
    slot_count,
    tokens,
    w_qkv_hbm,
    q_bias,
    v_bias,
    w_proj_hbm,
    proj_bias,
    gain_one,
    shift_one,
    gain_two,
    shift_two,
    ids,
    slots,
    normed_one_out,
    qkv_out,
    weights_out,
    inverse_out,
    context_out,
    residual_out,
    dispatched_out,
    value_side,
    normed_two,
    w_qkv,
    w_proj,
    normed_one,
    qkv,
    residual_held,
    arrivals,
    departures,
):
    image = pl.program_id(0)
    pair = pl.program_id(1)
    pairs = context_out.shape[1]
    here = pl.ds(pl.multiple_of(image * SEQ, SEQ), SEQ)
    load_qkv = pltpu.make_async_copy(w_qkv_hbm, w_qkv, arrivals.at[0])
    load_proj = pltpu.make_async_copy(w_proj_hbm, w_proj, arrivals.at[1])
    save_normed = pltpu.make_async_copy(normed_one, normed_one_out.at[here], departures.at[0])
    save_qkv = pltpu.make_async_copy(qkv, qkv_out.at[image], departures.at[1])
    save_residual = pltpu.make_async_copy(residual_held, residual_out.at[here], departures.at[2])

    @pl.when((image == 0) & (pair == 0))
    def _():
        load_qkv.start()
        load_proj.start()
        is_first, lane = key_sides()
        value_side[:, PAIR:] = jnp.where(is_first == (lane < HEAD_DIM), 1.0, 0.0).astype(BF16)

    @pl.when(pair == 0)
    def _():
        unit, _ = standardize(tokens[...].astype(F32))
        normed_one[...] = (unit * as_row(gain_one) + as_row(shift_one)).astype(BF16)

    @pl.when((image == 0) & (pair == 0))
    def _():
        load_qkv.wait()

    @pl.when(pair == 0)
    def _():
        normed = normed_one[...]
        width = w_qkv.shape[1]
        third = width // 3
        step = 2 * PAIR
        for at in range(0, width, step):
            part = dot(normed, w_qkv[:, at : at + step])
            if at < third:
                part = part + as_row(q_bias)[:, at : at + step]
            if at >= 2 * third:
                part = part + as_row(v_bias)[:, at - 2 * third : at - 2 * third + step]
            part = part.astype(BF16)
            if at < third:
                part = part * jnp.asarray(HEAD_DIM**-0.5, BF16)
            qkv[at // PAIR] = part[:, :PAIR]
            qkv[at // PAIR + 1] = part[:, PAIR:]
        save_normed.start()
        save_qkv.start()

    keys = split_heads(qkv[pairs + pair])
    value_side[:, :PAIR] = split_heads(qkv[2 * pairs + pair])
    values = value_side[...]
    low = lax.broadcasted_iota(jnp.int32, (chunk, PAIR), 1) < HEAD_DIM

    def soften(scores):
        first = scores[:, :SPLIT]
        second = scores[:, SPLIT : 2 * SPLIT]
        tail = scores[:, 2 * SPLIT :]
        first_max = jnp.maximum(
            jnp.max(first, axis=1, keepdims=True),
            jnp.max(jnp.where(low, tail, -jnp.inf), axis=1, keepdims=True),
        )
        second_max = jnp.maximum(
            jnp.max(second, axis=1, keepdims=True),
            jnp.max(jnp.where(low, -jnp.inf, tail), axis=1, keepdims=True),
        )
        return jnp.concatenate(
            [
                jnp.exp(first - first_max).astype(BF16),
                jnp.exp(second - second_max).astype(BF16),
                jnp.exp(tail - jnp.where(low, first_max, second_max)).astype(BF16),
            ],
            axis=1,
        )

    def settle(rows, exponent):
        summed = dot(exponent, values)
        inverse = 1.0 / summed[:, PAIR:]
        inverse_out[0, 0, rows] = inverse
        context_out[0, pair, rows] = (summed[:, :PAIR] * inverse).astype(BF16)

    spans = [slice(at, at + chunk) for at in range(0, SEQ, chunk)]
    coming = dot_last(qkv[pair, spans[0]], keys)
    waiting = None
    for at, rows in enumerate(spans):
        scores = coming
        if at + 1 < len(spans):
            coming = dot_last(qkv[pair, spans[at + 1]], keys)
        if waiting is not None:
            settle(*waiting)
        exponent = soften(scores)
        weights_out[0, 0, rows] = exponent
        waiting = (rows, exponent)
    settle(*waiting)

    @pl.when((image == 0) & (pair == pairs - 1))
    def _():
        load_proj.wait()

    @pl.when((image > 0) & (pair == pairs - 1))
    def _():
        before = pl.ds(pl.multiple_of((image - 1) * SEQ, SEQ), SEQ)
        pltpu.make_async_copy(residual_held, residual_out.at[before], departures.at[2]).wait()

    @pl.when(pair == pairs - 1)
    def _():
        context = jnp.concatenate([context_out[0, at] for at in range(pairs)], axis=1)
        offset = as_row(proj_bias)
        residual = tokens[...].astype(F32) + (dot(context, w_proj[...]) + offset)
        residual_held[...] = residual
        save_residual.start()
        unit, _ = standardize(residual)
        normed = (unit * as_row(gain_two) + as_row(shift_two)).astype(BF16)
        normed_two[here] = normed
        save_normed.wait()
        save_qkv.wait()

    @pl.when((pair == pairs - 1) & (image == pl.num_programs(0) - 1))
    def _():
        columns = columns_of(ids, slots, slot_count)
        part = SEQ // 2
        for at in range(0, dispatched_out.shape[0], part):
            hits = slot_hits(columns, at, part)
            dispatched_out[at : at + part] = dot(hits, normed_two[...]).astype(BF16)
        save_residual.wait()


def front(tokens, w_qkv, q_bias, v_bias, w_proj, proj_bias, gain_one, shift_one, gain_two, shift_two, ids, slots, slot_count):
    rows, width = tokens.shape
    images = rows // SEQ
    pairs = width // PAIR

    def per_image(columns):
        return pl.BlockSpec((SEQ, columns), lambda i, p: (i, 0))

    anywhere = pl.BlockSpec(memory_space=pl.ANY)
    fixed = (proj_bias, gain_one, shift_one, gain_two, shift_two, ids, slots)
    return pl.pallas_call(
        functools.partial(front_kernel, SEQ // 2, slot_count),
        grid=(images, pairs),
        in_specs=[per_image(width), anywhere, whole(q_bias), whole(v_bias), anywhere]
        + [whole(array) for array in fixed],
        out_specs=[
            anywhere,
            anywhere,
            pl.BlockSpec((1, 1, SEQ, 2 * SEQ), lambda i, p: (i, p, 0, 0)),
            pl.BlockSpec((1, 1, SEQ, PAIR), lambda i, p: (i, p, 0, 0)),
            pl.BlockSpec((1, pairs, SEQ, PAIR), lambda i, p: (i, 0, 0, 0)),
            anywhere,
            pl.BlockSpec((rows, width), lambda i, p: (0, 0)),
        ],
        out_shape=[
            shape((rows, width), BF16),
            shape((images, 3 * pairs, SEQ, PAIR), BF16),
            shape((images, pairs, SEQ, 2 * SEQ), BF16),
            shape((images, pairs, SEQ, PAIR), F32),
            shape((images, pairs, SEQ, PAIR), BF16),
            shape((rows, width), F32),
            shape((rows, width), BF16),
        ],
        scratch_shapes=[
            pltpu.VMEM((2 * SEQ, 2 * PAIR), BF16),
            pltpu.VMEM((rows, width), BF16),
            pltpu.VMEM(w_qkv.shape, BF16),
            pltpu.VMEM(w_proj.shape, BF16),
            pltpu.VMEM((SEQ, width), BF16),
            pltpu.VMEM((3 * pairs, SEQ, PAIR), BF16),
            pltpu.VMEM((SEQ, width), F32),
            pltpu.SemaphoreType.DMA((2,)),
            pltpu.SemaphoreType.DMA((3,)),
        ],
        compiler_params=params(True),
        cost_estimate=cost(30e9, 60e6),
        name="front",
    )(tokens, w_qkv, q_bias, v_bias, w_proj, *fixed)


def gather_kernel(chunk, slot_count, ids, slots, rows, out):
    columns = columns_of(ids, slots, slot_count)
    for at in range(0, rows.shape[0], chunk):
        out[at : at + chunk] = dot(slot_hits(columns, at, chunk), rows[...]).astype(BF16)


def gather(ids, slots, rows, slot_count, chunk=288):
    return pl.pallas_call(
        functools.partial(gather_kernel, chunk, slot_count),
        out_shape=shape(rows.shape, BF16),
        compiler_params=params(True),
        cost_estimate=cost(4e9, 8e6),
        name="gather",
    )(ids, slots, rows)


def raw_kernel(slot_count, ids, slots, cotangent, weight_out, bias_out, out, columns_out, turned, along):
    @pl.when(pl.program_id(0) == 0)
    def _():
        columns = columns_of(ids, slots, slot_count)
        pad = jnp.full((6, columns.shape[1]), -1, jnp.int32)
        columns_out[...] = jnp.concatenate([columns, pad], axis=0).T
        turned[...] = cotangent[...].T
        for at in range(0, along.shape[0], 32):
            rows = slice(at, at + 32)
            along[rows, :] = lane_sums(cotangent[rows, :].astype(F32) * bias_out[...])

    out[...] = dot_last(cotangent[...], weight_out[...]).astype(BF16)


def raw_active(ids, slots, cotangent, weight_out, bias_out, slot_count, chunk=768):
    count, width = cotangent.shape
    hidden = weight_out.shape[0]
    return pl.pallas_call(
        functools.partial(raw_kernel, slot_count),
        grid=(hidden // chunk,),
        in_specs=[
            whole(ids),
            whole(slots),
            whole(cotangent),
            pl.BlockSpec((chunk, width), lambda i: (i, 0)),
            whole(bias_out),
        ],
        out_specs=[
            pl.BlockSpec((count, chunk), lambda i: (0, i)),
            pl.BlockSpec((count, 8), lambda i: (0, 0)),
            pl.BlockSpec((width, count), lambda i: (0, 0)),
            pl.BlockSpec((count, AUX), lambda i: (0, 0)),
        ],
        out_shape=[
            shape((count, hidden), BF16),
            shape((count, 8), jnp.int32),
            shape((width, count), BF16),
            shape((count, AUX), F32),
        ],
        compiler_params=params(True),
        cost_estimate=cost(9e9, 14e6),
        name="raw_active",
    )(ids, slots, cotangent, weight_out, bias_out)


def joined_thirds(value, order):
    parts = thirds(value)
    return jnp.concatenate([parts[at] for at in order], axis=1)


LEFT = (0, 0, 1, 1, 0, 2)
RIGHT = (0, 1, 0, 1, 2, 0)


def expert_kernel(
    row_chunk,
    arrived,
    cot_turned,
    weight_in,
    bias_in,
    raw,
    along,
    w_router,
    active_out,
    hidden_out,
    weight_grad,
    gate_out,
    logits_grad,
    produced_grad,
    gate_total,
    router,
):
    step = pl.program_id(0)
    count = arrived.shape[0]
    experts = w_router.shape[0]

    @pl.when(step == 0)
    def _():
        parts = dot_last(arrived[...], jnp.concatenate(thirds(w_router[...]), axis=0))
        logits = parts[:, :experts] + (parts[:, experts : 2 * experts] + parts[:, 2 * experts :])
        exponent = jnp.exp(logits - jnp.max(logits, axis=1, keepdims=True))
        probs = exponent / jnp.sum(exponent, axis=1, keepdims=True)
        router[...] = probs
        own = lax.broadcasted_iota(jnp.int32, (count, experts), 1) == lax.axis_index("exp")
        gate = jnp.sum(jnp.where(own, probs, 0.0), axis=1, keepdims=True)
        gate_out[...] = jnp.broadcast_to(gate, gate_out.shape)
        gate_row = gate_out[...].T[0:1]
        produced_grad[...] = (cot_turned[...].astype(F32) * gate_row).astype(BF16)
        gate_total[...] = along[...]

    for at in range(0, count, row_chunk):
        rows = slice(at, at + row_chunk)
        hidden = dot(arrived[rows, :], weight_in[...]) + bias_in[...]
        scaled = hidden * (0.5**0.5)
        curve = lax.erf(scaled)
        cdf = 0.5 + 0.5 * curve
        active = (hidden * cdf).astype(BF16)
        bell = jnp.exp(scaled * -scaled) * (0.5 * 1.1283791670955126 * 0.5**0.5)
        slope = (cdf + hidden * bell).astype(BF16)
        incoming = raw[rows, :]
        active_out[rows, :] = active
        hidden_out[rows, :] = incoming * slope
        gate_total[rows, :] += lane_sums((incoming * active).astype(F32))
    weight_grad[0] = dot(produced_grad[...], active_out[...]).astype(BF16)

    @pl.when(step == pl.num_programs(0) - 1)
    def _():
        own = lax.broadcasted_iota(jnp.int32, (count, experts), 1) == lax.axis_index("exp")
        scale = jnp.sum(gate_total[...], axis=1, keepdims=True) * gate_out[:, 0:1]
        logits_grad[...] = scale * (jnp.where(own, 1.0, 0.0) - router[...])


def lane_sums(field):
    total = field[:, :AUX]
    for at in range(AUX, field.shape[1], AUX):
        total = total + field[:, at : at + AUX]
    return total


def expert(arrived, cot_turned, weight_in, bias_in, raw, along, w_router, reps, chunk=EXPERT_CHUNK):
    count, width = arrived.shape
    hidden = weight_in.shape[1]
    experts = w_router.shape[0]
    part = hidden // reps
    cuts = part // chunk

    def column_block(rows):
        return pl.BlockSpec((rows, chunk), lambda i: (0, i))

    def fixed(rows, columns):
        return pl.BlockSpec((rows, columns), lambda i: (0, 0))

    return pl.pallas_call(
        functools.partial(expert_kernel, EXPERT_ROWS),
        grid=(hidden // chunk,),
        in_specs=[
            whole(arrived),
            whole(cot_turned),
            column_block(width),
            column_block(1),
            column_block(count),
            whole(along),
            whole(w_router),
        ],
        out_specs=[
            column_block(count),
            column_block(count),
            pl.BlockSpec((1, width, chunk), lambda i: (i // cuts, 0, i % cuts)),
            fixed(count, AUX),
            fixed(count, experts),
        ],
        out_shape=[
            shape((count, hidden), BF16),
            shape((count, hidden), BF16),
            shape((reps, width, part), BF16),
            shape((count, AUX), F32),
            shape((count, experts), F32),
        ],
        scratch_shapes=[
            pltpu.VMEM((width, count), BF16),
            pltpu.VMEM((count, AUX), F32),
            pltpu.VMEM((count, experts), F32),
        ],
        compiler_params=params(True),
        cost_estimate=cost(24e9, 35e6),
        name="expert",
    )(arrived, cot_turned, weight_in, bias_in, raw, along, w_router)


def expert_back_kernel(grad_hidden, weight_in, gate, logits_grad, w_router, out):
    right = jnp.concatenate([thirds(w_router[...])[at] for at in RIGHT], axis=0)
    total = gate[:, 0:1] * dot_last(grad_hidden[...], weight_in[...])
    total += dot(joined_thirds(logits_grad[...], LEFT), right)
    out[...] = total.astype(BF16)


def expert_back(grad_hidden, weight_in, gate, logits_grad, w_router, chunk=288):
    count, hidden = grad_hidden.shape
    experts, width = w_router.shape

    def rows(columns):
        return pl.BlockSpec((chunk, columns), lambda i: (i, 0))

    return pl.pallas_call(
        expert_back_kernel,
        grid=(count // chunk,),
        in_specs=[rows(hidden), whole(weight_in), rows(AUX), rows(experts), whole(w_router)],
        out_specs=rows(width),
        out_shape=shape((count, width), BF16),
        compiler_params=params(True),
        cost_estimate=cost(12e9, 15e6),
        name="expert_back",
    )(grad_hidden, weight_in, gate, logits_grad, w_router)


def turn_kernel(field, out):
    out[...] = field[...].T.astype(F32)


def turn(field):
    return pl.pallas_call(
        turn_kernel,
        out_shape=shape(field.shape[::-1], F32),
        compiler_params=params(),
        cost_estimate=cost(1e9, 5e6),
        name="turn",
    )(field)


def early_rows(width):
    return width // 48 * EARLY


def weight_in_kernel(steps, arrived, gate, grad_hidden, out_bias_grad, logits_grad, first, second, router_grad, turned):
    width = arrived.shape[1]
    experts = logits_grad.shape[1]
    half = first.shape[1] - 16

    @pl.when(pl.program_id(0) == 0)
    def _():
        for at in range(0, arrived.shape[0], 128):
            rows = slice(at, at + 128)
            turned[:width, rows] = (arrived[rows, :].astype(F32) * gate[rows, 0:1]).astype(BF16).T
        gate_row = jnp.broadcast_to(gate[...].T[0:1], (16, arrived.shape[0]))
        high = gate_row.astype(BF16)
        row = lax.broadcasted_iota(jnp.int32, high.shape, 0)
        low = (gate_row - high.astype(F32)).astype(BF16)
        turned[width:] = jnp.where(row == 0, high, jnp.where(row == 1, low, jnp.zeros_like(low)))
        parts = dot_first(joined_thirds(logits_grad[...], (0, 1, 2)), arrived[...])
        router_grad[...] = parts[:experts] + parts[experts : 2 * experts] + parts[2 * experts :]

    total = dot(turned[...], grad_hidden[...])
    second[0] = total[half:width].astype(BF16)
    first[0, :half] = total[:half].astype(BF16)
    row = lax.broadcasted_iota(jnp.int32, (first.shape[1] - half, first.shape[2]), 0)
    bias_grad = total[width : width + 1] + total[width + 1 : width + 2]
    share_of = width // steps
    tail = jnp.zeros((1, total.shape[1]), F32)
    for at in range(steps):
        part = out_bias_grad[:, at * share_of : (at + 1) * share_of]
        part = jnp.concatenate([part, jnp.zeros((1, total.shape[1] - share_of), F32)], axis=1)
        tail = jnp.where(pl.program_id(0) == at, part, tail)
    first[0, half:] = jnp.where(row == 0, bias_grad, jnp.where(row == 1, tail, 0.0)).astype(BF16)


def weight_in_grad(arrived, gate, grad_hidden, out_bias_grad, logits_grad, reps):
    count, hidden = grad_hidden.shape
    width = arrived.shape[1]
    early = early_rows(width)
    part = hidden // reps
    return pl.pallas_call(
        functools.partial(weight_in_kernel, reps),
        grid=(reps,),
        in_specs=[
            whole(arrived),
            whole(gate),
            pl.BlockSpec((count, part), lambda i: (0, i)),
            whole(out_bias_grad),
            whole(logits_grad),
        ],
        out_specs=[
            pl.BlockSpec((1, early + 16, part), lambda i: (i, 0, 0)),
            pl.BlockSpec((1, width - early, part), lambda i: (i, 0, 0)),
            pl.BlockSpec((logits_grad.shape[1], width), lambda i: (0, 0)),
        ],
        out_shape=[
            shape((reps, early + 16, part), BF16),
            shape((reps, width - early, part), BF16),
            shape((logits_grad.shape[1], width), F32),
        ],
        scratch_shapes=[pltpu.VMEM((width + 16, count), BF16)],
        compiler_params=params(True),
        cost_estimate=cost(10e9, 15e6),
        name="weight_in_grad",
    )(arrived, gate, grad_hidden, out_bias_grad, logits_grad)


def produce_kernel(gate, active, cotangent, weight_out, bias_out, out, bias_grad):
    @pl.when(pl.program_id(0) == 0)
    def _():
        bias_grad[...] = jnp.zeros_like(bias_grad)

    bias_grad[...] += column_sum(gate[:, 0:1] * cotangent[...].astype(F32))
    out[...] = (gate[:, 0:1] * (dot(active[...], weight_out[...]) + bias_out[...])).astype(BF16)


def produce(gate, active, cotangent, weight_out, bias_out, chunk=288):
    count, hidden = active.shape
    width = weight_out.shape[1]

    def rows(columns):
        return pl.BlockSpec((chunk, columns), lambda i: (i, 0))

    return pl.pallas_call(
        produce_kernel,
        grid=(count // chunk,),
        in_specs=[rows(AUX), rows(hidden), rows(width), whole(weight_out), whole(bias_out)],
        out_specs=[rows(width), pl.BlockSpec((1, width), lambda i: (0, 0))],
        out_shape=[shape((count, width), BF16), shape((1, width), F32)],
        compiler_params=params(True),
        cost_estimate=cost(10e9, 15e6),
        name="produce",
    )(gate, active, cotangent, weight_out, bias_out)


def token_hits(columns, slots):
    slot = lax.broadcasted_iota(jnp.int32, (columns.shape[0], slots), 1)
    hit = (columns[:, 0:1] == slot) | (columns[:, 1:2] == slot)
    return jnp.where(hit, 1.0, 0.0).astype(BF16)


def split_rows(value, kept, sent):
    half = value.shape[0] // 2
    first = (lax.axis_index("exp") & 1) == 0
    low, high = value[:half], value[half:]
    kept[...] = jnp.where(first, low, high)
    sent[...] = jnp.where(first, high, low)


def middle_kernel(
    sub,
    columns,
    source,
    residual,
    cotangent,
    context,
    w_proj,
    gain_two,
    grad_residual_out,
    grad_context_out,
    proj_kept,
    proj_sent,
    vectors,
    branch,
    proj_total,
):
    step = pl.program_id(0)
    chunk = residual.shape[0]
    pairs = context.shape[1]

    @pl.when(step == 0)
    def _():
        vectors[...] = jnp.zeros_like(vectors)
        proj_total[...] = jnp.zeros_like(proj_total)

    hits = token_hits(columns, source.shape[0])
    grad_residual_out[...] = dot(hits, source[...])
    gain = as_row(gain_two)
    for at in range(0, chunk, sub):
        rows = slice(at, at + sub)
        grad_normed = grad_residual_out[rows, :]
        unit, inverse = standardize(residual[rows, :])
        grad_residual = cotangent[rows, :].astype(F32) + standardize_back(grad_normed, gain, unit, inverse)
        grad_residual_out[rows, :] = grad_residual
        rounded = grad_residual.astype(BF16)
        branch[rows, :] = rounded
        vectors[0:1] += column_sum(grad_normed * unit)
        vectors[1:2] += column_sum(grad_normed)
        vectors[2:3] += column_sum(rounded.astype(F32))
    grad_context = dot_last(branch[...], w_proj[...]).astype(BF16)
    for pair in range(pairs):
        grad_context_out[0, pair] = grad_context[:, pair * PAIR : (pair + 1) * PAIR]
    joined = jnp.concatenate([context[0, pair] for pair in range(pairs)], axis=1)
    proj_total[...] += dot_first(joined, branch[...])

    @pl.when(step == pl.num_programs(0) - 1)
    def _():
        split_rows(proj_total[...].astype(BF16), proj_kept, proj_sent)


def middle(columns, source, residual, cotangent, context, w_proj, gain_two, chunk=288):
    rows, width = residual.shape
    images, pairs = context.shape[:2]
    parts = SEQ // chunk

    def rows_of(columns):
        return pl.BlockSpec((chunk, columns), lambda i: (i, 0))

    by_pair = pl.BlockSpec((1, pairs, chunk, PAIR), lambda i: (i // parts, 0, i % parts, 0))
    return pl.pallas_call(
        functools.partial(middle_kernel, 32),
        grid=(rows // chunk,),
        in_specs=[
            rows_of(8),
            whole(source),
            rows_of(width),
            rows_of(width),
            by_pair,
            whole(w_proj),
            whole(gain_two),
        ],
        out_specs=[
            rows_of(width),
            by_pair,
            pl.BlockSpec((width // 2, width), lambda i: (0, 0)),
            pl.BlockSpec((width // 2, width), lambda i: (0, 0)),
            pl.BlockSpec((8, width), lambda i: (0, 0)),
        ],
        out_shape=[
            shape((rows, width), F32),
            shape((images, pairs, SEQ, PAIR), BF16),
            shape((width // 2, width), BF16),
            shape((width // 2, width), BF16),
            shape((8, width), F32),
        ],
        scratch_shapes=[pltpu.VMEM((chunk, width), BF16), pltpu.VMEM((width, width), F32)],
        compiler_params=params(True),
        cost_estimate=cost(14e9, 20e6),
        name="middle",
    )(columns, source, residual, cotangent, context, w_proj, gain_two)


def merge_heads(turned):
    first = jnp.concatenate([turned[:HEAD_DIM, :SPLIT], turned[:HEAD_DIM, 2 * SPLIT : SPLIT + SEQ]], axis=1)
    second = jnp.concatenate([turned[HEAD_DIM:, SPLIT : 2 * SPLIT], turned[HEAD_DIM:, SPLIT + SEQ :]], axis=1)
    return jnp.concatenate([first, second], axis=0).T


def attend_back_kernel(
    chunk,
    grad_context,
    queries,
    keys,
    values,
    weights,
    inverse,
    context,
    normed_one,
    grad_out,
    kept,
    sent,
    value_side,
    grad_scores,
):
    pair = pl.program_id(0)
    image = pl.program_id(1)

    @pl.when((pair == 0) & (image == 0))
    def _():
        is_first, lane = key_sides()
        taken = (is_first & (lane < 2)) | (jnp.logical_not(is_first) & (lane >= 2) & (lane < 4))
        value_side[:, PAIR:] = jnp.where(taken, -1.0, 0.0).astype(BF16)

    key_side = split_heads(keys[0, 0])
    value_side[:, :PAIR] = split_heads(values[0, 0])
    lane = lax.broadcasted_iota(jnp.int32, (chunk, PAIR), 1)
    low = lane < HEAD_DIM
    scaled = []
    for at in range(0, SEQ, chunk):
        rows = slice(at, at + chunk)
        grads = (grad_context[0, 0, rows].astype(F32) * inverse[0, 0, rows]).astype(BF16)
        scaled.append(grads)
        product = grads.astype(F32) * context[0, 0, rows].astype(F32)
        first = jnp.sum(jnp.where(low, product, 0.0), axis=1, keepdims=True)
        second = jnp.sum(jnp.where(low, 0.0, product), axis=1, keepdims=True)
        offset = jnp.where(lane < 2, first, second)
        high = offset.astype(BF16).astype(F32)
        extra = jnp.where(
            (lane == 0) | (lane == 2), high, jnp.where((lane == 1) | (lane == 3), offset - high, 0.0)
        ).astype(BF16)
        grad_weights = dot_last(jnp.concatenate([grads, extra], axis=1), value_side[...])
        part = grad_weights.astype(BF16) * weights[0, 0, rows]
        grad_scores[rows] = part
        place = pl.ds(pl.multiple_of(image * SEQ + at, 32), chunk)
        grad_out[0, pair, place] = (dot(part, key_side) * HEAD_DIM**-0.5).astype(BF16)
    grads = jnp.concatenate(scaled, axis=0)
    place = pl.ds(pl.multiple_of(image * SEQ, 64), SEQ)
    grad_out[1, pair, place] = merge_heads(dot_first(queries[0, 0], grad_scores[...])).astype(BF16)
    grad_out[2, pair, place] = merge_heads(dot_first(grads, weights[0, 0])).astype(BF16)

    @pl.when((pair == pl.num_programs(0) - 1) & (image == pl.num_programs(1) - 1))
    def _():
        for kind in range(3):
            joined = jnp.concatenate([grad_out[kind, at] for at in range(grad_out.shape[1])], axis=1)
            span = joined.shape[1]
            columns = slice(kind * span, (kind + 1) * span)
            total = dot_first(normed_one[...], joined).astype(BF16)
            split_rows(total, kept.at[:, columns], sent.at[:, columns])


def attend_back(grad_context, qkv, weights, inverse, context, normed_one, first, count):
    images, pairs = context.shape[:2]
    rows, width = normed_one.shape

    def block(offset):
        return pl.BlockSpec((1, 1, SEQ, PAIR), lambda p, i: (i, offset + p, 0, 0))

    return pl.pallas_call(
        functools.partial(attend_back_kernel, SEQ),
        grid=(count, images),
        in_specs=[
            block(first),
            block(first),
            block(pairs + first),
            block(2 * pairs + first),
            pl.BlockSpec((1, 1, SEQ, 2 * SEQ), lambda p, i: (i, first + p, 0, 0)),
            block(first),
            block(first),
            whole(normed_one),
        ],
        out_specs=[
            pl.BlockSpec((3, count, rows, PAIR), lambda p, i: (0, 0, 0, 0)),
            pl.BlockSpec((width // 2, 3 * count * PAIR), lambda p, i: (0, 0)),
            pl.BlockSpec((width // 2, 3 * count * PAIR), lambda p, i: (0, 0)),
        ],
        out_shape=[shape((3, count, rows, PAIR), BF16)] + [shape((width // 2, 3 * count * PAIR), BF16)] * 2,
        scratch_shapes=[pltpu.VMEM((2 * SEQ, 2 * PAIR), BF16), pltpu.VMEM((SEQ, 2 * SEQ), BF16)],
        compiler_params=params(),
        cost_estimate=cost(17e9 * (1 if first else 1), 20e6 * (1 if first else 1)),
        name="attend_back",
    )(grad_context, qkv, qkv, qkv, weights, inverse, context, normed_one)


def last_kernel(groups, sub, tokens, w_qkv, grad_residual, gain_one, *rest):
    grads = rest[:groups]
    out, vectors = rest[groups:]
    width = tokens.shape[1]

    @pl.when(pl.program_id(0) == 0)
    def _():
        vectors[...] = jnp.zeros_like(vectors)

    total = jnp.zeros(tokens.shape, F32)
    for kind in range(3):
        joined = jnp.concatenate(
            [grad[kind, at] for grad in grads for at in range(grad.shape[1])], axis=1
        )
        total += dot_last(joined, w_qkv[:, kind * width : (kind + 1) * width])
        if kind == 0:
            vectors[2:3] += column_sum(joined.astype(F32))
        if kind == 2:
            vectors[3:4] += column_sum(joined.astype(F32))
    out[...] = total
    gain = as_row(gain_one)
    for at in range(0, tokens.shape[0], sub):
        rows = slice(at, at + sub)
        grad_normed = out[rows, :]
        unit, inverse = standardize(tokens[rows, :].astype(F32))
        out[rows, :] = grad_residual[rows, :] + standardize_back(grad_normed, gain, unit, inverse)
        vectors[0:1] += column_sum(grad_normed * unit)
        vectors[1:2] += column_sum(grad_normed)


def last(tokens, grads, w_qkv, grad_residual, gain_one, chunk=288):
    rows, width = tokens.shape
    block = pl.BlockSpec((chunk, width), lambda i: (i, 0))
    return pl.pallas_call(
        functools.partial(last_kernel, len(grads), 32),
        grid=(rows // chunk,),
        in_specs=[block, whole(w_qkv), block, whole(gain_one)]
        + [pl.BlockSpec((3, grad.shape[1], chunk, PAIR), lambda i: (0, 0, i, 0)) for grad in grads],
        out_specs=[block, pl.BlockSpec((8, width), lambda i: (0, 0))],
        out_shape=[shape((rows, width), F32), shape((8, width), F32)],
        compiler_params=params(),
        cost_estimate=cost(10e9, 15e6),
        name="last",
    )(tokens, w_qkv, grad_residual, gain_one, *grads)


def fold_kernel(count, *refs):
    inputs, outs = refs[: 2 * count], refs[2 * count :]
    at = lax.axis_index("exp") >> 1
    rows = outs[0].shape[0]
    for other, out in enumerate(outs):
        here = pl.ds(pl.multiple_of((at ^ other) * rows, rows), rows)
        column = 0
        for kept, received in zip(inputs[:count], inputs[count:]):
            span = slice(column, column + kept.shape[1])
            out[:, span] = (kept[here, :].astype(F32) + received[here, :].astype(F32)).astype(BF16)
            column = span.stop


def fold(kept, received, chips):
    rows = kept[0].shape[0] // chips
    width = sum(part.shape[1] for part in kept)
    return pl.pallas_call(
        functools.partial(fold_kernel, len(kept)),
        out_shape=[shape((rows, width), BF16)] * chips,
        compiler_params=params(),
        cost_estimate=cost(1e9, 10e6),
        name="fold",
    )(*kept, *received)


def finish_kernel(left, where, *refs):
    inputs, (proj_out, out) = refs[:-2], refs[-2:]
    width = proj_out.shape[1]
    right = width - left
    for step, part in enumerate(inputs):

        @pl.when(pl.program_id(0) == step)
        def _():
            proj_out[...] = part[:, :width].astype(F32)
            for kind in range(3):
                to = kind * width
                at = width + kind * left
                out[:, to : to + left] = part[:, at : at + left].astype(F32)
                at = width + 3 * left + kind * right
                out[:, to + left : to + width] = part[:, at : at + right].astype(F32)


def finish(parts, where, left):
    steps = len(parts)
    rows = parts[0].shape[0]
    width = parts[0].shape[1] // 4

    def landing(columns):
        return pl.BlockSpec((rows, columns), lambda i, at: (at[i], 0))

    return pl.pallas_call(
        functools.partial(finish_kernel, left),
        grid_spec=pltpu.PrefetchScalarGridSpec(
            num_scalar_prefetch=1,
            grid=(steps,),
            in_specs=[pl.BlockSpec(part.shape, lambda i, at: (0, 0)) for part in parts],
            out_specs=[landing(width), landing(3 * width)],
        ),
        out_shape=[shape((rows * steps, width), F32), shape((rows * steps, 3 * width), F32)],
        compiler_params=params(),
        cost_estimate=cost(1e9, 10e6),
        name="finish",
    )(where, *parts)


def combine_kernel(columns, source, residual, out):
    hits = token_hits(columns, source.shape[0])
    out[...] = (residual[...] + dot(hits, source[...])).astype(BF16)


def combine(columns, source, residual, chunk=288):
    rows, width = residual.shape
    return pl.pallas_call(
        combine_kernel,
        grid=(rows // chunk,),
        in_specs=[
            pl.BlockSpec((chunk, 8), lambda i: (i, 0)),
            whole(source),
            pl.BlockSpec((chunk, width), lambda i: (i, 0)),
        ],
        out_specs=pl.BlockSpec((chunk, width), lambda i: (i, 0)),
        out_shape=shape((rows, width), BF16),
        compiler_params=params(),
        cost_estimate=cost(6e9, 10e6),
        name="combine",
    )(columns, source, residual)


def exchange(rows, experts):
    blocks = rows.reshape(experts, rows.shape[0] // experts, rows.shape[1])
    return lax.all_to_all(blocks, "exp", split_axis=0, concat_axis=0, tiled=True).reshape(rows.shape)


def share(block, name, size):
    copies = jnp.broadcast_to(block[None], (size,) + block.shape)
    return lax.all_to_all(copies, name, split_axis=0, concat_axis=0, tiled=True)


def sum_blocks(blocks, kind):
    return jnp.sum(blocks.astype(F32), axis=0).astype(kind)


def scatter_reps(blocks):
    rows = blocks.reshape((-1,) + blocks.shape[2:])
    return lax.psum_scatter(rows, "rep", scatter_dimension=0, tiled=True)


def swap(block, name, bits, size):
    return lax.ppermute(block, name, [(at, at ^ bits) for at in range(size)])


def chip_scatter(kept, sent, sizes):
    size = sizes["exp"]
    chips = size // 2
    received = [swap(part, "exp", 1, size) for part in sent]
    parts = fold(kept, received, chips)
    return parts


def plane_sum(parts, sizes, after=()):
    size = sizes["exp"]
    chips = size // 2
    received = [swap(parts[other], "exp", 2 * other, size) for other in range(1, chips)]
    total = tie(parts[0], *after).astype(F32)
    for part in received:
        total += part.astype(F32)
    return total.astype(BF16)


def rep_sum(block, sizes):
    reps = sizes["rep"]
    blocks = block.reshape((reps, -1) + block.shape[1:])
    at = lax.convert_element_type(lax.axis_index("rep"), jnp.uint32)

    def pick(other):
        return lax.dynamic_index_in_dim(blocks, at ^ jnp.uint32(other), 0, keepdims=False)

    received = [swap(pick(other), "rep", other, reps) for other in range(1, reps)]
    total = pick(0).astype(F32)
    for part in received:
        total += part.astype(F32)
    return total.astype(BF16)


def rep_gather(block, sizes):
    reps = sizes["rep"]
    at = lax.axis_index("rep")
    parts = [block] + [swap(block, "rep", other, reps) for other in range(1, reps)]
    rows = []
    for slot in range(reps):
        chosen = parts[0]
        for other in range(1, reps):
            chosen = jnp.where((at ^ other) == slot, parts[other], chosen)
        rows.append(chosen)
    return jnp.concatenate(rows, axis=0)


def plane_gather(block, sizes):
    size = sizes["exp"]
    mine = [block] + [swap(block, "exp", 2 * other, size) for other in range(1, size // 2)]
    return mine + [swap(part, "exp", 1, size) for part in mine]


def join_halves(kept, sent):
    first = (lax.axis_index("exp") & 1) == 0
    return jnp.where(first, jnp.concatenate([kept, sent]), jnp.concatenate([sent, kept]))


def small_sums(vectors_two, vectors_one, router_grad):
    blank = jnp.zeros_like(vectors_one[:1])
    return jnp.concatenate([vectors_two[:3], vectors_one[:4], blank, router_grad], axis=0)


def tie(value, *after):
    return lax.optimization_barrier((value,) + after)[0]


def on_device(
    sizes,
    tokens,
    cotangent,
    expert_ids,
    expert_slots,
    w_qkv,
    q_bias,
    v_bias,
    w_proj,
    proj_bias,
    gain_one,
    shift_one,
    gain_two,
    shift_two,
    w_router,
    expert_in,
    expert_in_bias,
    expert_out,
    expert_out_bias,
):
    row_count, width = tokens.shape
    experts = w_router.shape[1]
    slot_count = row_count // experts
    reps = sizes["rep"]
    ids = expert_ids.T
    slots = expert_slots.T
    router_turned = w_router.T
    weight_in = expert_in[0]
    weight_out = expert_out[0]
    bias_in = expert_in_bias.astype(F32)
    bias_out = expert_out_bias.astype(F32)

    cot_arrived = exchange(gather(ids, slots, cotangent, slot_count), experts)
    normed_one, qkv, weights, inverse, context, residual, dispatched = front(
        tokens,
        w_qkv,
        q_bias,
        v_bias,
        w_proj,
        proj_bias,
        gain_one,
        shift_one,
        gain_two,
        shift_two,
        ids,
        slots,
        slot_count,
    )
    arrived = exchange(dispatched, experts)
    raw, columns, cot_turned, along = raw_active(ids, slots, cot_arrived, weight_out, bias_out, slot_count)
    active, grad_hidden, out_grad, gate, logits_grad = expert(
        arrived, cot_turned, weight_in, bias_in, raw, along, router_turned, reps
    )
    grad_eout = scatter_reps(out_grad)
    back = expert_back(grad_hidden, weight_in, gate, logits_grad, router_turned)
    source = exchange(back, experts)
    made, out_bias_grad = produce(gate, active, cot_arrived, weight_out, bias_out)
    out_part = width // reps
    early = early_rows(width)
    in_first, in_second, router_grad = weight_in_grad(arrived, gate, grad_hidden, out_bias_grad, logits_grad, reps)
    source, made, in_first, in_second = lax.optimization_barrier((source, made, in_first, in_second))
    in_first = scatter_reps(in_first)
    returned = exchange(made, experts)
    grad_residual, grad_context, proj_kept, proj_sent, vectors_two = middle(
        columns, source, residual, cotangent, context, w_proj, gain_two
    )
    pairs = width // PAIR
    most = pairs // 2
    saved = (qkv, weights, inverse, context, normed_one)
    grads_a, kept_a, sent_a = attend_back(grad_context, *saved, 0, most)
    chips = sizes["exp"] // 2
    if (width // sizes["exp"]) % 16 == 0:
        sent_a, proj_sent, returned = lax.optimization_barrier((sent_a, proj_sent, returned))
        parts_a = chip_scatter((proj_kept, kept_a), (proj_sent, sent_a), sizes)
        grads_b, kept_b, sent_b = attend_back(
            tie(grad_context, grads_a, parts_a[0], grad_eout), *saved, most, pairs - most
        )
        sum_a = plane_sum(parts_a, sizes, (sent_b,))
        sum_a, sent_b = lax.optimization_barrier((sum_a, sent_b))
        parts_b = chip_scatter((kept_b,), (sent_b,), sizes)
        sum_b = plane_sum(parts_b, sizes)
        grad_tokens, vectors_one = last(
            tokens, (grads_a, grads_b), w_qkv, tie(grad_residual, parts_b[0]), gain_one
        )
        sum_a, sum_b, vectors_one, in_first = lax.optimization_barrier((sum_a, sum_b, vectors_one, in_first))
        block = jnp.concatenate([sum_a, sum_b], axis=1)
        small = small_sums(vectors_two, vectors_one, router_grad)
        small = sum_blocks(share(small, "exp", sizes["exp"]), F32)
        block = rep_sum(block, sizes)
        block, small, in_second = lax.optimization_barrier((block, small, in_second))
        in_second = scatter_reps(in_second)
        mixed = combine(columns, tie(returned, block), residual)
        block = rep_gather(block, sizes)
        block, mixed = lax.optimization_barrier((block, mixed))
        small = sum_blocks(share(small, "rep", reps), F32)
        parts = plane_gather(block, sizes)
        here = lax.axis_index("exp")
        order = jnp.arange(chips, dtype=jnp.int32) ^ (here >> 1)
        core = here & 1
        where = jnp.concatenate([core * chips + order, (1 - core) * chips + order]).astype(jnp.int32)
        grad_w_proj, grad_w_qkv = finish(parts, where, most * PAIR)
    else:
        in_second = scatter_reps(in_second)
        grads_b, kept_b, sent_b = attend_back(grad_context, *saved, most, pairs - most)
        mixed = combine(columns, returned, residual)
        grad_tokens, vectors_one = last(tokens, (grads_a, grads_b), w_qkv, grad_residual, gain_one)
        block = join_halves(
            jnp.concatenate([proj_kept, kept_a, kept_b], axis=1),
            jnp.concatenate([proj_sent, sent_a, sent_b], axis=1),
        )
        small = lax.psum(small_sums(vectors_two, vectors_one, router_grad), ("rep", "exp"))
        block = lax.psum(block, ("rep", "exp"))
        where = jnp.zeros((1,), jnp.int32)
        grad_w_proj, grad_w_qkv = finish((block,), where, most * PAIR)
    return (
        mixed,
        grad_tokens,
        grad_w_qkv,
        small[5],
        small[6],
        grad_w_proj,
        small[2],
        small[3],
        small[4],
        small[0],
        small[1],
        small[8 : 8 + experts].T,
        jnp.concatenate([in_first[:early], in_second], axis=0)[None].astype(F32),
        in_first[early : early + 1].astype(F32),
        turn(grad_eout)[None],
        in_first[early + 1 : early + 2, :out_part].astype(F32),
    )


def solution(mesh):
    rows = P(("rep", "exp"), None)
    placed = (rows,) * 4 + (P(),) * 10 + (
        P("exp", None, None),
        P("exp", None),
        P("exp", None, None),
        P("exp", None),
    )
    return jax.shard_map(
        functools.partial(on_device, dict(mesh.shape)),
        mesh=mesh,
        in_specs=placed,
        out_specs=(rows, rows)
        + (P(),) * 10
        + (P("exp", None, "rep"), P("exp", "rep"), P("exp", "rep", None), P("exp", "rep")),
        check_vma=False,
    )
```

```python
import functools

import jax
import jax.numpy as jnp
from jax import lax
from jax.experimental import pallas as pl
from jax.experimental.pallas import tpu as pltpu
from jax.sharding import PartitionSpec as P

HEAD_DIM = 64
SEQ = 576
PAIR = 2 * HEAD_DIM
SPLIT = 512
AUX = 128
EPSILON = 1e-06
F32 = jnp.float32
BF16 = jnp.bfloat16
VMEM_BYTES = 56 * 2**20


def dot(left, right):
    return lax.dot_general(left, right, (((1,), (0,)), ((), ())), preferred_element_type=F32)


def dot_last(left, right):
    return lax.dot_general(left, right, (((1,), (1,)), ((), ())), preferred_element_type=F32)


def dot_first(left, right):
    return lax.dot_general(left, right, (((0,), (0,)), ((), ())), preferred_element_type=F32)


def thirds(value):
    high = value.astype(BF16)
    rest = value - high.astype(F32)
    middle = rest.astype(BF16)
    return high, middle, (rest - middle.astype(F32)).astype(BF16)


def standardize(field):
    centred = field - jnp.mean(field, axis=-1, keepdims=True)
    inverse = lax.rsqrt(jnp.mean(centred * centred, axis=-1, keepdims=True) + EPSILON)
    return centred * inverse, inverse


def standardize_back(grad, gain, unit, inverse):
    scaled = grad * gain
    along = jnp.mean(scaled * unit, axis=-1, keepdims=True)
    return inverse * (scaled - jnp.mean(scaled, axis=-1, keepdims=True) - unit * along)


def as_row(ref):
    return ref[...].astype(F32).reshape(1, -1)


def column_sum(field):
    return jnp.sum(field, axis=0, keepdims=True)


def params(most=False):
    return pltpu.CompilerParams(vmem_limit_bytes=63 * 2**20 if most else VMEM_BYTES)


SCALE = 0.01
EARLY = 17
EXPERT_CHUNK = 768
EXPERT_ROWS = 576


def cost(flops, bytes_moved):
    return pl.CostEstimate(flops=int(flops * SCALE), transcendentals=0, bytes_accessed=int(bytes_moved * SCALE))


def whole(array):
    return pl.BlockSpec(array.shape, lambda *ids: (0,) * array.ndim)


def shape(dims, kind):
    return jax.ShapeDtypeStruct(dims, kind)


def split_heads(pair):
    lane = lax.broadcasted_iota(jnp.int32, pair.shape, 1)
    zero = jnp.zeros_like(pair)
    first = jnp.where(lane < HEAD_DIM, pair, zero)
    second = jnp.where(lane < HEAD_DIM, zero, pair)
    return jnp.concatenate([first[:SPLIT], second[:SPLIT], first[SPLIT:], second[SPLIT:]], axis=0)


def key_sides():
    row = lax.broadcasted_iota(jnp.int32, (2 * SEQ, PAIR), 0)
    lane = lax.broadcasted_iota(jnp.int32, (2 * SEQ, PAIR), 1)
    is_first = (row < SPLIT) | ((row >= 2 * SPLIT) & (row < SPLIT + SEQ))
    return is_first, lane


def columns_of(ids, slots, slot_count):
    return jnp.where(slots[...] >= 0, ids[...] * slot_count + slots[...], -1)


def slot_hits(columns, at, count):
    slot = at + lax.broadcasted_iota(jnp.int32, (count, columns.shape[1]), 0)
    hit = (columns[0:1, :] == slot) | (columns[1:2, :] == slot)
    return jnp.where(hit, 1.0, 0.0).astype(BF16)


def front_kernel(
    chunk,
    slot_count,
    tokens,
    w_qkv_hbm,
    q_bias,
    v_bias,
    w_proj_hbm,
    proj_bias,
    gain_one,
    shift_one,
    gain_two,
    shift_two,
    ids,
    slots,
    normed_one_out,
    qkv_out,
    weights_out,
    inverse_out,
    context_out,
    residual_out,
    dispatched_out,
    value_side,
    normed_two,
    w_qkv,
    w_proj,
    normed_one,
    qkv,
    residual_held,
    arrivals,
    departures,
):
    image = pl.program_id(0)
    pair = pl.program_id(1)
    pairs = context_out.shape[1]
    here = pl.ds(pl.multiple_of(image * SEQ, SEQ), SEQ)
    load_qkv = pltpu.make_async_copy(w_qkv_hbm, w_qkv, arrivals.at[0])
    load_proj = pltpu.make_async_copy(w_proj_hbm, w_proj, arrivals.at[1])
    save_normed = pltpu.make_async_copy(normed_one, normed_one_out.at[here], departures.at[0])
    save_qkv = pltpu.make_async_copy(qkv, qkv_out.at[image], departures.at[1])
    save_residual = pltpu.make_async_copy(residual_held, residual_out.at[here], departures.at[2])

    @pl.when((image == 0) & (pair == 0))
    def _():
        load_qkv.start()
        load_proj.start()
        is_first, lane = key_sides()
        value_side[:, PAIR:] = jnp.where(is_first == (lane < HEAD_DIM), 1.0, 0.0).astype(BF16)

    @pl.when(pair == 0)
    def _():
        unit, _ = standardize(tokens[...].astype(F32))
        normed_one[...] = (unit * as_row(gain_one) + as_row(shift_one)).astype(BF16)

    @pl.when((image == 0) & (pair == 0))
    def _():
        load_qkv.wait()

    @pl.when(pair == 0)
    def _():
        normed = normed_one[...]
        width = w_qkv.shape[1]
        third = width // 3
        step = 2 * PAIR
        for at in range(0, width, step):
            part = dot(normed, w_qkv[:, at : at + step])
            if at < third:
                part = part + as_row(q_bias)[:, at : at + step]
            if at >= 2 * third:
                part = part + as_row(v_bias)[:, at - 2 * third : at - 2 * third + step]
            part = part.astype(BF16)
            if at < third:
                part = part * jnp.asarray(HEAD_DIM**-0.5, BF16)
            qkv[at // PAIR] = part[:, :PAIR]
            qkv[at // PAIR + 1] = part[:, PAIR:]
        save_normed.start()
        save_qkv.start()

    keys = split_heads(qkv[pairs + pair])
    value_side[:, :PAIR] = split_heads(qkv[2 * pairs + pair])
    values = value_side[...]
    low = lax.broadcasted_iota(jnp.int32, (chunk, PAIR), 1) < HEAD_DIM

    def soften(scores):
        first = scores[:, :SPLIT]
        second = scores[:, SPLIT : 2 * SPLIT]
        tail = scores[:, 2 * SPLIT :]
        first_max = jnp.maximum(
            jnp.max(first, axis=1, keepdims=True),
            jnp.max(jnp.where(low, tail, -jnp.inf), axis=1, keepdims=True),
        )
        second_max = jnp.maximum(
            jnp.max(second, axis=1, keepdims=True),
            jnp.max(jnp.where(low, -jnp.inf, tail), axis=1, keepdims=True),
        )
        return jnp.concatenate(
            [
                jnp.exp(first - first_max).astype(BF16),
                jnp.exp(second - second_max).astype(BF16),
                jnp.exp(tail - jnp.where(low, first_max, second_max)).astype(BF16),
            ],
            axis=1,
        )

    def settle(rows, exponent):
        summed = dot(exponent, values)
        inverse = 1.0 / summed[:, PAIR:]
        inverse_out[0, 0, rows] = inverse
        context_out[0, pair, rows] = (summed[:, :PAIR] * inverse).astype(BF16)

    spans = [slice(at, at + chunk) for at in range(0, SEQ, chunk)]
    coming = dot_last(qkv[pair, spans[0]], keys)
    waiting = None
    for at, rows in enumerate(spans):
        scores = coming
        if at + 1 < len(spans):
            coming = dot_last(qkv[pair, spans[at + 1]], keys)
        if waiting is not None:
            settle(*waiting)
        exponent = soften(scores)
        weights_out[0, 0, rows] = exponent
        waiting = (rows, exponent)
    settle(*waiting)

    @pl.when((image == 0) & (pair == pairs - 1))
    def _():
        load_proj.wait()

    @pl.when((image > 0) & (pair == pairs - 1))
    def _():
        before = pl.ds(pl.multiple_of((image - 1) * SEQ, SEQ), SEQ)
        pltpu.make_async_copy(residual_held, residual_out.at[before], departures.at[2]).wait()

    @pl.when(pair == pairs - 1)
    def _():
        context = jnp.concatenate([context_out[0, at] for at in range(pairs)], axis=1)
        offset = as_row(proj_bias)
        residual = tokens[...].astype(F32) + (dot(context, w_proj[...]) + offset)
        residual_held[...] = residual
        save_residual.start()
        unit, _ = standardize(residual)
        normed = (unit * as_row(gain_two) + as_row(shift_two)).astype(BF16)
        normed_two[here] = normed
        save_normed.wait()
        save_qkv.wait()

    @pl.when((pair == pairs - 1) & (image == pl.num_programs(0) - 1))
    def _():
        columns = columns_of(ids, slots, slot_count)
        part = SEQ // 2
        for at in range(0, dispatched_out.shape[0], part):
            hits = slot_hits(columns, at, part)
            dispatched_out[at : at + part] = dot(hits, normed_two[...]).astype(BF16)
        save_residual.wait()


def front(tokens, w_qkv, q_bias, v_bias, w_proj, proj_bias, gain_one, shift_one, gain_two, shift_two, ids, slots, slot_count):
    rows, width = tokens.shape
    images = rows // SEQ
    pairs = width // PAIR

    def per_image(columns):
        return pl.BlockSpec((SEQ, columns), lambda i, p: (i, 0))

    anywhere = pl.BlockSpec(memory_space=pl.ANY)
    fixed = (proj_bias, gain_one, shift_one, gain_two, shift_two, ids, slots)
    return pl.pallas_call(
        functools.partial(front_kernel, SEQ // 2, slot_count),
        grid=(images, pairs),
        in_specs=[per_image(width), anywhere, whole(q_bias), whole(v_bias), anywhere]
        + [whole(array) for array in fixed],
        out_specs=[
            anywhere,
            anywhere,
            pl.BlockSpec((1, 1, SEQ, 2 * SEQ), lambda i, p: (i, p, 0, 0)),
            pl.BlockSpec((1, 1, SEQ, PAIR), lambda i, p: (i, p, 0, 0)),
            pl.BlockSpec((1, pairs, SEQ, PAIR), lambda i, p: (i, 0, 0, 0)),
            anywhere,
            pl.BlockSpec((rows, width), lambda i, p: (0, 0)),
        ],
        out_shape=[
            shape((rows, width), BF16),
            shape((images, 3 * pairs, SEQ, PAIR), BF16),
            shape((images, pairs, SEQ, 2 * SEQ), BF16),
            shape((images, pairs, SEQ, PAIR), F32),
            shape((images, pairs, SEQ, PAIR), BF16),
            shape((rows, width), F32),
            shape((rows, width), BF16),
        ],
        scratch_shapes=[
            pltpu.VMEM((2 * SEQ, 2 * PAIR), BF16),
            pltpu.VMEM((rows, width), BF16),
            pltpu.VMEM(w_qkv.shape, BF16),
            pltpu.VMEM(w_proj.shape, BF16),
            pltpu.VMEM((SEQ, width), BF16),
            pltpu.VMEM((3 * pairs, SEQ, PAIR), BF16),
            pltpu.VMEM((SEQ, width), F32),
            pltpu.SemaphoreType.DMA((2,)),
            pltpu.SemaphoreType.DMA((3,)),
        ],
        compiler_params=params(True),
        cost_estimate=cost(30e9, 60e6),
        name="front",
    )(tokens, w_qkv, q_bias, v_bias, w_proj, *fixed)


def gather_kernel(chunk, slot_count, ids, slots, rows, out):
    columns = columns_of(ids, slots, slot_count)
    for at in range(0, rows.shape[0], chunk):
        out[at : at + chunk] = dot(slot_hits(columns, at, chunk), rows[...]).astype(BF16)


def gather(ids, slots, rows, slot_count, chunk=288):
    return pl.pallas_call(
        functools.partial(gather_kernel, chunk, slot_count),
        out_shape=shape(rows.shape, BF16),
        compiler_params=params(True),
        cost_estimate=cost(4e9, 8e6),
        name="gather",
    )(ids, slots, rows)


def raw_kernel(slot_count, ids, slots, cotangent, weight_out, bias_out, out, columns_out, turned, along):
    @pl.when(pl.program_id(0) == 0)
    def _():
        columns = columns_of(ids, slots, slot_count)
        pad = jnp.full((6, columns.shape[1]), -1, jnp.int32)
        columns_out[...] = jnp.concatenate([columns, pad], axis=0).T
        turned[...] = cotangent[...].T
        for at in range(0, along.shape[0], 32):
            rows = slice(at, at + 32)
            along[rows, :] = lane_sums(cotangent[rows, :].astype(F32) * bias_out[...])

    out[...] = dot_last(cotangent[...], weight_out[...]).astype(BF16)


def raw_active(ids, slots, cotangent, weight_out, bias_out, slot_count, chunk=768):
    count, width = cotangent.shape
    hidden = weight_out.shape[0]
    return pl.pallas_call(
        functools.partial(raw_kernel, slot_count),
        grid=(hidden // chunk,),
        in_specs=[
            whole(ids),
            whole(slots),
            whole(cotangent),
            pl.BlockSpec((chunk, width), lambda i: (i, 0)),
            whole(bias_out),
        ],
        out_specs=[
            pl.BlockSpec((count, chunk), lambda i: (0, i)),
            pl.BlockSpec((count, 8), lambda i: (0, 0)),
            pl.BlockSpec((width, count), lambda i: (0, 0)),
            pl.BlockSpec((count, AUX), lambda i: (0, 0)),
        ],
        out_shape=[
            shape((count, hidden), BF16),
            shape((count, 8), jnp.int32),
            shape((width, count), BF16),
            shape((count, AUX), F32),
        ],
        compiler_params=params(True),
        cost_estimate=cost(9e9, 14e6),
        name="raw_active",
    )(ids, slots, cotangent, weight_out, bias_out)


def joined_thirds(value, order):
    parts = thirds(value)
    return jnp.concatenate([parts[at] for at in order], axis=1)


LEFT = (0, 0, 1, 1, 0, 2)
RIGHT = (0, 1, 0, 1, 2, 0)


def expert_kernel(
    row_chunk,
    arrived,
    cot_turned,
    weight_in,
    bias_in,
    raw,
    along,
    w_router,
    active_out,
    hidden_out,
    weight_grad,
    gate_out,
    logits_grad,
    produced_grad,
    gate_total,
    router,
):
    step = pl.program_id(0)
    count = arrived.shape[0]
    experts = w_router.shape[0]

    @pl.when(step == 0)
    def _():
        parts = dot_last(arrived[...], jnp.concatenate(thirds(w_router[...]), axis=0))
        logits = parts[:, :experts] + (parts[:, experts : 2 * experts] + parts[:, 2 * experts :])
        exponent = jnp.exp(logits - jnp.max(logits, axis=1, keepdims=True))
        probs = exponent / jnp.sum(exponent, axis=1, keepdims=True)
        router[...] = probs
        own = lax.broadcasted_iota(jnp.int32, (count, experts), 1) == lax.axis_index("exp")
        gate = jnp.sum(jnp.where(own, probs, 0.0), axis=1, keepdims=True)
        gate_out[...] = jnp.broadcast_to(gate, gate_out.shape)
        gate_row = gate_out[...].T[0:1]
        produced_grad[...] = (cot_turned[...].astype(F32) * gate_row).astype(BF16)
        gate_total[...] = along[...]

    for at in range(0, count, row_chunk):
        rows = slice(at, at + row_chunk)
        hidden = dot(arrived[rows, :], weight_in[...]) + bias_in[...]
        scaled = hidden * (0.5**0.5)
        curve = lax.erf(scaled)
        cdf = 0.5 + 0.5 * curve
        active = (hidden * cdf).astype(BF16)
        bell = jnp.exp(scaled * -scaled) * (0.5 * 1.1283791670955126 * 0.5**0.5)
        slope = (cdf + hidden * bell).astype(BF16)
        incoming = raw[rows, :]
        active_out[rows, :] = active
        hidden_out[rows, :] = incoming * slope
        gate_total[rows, :] += lane_sums((incoming * active).astype(F32))
    weight_grad[0] = dot(produced_grad[...], active_out[...]).astype(BF16)

    @pl.when(step == pl.num_programs(0) - 1)
    def _():
        own = lax.broadcasted_iota(jnp.int32, (count, experts), 1) == lax.axis_index("exp")
        scale = jnp.sum(gate_total[...], axis=1, keepdims=True) * gate_out[:, 0:1]
        logits_grad[...] = scale * (jnp.where(own, 1.0, 0.0) - router[...])


def lane_sums(field):
    total = field[:, :AUX]
    for at in range(AUX, field.shape[1], AUX):
        total = total + field[:, at : at + AUX]
    return total


def expert(arrived, cot_turned, weight_in, bias_in, raw, along, w_router, reps, chunk=EXPERT_CHUNK):
    count, width = arrived.shape
    hidden = weight_in.shape[1]
    experts = w_router.shape[0]
    part = hidden // reps
    cuts = part // chunk

    def column_block(rows):
        return pl.BlockSpec((rows, chunk), lambda i: (0, i))

    def fixed(rows, columns):
        return pl.BlockSpec((rows, columns), lambda i: (0, 0))

    return pl.pallas_call(
        functools.partial(expert_kernel, EXPERT_ROWS),
        grid=(hidden // chunk,),
        in_specs=[
            whole(arrived),
            whole(cot_turned),
            column_block(width),
            column_block(1),
            column_block(count),
            whole(along),
            whole(w_router),
        ],
        out_specs=[
            column_block(count),
            column_block(count),
            pl.BlockSpec((1, width, chunk), lambda i: (i // cuts, 0, i % cuts)),
            fixed(count, AUX),
            fixed(count, experts),
        ],
        out_shape=[
            shape((count, hidden), BF16),
            shape((count, hidden), BF16),
            shape((reps, width, part), BF16),
            shape((count, AUX), F32),
            shape((count, experts), F32),
        ],
        scratch_shapes=[
            pltpu.VMEM((width, count), BF16),
            pltpu.VMEM((count, AUX), F32),
            pltpu.VMEM((count, experts), F32),
        ],
        compiler_params=params(True),
        cost_estimate=cost(24e9, 35e6),
        name="expert",
    )(arrived, cot_turned, weight_in, bias_in, raw, along, w_router)


def expert_back_kernel(grad_hidden, weight_in, gate, logits_grad, w_router, out):
    right = jnp.concatenate([thirds(w_router[...])[at] for at in RIGHT], axis=0)
    total = gate[:, 0:1] * dot_last(grad_hidden[...], weight_in[...])
    total += dot(joined_thirds(logits_grad[...], LEFT), right)
    out[...] = total.astype(BF16)


def expert_back(grad_hidden, weight_in, gate, logits_grad, w_router, chunk=288):
    count, hidden = grad_hidden.shape
    experts, width = w_router.shape

    def rows(columns):
        return pl.BlockSpec((chunk, columns), lambda i: (i, 0))

    return pl.pallas_call(
        expert_back_kernel,
        grid=(count // chunk,),
        in_specs=[rows(hidden), whole(weight_in), rows(AUX), rows(experts), whole(w_router)],
        out_specs=rows(width),
        out_shape=shape((count, width), BF16),
        compiler_params=params(True),
        cost_estimate=cost(12e9, 15e6),
        name="expert_back",
    )(grad_hidden, weight_in, gate, logits_grad, w_router)


def turn_kernel(field, out):
    out[...] = field[...].T.astype(F32)


def turn(field):
    return pl.pallas_call(
        turn_kernel,
        out_shape=shape(field.shape[::-1], F32),
        compiler_params=params(),
        cost_estimate=cost(1e9, 5e6),
        name="turn",
    )(field)


def early_rows(width):
    return width // 48 * EARLY


def weight_in_kernel(steps, arrived, gate, grad_hidden, out_bias_grad, logits_grad, first, second, router_grad, turned):
    width = arrived.shape[1]
    experts = logits_grad.shape[1]
    half = first.shape[1] - 16

    @pl.when(pl.program_id(0) == 0)
    def _():
        for at in range(0, arrived.shape[0], 128):
            rows = slice(at, at + 128)
            turned[:width, rows] = (arrived[rows, :].astype(F32) * gate[rows, 0:1]).astype(BF16).T
        gate_row = jnp.broadcast_to(gate[...].T[0:1], (16, arrived.shape[0]))
        high = gate_row.astype(BF16)
        row = lax.broadcasted_iota(jnp.int32, high.shape, 0)
        low = (gate_row - high.astype(F32)).astype(BF16)
        turned[width:] = jnp.where(row == 0, high, jnp.where(row == 1, low, jnp.zeros_like(low)))
        parts = dot_first(joined_thirds(logits_grad[...], (0, 1, 2)), arrived[...])
        router_grad[...] = parts[:experts] + parts[experts : 2 * experts] + parts[2 * experts :]

    total = dot(turned[...], grad_hidden[...])
    second[0] = total[half:width].astype(BF16)
    first[0, :half] = total[:half].astype(BF16)
    row = lax.broadcasted_iota(jnp.int32, (first.shape[1] - half, first.shape[2]), 0)
    bias_grad = total[width : width + 1] + total[width + 1 : width + 2]
    share_of = width // steps
    tail = jnp.zeros((1, total.shape[1]), F32)
    for at in range(steps):
        part = out_bias_grad[:, at * share_of : (at + 1) * share_of]
        part = jnp.concatenate([part, jnp.zeros((1, total.shape[1] - share_of), F32)], axis=1)
        tail = jnp.where(pl.program_id(0) == at, part, tail)
    first[0, half:] = jnp.where(row == 0, bias_grad, jnp.where(row == 1, tail, 0.0)).astype(BF16)


def weight_in_grad(arrived, gate, grad_hidden, out_bias_grad, logits_grad, reps):
    count, hidden = grad_hidden.shape
    width = arrived.shape[1]
    early = early_rows(width)
    part = hidden // reps
    return pl.pallas_call(
        functools.partial(weight_in_kernel, reps),
        grid=(reps,),
        in_specs=[
            whole(arrived),
            whole(gate),
            pl.BlockSpec((count, part), lambda i: (0, i)),
            whole(out_bias_grad),
            whole(logits_grad),
        ],
        out_specs=[
            pl.BlockSpec((1, early + 16, part), lambda i: (i, 0, 0)),
            pl.BlockSpec((1, width - early, part), lambda i: (i, 0, 0)),
            pl.BlockSpec((logits_grad.shape[1], width), lambda i: (0, 0)),
        ],
        out_shape=[
            shape((reps, early + 16, part), BF16),
            shape((reps, width - early, part), BF16),
            shape((logits_grad.shape[1], width), F32),
        ],
        scratch_shapes=[pltpu.VMEM((width + 16, count), BF16)],
        compiler_params=params(True),
        cost_estimate=cost(10e9, 15e6),
        name="weight_in_grad",
    )(arrived, gate, grad_hidden, out_bias_grad, logits_grad)


def produce_kernel(gate, active, cotangent, weight_out, bias_out, out, bias_grad):
    @pl.when(pl.program_id(0) == 0)
    def _():
        bias_grad[...] = jnp.zeros_like(bias_grad)

    bias_grad[...] += column_sum(gate[:, 0:1] * cotangent[...].astype(F32))
    out[...] = (gate[:, 0:1] * (dot(active[...], weight_out[...]) + bias_out[...])).astype(BF16)


def produce(gate, active, cotangent, weight_out, bias_out, chunk=288):
    count, hidden = active.shape
    width = weight_out.shape[1]

    def rows(columns):
        return pl.BlockSpec((chunk, columns), lambda i: (i, 0))

    return pl.pallas_call(
        produce_kernel,
        grid=(count // chunk,),
        in_specs=[rows(AUX), rows(hidden), rows(width), whole(weight_out), whole(bias_out)],
        out_specs=[rows(width), pl.BlockSpec((1, width), lambda i: (0, 0))],
        out_shape=[shape((count, width), BF16), shape((1, width), F32)],
        compiler_params=params(True),
        cost_estimate=cost(10e9, 15e6),
        name="produce",
    )(gate, active, cotangent, weight_out, bias_out)


def token_hits(columns, slots):
    slot = lax.broadcasted_iota(jnp.int32, (columns.shape[0], slots), 1)
    hit = (columns[:, 0:1] == slot) | (columns[:, 1:2] == slot)
    return jnp.where(hit, 1.0, 0.0).astype(BF16)


def split_rows(value, kept, sent):
    half = value.shape[0] // 2
    first = (lax.axis_index("exp") & 1) == 0
    low, high = value[:half], value[half:]
    kept[...] = jnp.where(first, low, high)
    sent[...] = jnp.where(first, high, low)


def middle_kernel(
    sub,
    columns,
    source,
    residual,
    cotangent,
    context,
    w_proj,
    gain_two,
    grad_residual_out,
    grad_context_out,
    proj_kept,
    proj_sent,
    vectors,
    branch,
    proj_total,
):
    step = pl.program_id(0)
    chunk = residual.shape[0]
    pairs = context.shape[1]

    @pl.when(step == 0)
    def _():
        vectors[...] = jnp.zeros_like(vectors)
        proj_total[...] = jnp.zeros_like(proj_total)

    hits = token_hits(columns, source.shape[0])
    grad_residual_out[...] = dot(hits, source[...])
    gain = as_row(gain_two)
    for at in range(0, chunk, sub):
        rows = slice(at, at + sub)
        grad_normed = grad_residual_out[rows, :]
        unit, inverse = standardize(residual[rows, :])
        grad_residual = cotangent[rows, :].astype(F32) + standardize_back(grad_normed, gain, unit, inverse)
        grad_residual_out[rows, :] = grad_residual
        rounded = grad_residual.astype(BF16)
        branch[rows, :] = rounded
        vectors[0:1] += column_sum(grad_normed * unit)
        vectors[1:2] += column_sum(grad_normed)
        vectors[2:3] += column_sum(rounded.astype(F32))
    grad_context = dot_last(branch[...], w_proj[...]).astype(BF16)
    for pair in range(pairs):
        grad_context_out[0, pair] = grad_context[:, pair * PAIR : (pair + 1) * PAIR]
    joined = jnp.concatenate([context[0, pair] for pair in range(pairs)], axis=1)
    proj_total[...] += dot_first(joined, branch[...])

    @pl.when(step == pl.num_programs(0) - 1)
    def _():
        split_rows(proj_total[...].astype(BF16), proj_kept, proj_sent)


def middle(columns, source, residual, cotangent, context, w_proj, gain_two, chunk=288):
    rows, width = residual.shape
    images, pairs = context.shape[:2]
    parts = SEQ // chunk

    def rows_of(columns):
        return pl.BlockSpec((chunk, columns), lambda i: (i, 0))

    by_pair = pl.BlockSpec((1, pairs, chunk, PAIR), lambda i: (i // parts, 0, i % parts, 0))
    return pl.pallas_call(
        functools.partial(middle_kernel, 32),
        grid=(rows // chunk,),
        in_specs=[
            rows_of(8),
            whole(source),
            rows_of(width),
            rows_of(width),
            by_pair,
            whole(w_proj),
            whole(gain_two),
        ],
        out_specs=[
            rows_of(width),
            by_pair,
            pl.BlockSpec((width // 2, width), lambda i: (0, 0)),
            pl.BlockSpec((width // 2, width), lambda i: (0, 0)),
            pl.BlockSpec((8, width), lambda i: (0, 0)),
        ],
        out_shape=[
            shape((rows, width), F32),
            shape((images, pairs, SEQ, PAIR), BF16),
            shape((width // 2, width), BF16),
            shape((width // 2, width), BF16),
            shape((8, width), F32),
        ],
        scratch_shapes=[pltpu.VMEM((chunk, width), BF16), pltpu.VMEM((width, width), F32)],
        compiler_params=params(True),
        cost_estimate=cost(14e9, 20e6),
        name="middle",
    )(columns, source, residual, cotangent, context, w_proj, gain_two)


def merge_heads(turned):
    first = jnp.concatenate([turned[:HEAD_DIM, :SPLIT], turned[:HEAD_DIM, 2 * SPLIT : SPLIT + SEQ]], axis=1)
    second = jnp.concatenate([turned[HEAD_DIM:, SPLIT : 2 * SPLIT], turned[HEAD_DIM:, SPLIT + SEQ :]], axis=1)
    return jnp.concatenate([first, second], axis=0).T


def attend_back_kernel(
    chunk,
    grad_context,
    queries,
    keys,
    values,
    weights,
    inverse,
    context,
    normed_one,
    grad_out,
    kept,
    sent,
    value_side,
    grad_scores,
):
    pair = pl.program_id(0)
    image = pl.program_id(1)

    @pl.when((pair == 0) & (image == 0))
    def _():
        is_first, lane = key_sides()
        taken = (is_first & (lane < 2)) | (jnp.logical_not(is_first) & (lane >= 2) & (lane < 4))
        value_side[:, PAIR:] = jnp.where(taken, -1.0, 0.0).astype(BF16)

    key_side = split_heads(keys[0, 0])
    value_side[:, :PAIR] = split_heads(values[0, 0])
    lane = lax.broadcasted_iota(jnp.int32, (chunk, PAIR), 1)
    low = lane < HEAD_DIM
    scaled = []
    for at in range(0, SEQ, chunk):
        rows = slice(at, at + chunk)
        grads = (grad_context[0, 0, rows].astype(F32) * inverse[0, 0, rows]).astype(BF16)
        scaled.append(grads)
        product = grads.astype(F32) * context[0, 0, rows].astype(F32)
        first = jnp.sum(jnp.where(low, product, 0.0), axis=1, keepdims=True)
        second = jnp.sum(jnp.where(low, 0.0, product), axis=1, keepdims=True)
        offset = jnp.where(lane < 2, first, second)
        high = offset.astype(BF16).astype(F32)
        extra = jnp.where(
            (lane == 0) | (lane == 2), high, jnp.where((lane == 1) | (lane == 3), offset - high, 0.0)
        ).astype(BF16)
        grad_weights = dot_last(jnp.concatenate([grads, extra], axis=1), value_side[...])
        part = grad_weights.astype(BF16) * weights[0, 0, rows]
        grad_scores[rows] = part
        place = pl.ds(pl.multiple_of(image * SEQ + at, 32), chunk)
        grad_out[0, pair, place] = (dot(part, key_side) * HEAD_DIM**-0.5).astype(BF16)
    grads = jnp.concatenate(scaled, axis=0)
    place = pl.ds(pl.multiple_of(image * SEQ, 64), SEQ)
    grad_out[1, pair, place] = merge_heads(dot_first(queries[0, 0], grad_scores[...])).astype(BF16)
    grad_out[2, pair, place] = merge_heads(dot_first(grads, weights[0, 0])).astype(BF16)

    @pl.when((pair == pl.num_programs(0) - 1) & (image == pl.num_programs(1) - 1))
    def _():
        for kind in range(3):
            joined = jnp.concatenate([grad_out[kind, at] for at in range(grad_out.shape[1])], axis=1)
            span = joined.shape[1]
            columns = slice(kind * span, (kind + 1) * span)
            total = dot_first(normed_one[...], joined).astype(BF16)
            split_rows(total, kept.at[:, columns], sent.at[:, columns])


def attend_back(grad_context, qkv, weights, inverse, context, normed_one, first, count):
    images, pairs = context.shape[:2]
    rows, width = normed_one.shape

    def block(offset):
        return pl.BlockSpec((1, 1, SEQ, PAIR), lambda p, i: (i, offset + p, 0, 0))

    return pl.pallas_call(
        functools.partial(attend_back_kernel, SEQ),
        grid=(count, images),
        in_specs=[
            block(first),
            block(first),
            block(pairs + first),
            block(2 * pairs + first),
            pl.BlockSpec((1, 1, SEQ, 2 * SEQ), lambda p, i: (i, first + p, 0, 0)),
            block(first),
            block(first),
            whole(normed_one),
        ],
        out_specs=[
            pl.BlockSpec((3, count, rows, PAIR), lambda p, i: (0, 0, 0, 0)),
            pl.BlockSpec((width // 2, 3 * count * PAIR), lambda p, i: (0, 0)),
            pl.BlockSpec((width // 2, 3 * count * PAIR), lambda p, i: (0, 0)),
        ],
        out_shape=[shape((3, count, rows, PAIR), BF16)] + [shape((width // 2, 3 * count * PAIR), BF16)] * 2,
        scratch_shapes=[pltpu.VMEM((2 * SEQ, 2 * PAIR), BF16), pltpu.VMEM((SEQ, 2 * SEQ), BF16)],
        compiler_params=params(),
        cost_estimate=cost(17e9 * (1 if first else 1), 20e6 * (1 if first else 1)),
        name="attend_back",
    )(grad_context, qkv, qkv, qkv, weights, inverse, context, normed_one)


def last_kernel(groups, sub, tokens, w_qkv, grad_residual, gain_one, *rest):
    grads = rest[:groups]
    out, vectors = rest[groups:]
    width = tokens.shape[1]

    @pl.when(pl.program_id(0) == 0)
    def _():
        vectors[...] = jnp.zeros_like(vectors)

    total = jnp.zeros(tokens.shape, F32)
    for kind in range(3):
        joined = jnp.concatenate(
            [grad[kind, at] for grad in grads for at in range(grad.shape[1])], axis=1
        )
        total += dot_last(joined, w_qkv[:, kind * width : (kind + 1) * width])
        if kind == 0:
            vectors[2:3] += column_sum(joined.astype(F32))
        if kind == 2:
            vectors[3:4] += column_sum(joined.astype(F32))
    out[...] = total
    gain = as_row(gain_one)
    for at in range(0, tokens.shape[0], sub):
        rows = slice(at, at + sub)
        grad_normed = out[rows, :]
        unit, inverse = standardize(tokens[rows, :].astype(F32))
        out[rows, :] = grad_residual[rows, :] + standardize_back(grad_normed, gain, unit, inverse)
        vectors[0:1] += column_sum(grad_normed * unit)
        vectors[1:2] += column_sum(grad_normed)


def last(tokens, grads, w_qkv, grad_residual, gain_one, chunk=288):
    rows, width = tokens.shape
    block = pl.BlockSpec((chunk, width), lambda i: (i, 0))
    return pl.pallas_call(
        functools.partial(last_kernel, len(grads), 32),
        grid=(rows // chunk,),
        in_specs=[block, whole(w_qkv), block, whole(gain_one)]
        + [pl.BlockSpec((3, grad.shape[1], chunk, PAIR), lambda i: (0, 0, i, 0)) for grad in grads],
        out_specs=[block, pl.BlockSpec((8, width), lambda i: (0, 0))],
        out_shape=[shape((rows, width), F32), shape((8, width), F32)],
        compiler_params=params(),
        cost_estimate=cost(10e9, 15e6),
        name="last",
    )(tokens, w_qkv, grad_residual, gain_one, *grads)


def fold_kernel(count, *refs):
    inputs, outs = refs[: 2 * count], refs[2 * count :]
    at = lax.axis_index("exp") >> 1
    rows = outs[0].shape[0]
    for other, out in enumerate(outs):
        here = pl.ds(pl.multiple_of((at ^ other) * rows, rows), rows)
        column = 0
        for kept, received in zip(inputs[:count], inputs[count:]):
            span = slice(column, column + kept.shape[1])
            out[:, span] = (kept[here, :].astype(F32) + received[here, :].astype(F32)).astype(BF16)
            column = span.stop


def fold(kept, received, chips):
    rows = kept[0].shape[0] // chips
    width = sum(part.shape[1] for part in kept)
    return pl.pallas_call(
        functools.partial(fold_kernel, len(kept)),
        out_shape=[shape((rows, width), BF16)] * chips,
        compiler_params=params(),
        cost_estimate=cost(1e9, 10e6),
        name="fold",
    )(*kept, *received)


def finish_kernel(left, where, *refs):
    inputs, (proj_out, out) = refs[:-2], refs[-2:]
    width = proj_out.shape[1]
    right = width - left
    for step, part in enumerate(inputs):

        @pl.when(pl.program_id(0) == step)
        def _():
            proj_out[...] = part[:, :width].astype(F32)
            for kind in range(3):
                to = kind * width
                at = width + kind * left
                out[:, to : to + left] = part[:, at : at + left].astype(F32)
                at = width + 3 * left + kind * right
                out[:, to + left : to + width] = part[:, at : at + right].astype(F32)


def finish(parts, where, left):
    steps = len(parts)
    rows = parts[0].shape[0]
    width = parts[0].shape[1] // 4

    def landing(columns):
        return pl.BlockSpec((rows, columns), lambda i, at: (at[i], 0))

    return pl.pallas_call(
        functools.partial(finish_kernel, left),
        grid_spec=pltpu.PrefetchScalarGridSpec(
            num_scalar_prefetch=1,
            grid=(steps,),
            in_specs=[pl.BlockSpec(part.shape, lambda i, at: (0, 0)) for part in parts],
            out_specs=[landing(width), landing(3 * width)],
        ),
        out_shape=[shape((rows * steps, width), F32), shape((rows * steps, 3 * width), F32)],
        compiler_params=params(),
        cost_estimate=cost(1e9, 10e6),
        name="finish",
    )(where, *parts)


def combine_kernel(columns, source, residual, out):
    hits = token_hits(columns, source.shape[0])
    out[...] = (residual[...] + dot(hits, source[...])).astype(BF16)


def combine(columns, source, residual, chunk=288):
    rows, width = residual.shape
    return pl.pallas_call(
        combine_kernel,
        grid=(rows // chunk,),
        in_specs=[
            pl.BlockSpec((chunk, 8), lambda i: (i, 0)),
            whole(source),
            pl.BlockSpec((chunk, width), lambda i: (i, 0)),
        ],
        out_specs=pl.BlockSpec((chunk, width), lambda i: (i, 0)),
        out_shape=shape((rows, width), BF16),
        compiler_params=params(),
        cost_estimate=cost(6e9, 10e6),
        name="combine",
    )(columns, source, residual)


def exchange(rows, experts):
    blocks = rows.reshape(experts, rows.shape[0] // experts, rows.shape[1])
    return lax.all_to_all(blocks, "exp", split_axis=0, concat_axis=0, tiled=True).reshape(rows.shape)


def share(block, name, size):
    copies = jnp.broadcast_to(block[None], (size,) + block.shape)
    return lax.all_to_all(copies, name, split_axis=0, concat_axis=0, tiled=True)


def sum_blocks(blocks, kind):
    return jnp.sum(blocks.astype(F32), axis=0).astype(kind)


def scatter_reps(blocks):
    rows = blocks.reshape((-1,) + blocks.shape[2:])
    return lax.psum_scatter(rows, "rep", scatter_dimension=0, tiled=True)


def swap(block, name, bits, size):
    return lax.ppermute(block, name, [(at, at ^ bits) for at in range(size)])


def chip_scatter(kept, sent, sizes):
    size = sizes["exp"]
    chips = size // 2
    received = [swap(part, "exp", 1, size) for part in sent]
    parts = fold(kept, received, chips)
    return parts


def plane_sum(parts, sizes, after=()):
    size = sizes["exp"]
    chips = size // 2
    received = [swap(parts[other], "exp", 2 * other, size) for other in range(1, chips)]
    total = tie(parts[0], *after).astype(F32)
    for part in received:
        total += part.astype(F32)
    return total.astype(BF16)


def rep_sum(block, sizes):
    reps = sizes["rep"]
    blocks = block.reshape((reps, -1) + block.shape[1:])
    at = lax.convert_element_type(lax.axis_index("rep"), jnp.uint32)

    def pick(other):
        return lax.dynamic_index_in_dim(blocks, at ^ jnp.uint32(other), 0, keepdims=False)

    received = [swap(pick(other), "rep", other, reps) for other in range(1, reps)]
    total = pick(0).astype(F32)
    for part in received:
        total += part.astype(F32)
    return total.astype(BF16)


def rep_gather(block, sizes):
    reps = sizes["rep"]
    at = lax.axis_index("rep")
    parts = [block] + [swap(block, "rep", other, reps) for other in range(1, reps)]
    rows = []
    for slot in range(reps):
        chosen = parts[0]
        for other in range(1, reps):
            chosen = jnp.where((at ^ other) == slot, parts[other], chosen)
        rows.append(chosen)
    return jnp.concatenate(rows, axis=0)


def plane_gather(block, sizes):
    size = sizes["exp"]
    mine = [block] + [swap(block, "exp", 2 * other, size) for other in range(1, size // 2)]
    return mine + [swap(part, "exp", 1, size) for part in mine]


def join_halves(kept, sent):
    first = (lax.axis_index("exp") & 1) == 0
    return jnp.where(first, jnp.concatenate([kept, sent]), jnp.concatenate([sent, kept]))


def small_sums(vectors_two, vectors_one, router_grad):
    blank = jnp.zeros_like(vectors_one[:1])
    return jnp.concatenate([vectors_two[:3], vectors_one[:4], blank, router_grad], axis=0)


def tie(value, *after):
    return lax.optimization_barrier((value,) + after)[0]


def on_device(
    sizes,
    tokens,
    cotangent,
    expert_ids,
    expert_slots,
    w_qkv,
    q_bias,
    v_bias,
    w_proj,
    proj_bias,
    gain_one,
    shift_one,
    gain_two,
    shift_two,
    w_router,
    expert_in,
    expert_in_bias,
    expert_out,
    expert_out_bias,
):
    row_count, width = tokens.shape
    experts = w_router.shape[1]
    slot_count = row_count // experts
    reps = sizes["rep"]
    ids = expert_ids.T
    slots = expert_slots.T
    router_turned = w_router.T
    weight_in = expert_in[0]
    weight_out = expert_out[0]
    bias_in = expert_in_bias.astype(F32)
    bias_out = expert_out_bias.astype(F32)

    cot_arrived = exchange(gather(ids, slots, cotangent, slot_count), experts)
    normed_one, qkv, weights, inverse, context, residual, dispatched = front(
        tokens,
        w_qkv,
        q_bias,
        v_bias,
        w_proj,
        proj_bias,
        gain_one,
        shift_one,
        gain_two,
        shift_two,
        ids,
        slots,
        slot_count,
    )
    arrived = exchange(dispatched, experts)
    raw, columns, cot_turned, along = raw_active(ids, slots, cot_arrived, weight_out, bias_out, slot_count)
    active, grad_hidden, out_grad, gate, logits_grad = expert(
        arrived, cot_turned, weight_in, bias_in, raw, along, router_turned, reps
    )
    grad_eout = scatter_reps(out_grad)
    back = expert_back(grad_hidden, weight_in, gate, logits_grad, router_turned)
    source = exchange(back, experts)
    made, out_bias_grad = produce(gate, active, cot_arrived, weight_out, bias_out)
    out_part = width // reps
    early = early_rows(width)
    in_first, in_second, router_grad = weight_in_grad(arrived, gate, grad_hidden, out_bias_grad, logits_grad, reps)
    source, made, in_first, in_second = lax.optimization_barrier((source, made, in_first, in_second))
    in_first = scatter_reps(in_first)
    returned = exchange(made, experts)
    grad_residual, grad_context, proj_kept, proj_sent, vectors_two = middle(
        columns, source, residual, cotangent, context, w_proj, gain_two
    )
    pairs = width // PAIR
    most = pairs // 2
    saved = (qkv, weights, inverse, context, normed_one)
    grads_a, kept_a, sent_a = attend_back(grad_context, *saved, 0, most)
    chips = sizes["exp"] // 2
    if (width // sizes["exp"]) % 16 == 0:
        sent_a, proj_sent, returned = lax.optimization_barrier((sent_a, proj_sent, returned))
        parts_a = chip_scatter((proj_kept, kept_a), (proj_sent, sent_a), sizes)
        grads_b, kept_b, sent_b = attend_back(
            tie(grad_context, grads_a, parts_a[0], grad_eout), *saved, most, pairs - most
        )
        sum_a = plane_sum(parts_a, sizes, (sent_b,))
        sum_a, sent_b = lax.optimization_barrier((sum_a, sent_b))
        parts_b = chip_scatter((kept_b,), (sent_b,), sizes)
        sum_b = plane_sum(parts_b, sizes)
        grad_tokens, vectors_one = last(
            tokens, (grads_a, grads_b), w_qkv, tie(grad_residual, parts_b[0]), gain_one
        )
        sum_a, sum_b, vectors_one, in_first = lax.optimization_barrier((sum_a, sum_b, vectors_one, in_first))
        block = jnp.concatenate([sum_a, sum_b], axis=1)
        small = small_sums(vectors_two, vectors_one, router_grad)
        small = sum_blocks(share(small, "exp", sizes["exp"]), F32)
        block = rep_sum(block, sizes)
        block, small, in_second = lax.optimization_barrier((block, small, in_second))
        in_second = scatter_reps(in_second)
        mixed = combine(columns, tie(returned, block), residual)
        block = rep_gather(block, sizes)
        block, mixed = lax.optimization_barrier((block, mixed))
        small = sum_blocks(share(small, "rep", reps), F32)
        parts = plane_gather(block, sizes)
        here = lax.axis_index("exp")
        order = jnp.arange(chips, dtype=jnp.int32) ^ (here >> 1)
        core = here & 1
        where = jnp.concatenate([core * chips + order, (1 - core) * chips + order]).astype(jnp.int32)
        grad_w_proj, grad_w_qkv = finish(parts, where, most * PAIR)
    else:
        in_second = scatter_reps(in_second)
        grads_b, kept_b, sent_b = attend_back(grad_context, *saved, most, pairs - most)
        mixed = combine(columns, returned, residual)
        grad_tokens, vectors_one = last(tokens, (grads_a, grads_b), w_qkv, grad_residual, gain_one)
        block = join_halves(
            jnp.concatenate([proj_kept, kept_a, kept_b], axis=1),
            jnp.concatenate([proj_sent, sent_a, sent_b], axis=1),
        )
        small = lax.psum(small_sums(vectors_two, vectors_one, router_grad), ("rep", "exp"))
        block = lax.psum(block, ("rep", "exp"))
        where = jnp.zeros((1,), jnp.int32)
        grad_w_proj, grad_w_qkv = finish((block,), where, most * PAIR)
    return (
        mixed,
        grad_tokens,
        grad_w_qkv,
        small[5],
        small[6],
        grad_w_proj,
        small[2],
        small[3],
        small[4],
        small[0],
        small[1],
        small[8 : 8 + experts].T,
        jnp.concatenate([in_first[:early], in_second], axis=0)[None].astype(F32),
        in_first[early : early + 1].astype(F32),
        turn(grad_eout)[None],
        in_first[early + 1 : early + 2, :out_part].astype(F32),
    )


def solution(mesh):
    rows = P(("rep", "exp"), None)
    placed = (rows,) * 4 + (P(),) * 10 + (
        P("exp", None, None),
        P("exp", None),
        P("exp", None, None),
        P("exp", None),
    )
    return jax.shard_map(
        functools.partial(on_device, dict(mesh.shape)),
        mesh=mesh,
        in_specs=placed,
        out_specs=(rows, rows)
        + (P(),) * 10
        + (P("exp", None, "rep"), P("exp", "rep"), P("exp", "rep", None), P("exp", "rep")),
        check_vma=False,
    )
```
